256 devices in a mesh: segment: 16 (over x_lo, y, core), tile: 16 (over x_hi, z).
Axes of the slice: x: 4 (x_hi: 2, x_lo: 2; x = x_hi * 2 + x_lo), y: 4, z: 8, core: 2. Of those that a mesh axis runs over, the one named last changes fastest.
Arguments:
- features: bfloat16 [8, 48, 128, 320], P(None, 'tile'), may hold values from -27 to 27
- timesteps: int32 [8], replicated, may hold values from 0 to 999
- plan: int32 [8], replicated, may hold values from 0 to 7, each once
- conv_weight: bfloat16 [16, 2880, 320], P('segment'), may hold values from -0.109375 to 0.109375
- skip_weight: bfloat16 [16, 320, 320], P('segment'), may hold values from -0.3125 to 0.3125
- time_weight: float32 [16, 320, 320], P('segment'), may hold values from -0.3125 to 0.3125
- norm_gain: float32 [16, 320], P('segment'), may hold values from 0.5 to 1.5
- norm_bias: float32 [16, 320], P('segment'), may hold values from -3 to 3
Outputs:
- activations: bfloat16 [16, 8, 48, 128, 320], P('segment', None, 'tile')
The draws below stay inside these ranges and needn't reach their ends.
All inputs are finite; a program needn't handle non-finite values.
Results may differ from the reference program's by a relative error of at most 0.017.
Values may be sent and summed in bfloat16 or wider, within the bound.
No kernel may reach another device: no remote copies, remote signals or barrier semaphores. Data moves between devices by JAX's collectives and lax.ppermute only.
A program may use at most 64 MiB of HBM per device.

```python
import math
import jax
import jax.numpy as jnp
from jax import lax

CHANNELS = 320
GROUPS = 32
FREQ = 320
COLS = 128
HEIGHT = 48
DOWN = 4
MICRO = 8
N_SEGMENT = 16


def draw_features(key, part):
    key = jax.random.fold_in(key, 11)
    noise_key, channel_key = jax.random.split(key)
    rise = jnp.arange(HEIGHT, dtype=jnp.float32) / (HEIGHT - 1)
    channel_scale = jnp.exp(jax.random.uniform(channel_key, (CHANNELS,), jnp.float32, math.log(0.2), math.log(2.0)))
    base = jnp.clip(jax.random.normal(noise_key, (MICRO, HEIGHT, COLS, CHANNELS), jnp.float32), -4.0, 4.0)
    row_scale = jnp.exp(rise * math.log(3.0))
    return (base * row_scale[None, :, None, None] * channel_scale[None, None, None, :]).astype(jnp.bfloat16)


def set_ends(entries, key, low, top_value):
    dims = entries.shape
    spot = [jax.random.randint(jax.random.fold_in(key, axis), (), 0, dims[axis]) for axis in range(len(dims))]
    entries = entries.at[tuple(spot)].set(low)
    longest = dims.index(max(dims))
    spot[longest] = (spot[longest] + 1) % dims[longest]
    return entries.at[tuple(spot)].set(top_value)


def steps_of(rng, extent, cuts, least, high):
    def one(axis_at, blocks):
        steps = jax.random.uniform(jax.random.fold_in(jax.random.fold_in(rng, 6), axis_at), (blocks,), jnp.float32, least / len(cuts), high / len(cuts))
        return jnp.repeat(jnp.exp(steps), extent[axis_at] // blocks).reshape((-1,) + (1,) * (len(extent) - axis_at - 1))

    level = one(*cuts[0])
    for cut in cuts[1:]:
        level = level * one(*cut)
    return level


def normal_values(own_key, shape, scale, bound, shards=(), kind=jnp.bfloat16):
    factor_of = steps_of(own_key, shape, shards, -0.22, 0.18) if shards else 1.0
    result = jax.random.normal(own_key, shape, jnp.float32) * scale * factor_of
    return jnp.minimum(jnp.maximum(result, -bound), bound).astype(kind)


def setup_inputs(seed: int = 0) -> dict:
    arg_keys = jax.random.split(jax.random.key(seed), 9)
    features = draw_features(jax.random.fold_in(arg_keys[8], 71), 0)
    timesteps = set_ends(jax.random.randint(arg_keys[1], (MICRO,), 0, 1000), jax.random.fold_in(arg_keys[1], 1), 0, 999).astype(jnp.int32)
    plan = jax.random.permutation(arg_keys[2], MICRO).astype(jnp.int32)
    conv_weight = normal_values(arg_keys[3], (N_SEGMENT, 9 * CHANNELS, CHANNELS), (9 * CHANNELS) ** -0.5, 0.109375, ((0, 16),))
    skip_weight = normal_values(arg_keys[4], (N_SEGMENT, CHANNELS, CHANNELS), CHANNELS ** -0.5, 0.3125, ((0, 16),))
    time_weight = normal_values(arg_keys[5], (N_SEGMENT, FREQ, CHANNELS), FREQ ** -0.5, 0.3125, ((0, 16),), jnp.float32)
    norm_gain = jnp.clip(1.0 + 0.1 * jax.random.normal(arg_keys[6], (N_SEGMENT, CHANNELS), jnp.float32), 0.5, 1.5)
    norm_bias = normal_values(arg_keys[7], (N_SEGMENT, CHANNELS), 0.5, 3.0, ((0, 16),), jnp.float32)
    return dict(features=features, timesteps=timesteps, plan=plan, conv_weight=conv_weight, skip_weight=skip_weight, time_weight=time_weight, norm_gain=norm_gain, norm_bias=norm_bias)


def sinusoid(steps):
    half_width = FREQ // 2
    rates = jnp.exp(-math.log(10000.0) * jnp.arange(half_width, dtype=jnp.float32) / half_width)
    angles = steps.astype(jnp.float32)[:, None] * rates[None, :]
    return jnp.concatenate([jnp.cos(angles), jnp.sin(angles)], axis=-1)

def convolve(padded, kernel, height, width):
    channels = padded.shape[-1]
    patches = jnp.concatenate([padded[row_shift:row_shift + height, col_shift:col_shift + width] for row_shift in range(3) for col_shift in range(3)], axis=-1)
    product = jnp.dot(patches.reshape(height * width, 9 * channels), kernel, preferred_element_type=jnp.float32)
    return product.reshape(height, width, kernel.shape[1])

def res_block(hidden_in, lateral, lateral_map, kernel, gains, biases, embedded):
    height, width, channels = hidden_in.shape
    summed = hidden_in.astype(jnp.float32)
    if lateral is not None:
        projected = jnp.dot(lateral.reshape(height * width, channels), lateral_map, preferred_element_type=jnp.float32)
        summed = summed + projected.reshape(height, width, channels)
    grouped = summed.reshape(height * width, GROUPS, channels // GROUPS)
    average = lax.optimization_barrier(jnp.mean(grouped, axis=(0, 2)))
    centred = grouped - average[None, :, None]
    variance = lax.optimization_barrier(jnp.mean(centred * centred, axis=(0, 2)))
    normed = (centred * lax.rsqrt(variance + 1e-05)[None, :, None]).reshape(height, width, channels) * gains + biases
    lifted = (jax.nn.silu(normed) + embedded).astype(jnp.bfloat16)
    padded = jnp.pad(lifted, ((1, 1), (1, 1), (0, 0)))
    return (summed + convolve(padded, kernel, height, width)).astype(jnp.bfloat16)

def reference(features, timesteps, plan, conv_weight, skip_weight, time_weight, norm_gain, norm_bias):
    columns = []
    for slot_index in range(MICRO):
        sample = plan[slot_index]
        hidden = features[sample]
        encoded = sinusoid(timesteps[sample][None])[0]
        laterals = []
        outputs = []
        for segment in range(N_SEGMENT):
            lateral = laterals[N_SEGMENT - 1 - segment] if segment >= N_SEGMENT - DOWN else None
            embedded = jnp.dot(encoded, time_weight[segment], precision=lax.Precision.HIGHEST)
            hidden = res_block(hidden, lateral, skip_weight[segment], conv_weight[segment], norm_gain[segment], norm_bias[segment], embedded)
            outputs.append(hidden)
            if segment < DOWN:
                laterals.append(hidden)
        columns.append(jnp.stack(outputs))
    return jnp.stack(columns, axis=1)
```

```python
import functools
import math

import jax
import jax.numpy as jnp
from jax import lax
from jax.experimental import pallas as pl
from jax.experimental.pallas import tpu as pltpu
from jax.sharding import PartitionSpec as P

BLOCKS, MICRO, TILES, DOWN = 16, 8, 16, 4
WIDTH, CH, GROUP = 128, 320, 10
CAT = 3 * CH
TAPS = 9 * CH
ROWS = 12
PIECE = 3 * CH
OWN = ROWS * CH
MEMBERS = float(48 * WIDTH * GROUP)
MIB = 1024 * 1024
LEAD = 2944
FULL = LEAD + 384
STATS = 48
BF, F32 = jnp.bfloat16, jnp.float32
ANY = pl.BlockSpec(memory_space=pl.ANY)
VM = pl.BlockSpec(memory_space=pltpu.VMEM)
SM = pl.BlockSpec(memory_space=pltpu.SMEM)
BOTH = ("segment", "tile")

PAIRS = ((0, 1), (2, 6), (3, 7), (4, 8), (5, 9), (10, 14), (11, 15), (12, 13))
FETCH_AFTER = {0: 3, 2: 4, 4: 5, 6: 6, 8: 7}
SWAP_AFTER = {0: 1, 1: 2, 2: 3, 3: 4, 6: 5, 8: 6, 10: 7}
GROUPS = ((2, 3, 4, 5, 6, 7), (8, 9, 10, 11), (0, 1, 12, 13, 14, 15))
SPREAD_AFTER = {9: 0, 13: 1}
COLUMN = {0: 4, 1: 5, 2: 1, 3: 5, 4: 2, 5: 6, 6: 3, 7: 7, 8: 4, 9: 1, 10: 5, 11: 6, 12: 6, 13: 2, 14: 7, 15: 0}


def place(slot, quarter):
    tile = (slot // 4) * 8 + 2 * (slot % 4) + (quarter in (1, 2))
    return (quarter // 2) * TILES + tile


def helper(block, slot, quarter):
    if block == BLOCKS - 1:
        return place(slot, quarter)
    segment = 2 * COLUMN[block] + slot // 4
    return segment * TILES + quarter // 2 * 8 + place(slot, quarter) % 8


def chunk_at(turn, k):
    return pl.multiple_of(lax.rem(k + turn, 4) * PIECE, PIECE)


def send_sums(info, totals, squares, source, near, cross, stats):
    ones = jnp.ones((8, WIDTH), F32)
    rows = jnp.concatenate(
        [
            lax.dot_general(
                ones,
                part,
                (((1,), (1,)), ((), ())),
                precision=lax.Precision.HIGHEST,
                preferred_element_type=F32,
            )[0:1]
            for part in (totals, squares)
        ],
        axis=0,
    )
    high = rows.astype(BF).astype(F32)
    left = rows - high
    middle = left.astype(BF).astype(F32)
    low = left - middle
    coded = jnp.concatenate([high, middle, low, jnp.zeros((10, CH), F32)], axis=0)
    coded = jnp.concatenate([coded, jnp.zeros((16, 64), F32)], axis=1).astype(BF)
    even = lax.rem(info[0], 2) == 0
    first, last = source[0:CH, :], source[OWN - CH : OWN, :]
    near[0:CH, :] = jnp.where(even, last, first)
    cross[0:CH, :] = jnp.where(even, first, last)
    for i in range(3):
        part = coded[:, i * 128 : (i + 1) * 128]
        near[CH + 16 * i : CH + 16 * (i + 1), :] = part
        cross[CH + 16 * i : CH + 16 * (i + 1), :] = part
        stats[16 * i : 16 * (i + 1), :] = part


def first_body(info, *refs):
    pieces, (near, cross, stats, whole), (xs, sem) = refs[:4], refs[4:8], refs[8:]

    @pl.when(info[2] == 1)
    def _():
        copies = [
            pltpu.make_async_copy(pieces[k], xs.at[pl.ds(chunk_at(info[1], k), PIECE)], sem.at[k])
            for k in range(4)
        ]
        for copy in copies:
            copy.start()
        for copy in copies:
            copy.wait()
        final = pltpu.make_async_copy(xs, whole, sem.at[0])
        final.start()
        totals = squares = jnp.zeros((CH, WIDTH), F32)
        for r in range(ROWS):
            row = xs[r * CH : (r + 1) * CH, :].astype(F32)
            totals, squares = totals + row, squares + row * row
        send_sums(info, totals, squares, xs, near, cross, stats)
        final.wait()


def block_body(at_core, next_core, up_in, up_out, last, info, *refs):
    refs = list(refs)

    def take(n):
        got = refs[:n]
        del refs[:n]
        return got

    source, near, cross, own_stats, far_stats, member = take(6)
    weights = take(2)
    if up_in:
        lateral_edges = take(2)
    if up_out:
        (lateral,), nexts = take(1), take(2)
    if last:
        passing = take(last)
    wholes = take(4 if last else 1)
    if not last:
        near_out, cross_out, stats_out = take(3)
    if up_out:
        (summed_out,) = take(1)
    xs, ws, cat, result, totals, squares, in_sem, w_sem, out_sem = take(9)
    if up_in:
        (sk_in,) = take(1)
    if up_out:
        ls, sk, sums, l_sem = take(4)

    @pl.when(info[2] == 1)
    def _():
        core = info[0] // 2
        x_copy = pltpu.make_async_copy(source, xs, in_sem.at[0])
        x_copy.start()
        lead, tail = pl.ds(0, LEAD), pl.ds(LEAD, FULL - LEAD)
        for at in range(2):

            @pl.when((core == at_core) == (at == 0))
            def _():
                pltpu.make_async_copy(weights[at].at[:, lead], ws, w_sem.at[0]).start()
                if up_in:
                    pltpu.make_async_copy(weights[at].at[:, tail], sk_in, w_sem.at[1]).start()

        if up_out:
            lateral_copy = pltpu.make_async_copy(lateral, ls, l_sem.at[0])
            lateral_copy.start()
            for at in range(2):

                @pl.when((core == next_core) == (at == 0))
                def _():
                    pltpu.make_async_copy(nexts[at].at[:, tail], sk, l_sem.at[1]).start()

        coded = [jnp.concatenate([ref[a + 16 * i : a + 16 * i + 16, :] for i in range(3)], axis=1)
                 for ref, a in ((own_stats, 0), (far_stats, 0), (near, CH), (cross, CH))]
        coded = jnp.concatenate(coded, axis=0)[:, 0:CH]
        groups = lax.dot_general(
            member[...], coded, (((1,), (1,)), ((), ())), preferred_element_type=F32
        )
        kind = lax.rem(lax.broadcasted_iota(jnp.int32, (CH, 64), 1), 16)
        even_kind = lax.rem(kind, 2) == 0
        mean = jnp.sum(jnp.where(even_kind, groups, 0.0), axis=1, keepdims=True) / MEMBERS
        mean_sq = jnp.sum(jnp.where(even_kind, 0.0, groups), axis=1, keepdims=True) / MEMBERS
        variance = jnp.maximum(mean_sq - mean * mean, 0.0)
        pltpu.make_async_copy(weights[0].at[:, lead], ws, w_sem.at[0]).wait()
        tailing = ws[:, TAPS : TAPS + 64].astype(F32)
        params = tailing[:, 0:16] + tailing[:, 16:32] + tailing[:, 32:48]
        lane = lax.broadcasted_iota(jnp.int32, (CH, 16), 1)
        shift = jnp.sum(jnp.where(lane == info[1] + 8, params, 0.0), axis=1, keepdims=True)
        wide = (CH, WIDTH)
        gain = jnp.broadcast_to(params[:, 0:1] * lax.rsqrt(variance + 1e-5) * 0.5, wide)
        bias = jnp.broadcast_to(params[:, 1:2] * 0.5, wide)
        mean = jnp.broadcast_to(mean, wide)
        shift = jnp.broadcast_to(shift, wide)
        column = lax.broadcasted_iota(jnp.int32, wide, 1)

        def lift(x, row, keep=None):
            h = (x - mean) * gain + bias
            lifted = h * jnp.tanh(h) + h + shift
            if keep is not None:
                lifted = jnp.where(keep, lifted, 0.0)
            left = jnp.where(column == 0, 0.0, pltpu.roll(lifted, 1, 1)).astype(BF)
            right = jnp.where(column == WIDTH - 1, 0.0, pltpu.roll(lifted, WIDTH - 1, 1)).astype(BF)
            cols = pl.ds(row * WIDTH, WIDTH)
            if not isinstance(row, int):
                cols = pl.ds(pl.multiple_of(row * WIDTH, WIDTH), WIDTH)
            cat[0:CH, cols] = left
            cat[CH : 2 * CH, cols] = lifted.astype(BF)
            cat[2 * CH : 3 * CH, cols] = right

        even = lax.rem(info[0], 2) == 0
        near_rows, cross_rows = near[0:CH, :].astype(F32), cross[0:CH, :].astype(F32)
        if up_in:
            pltpu.make_async_copy(weights[0].at[:, tail], sk_in, w_sem.at[1]).wait()
            skip_in = sk_in[:, 0:CH]
            near_rows, cross_rows = (
                rows + jnp.dot(skip_in, edge[0:CH, :], preferred_element_type=F32)
                for rows, edge in zip((near_rows, cross_rows), lateral_edges)
            )
        lift(jnp.where(even, cross_rows, near_rows), 0, info[0] > 0)
        lift(jnp.where(even, near_rows, cross_rows), ROWS + 1, info[0] < 3)
        x_copy.wait()

        def own_row(r):
            return pl.ds(pl.multiple_of(r * CH, CH), CH)

        @pl.loop(0, ROWS)
        def _(r):
            lift(xs[own_row(r), :].astype(F32), r + 1)

        if up_out:
            lateral_copy.wait()
            pltpu.make_async_copy(nexts[0].at[:, tail], sk, l_sem.at[1]).wait()
            skip = sk[:, 0:CH]
        totals[...] = jnp.zeros(wide, F32)
        squares[...] = jnp.zeros(wide, F32)

        @pl.loop(0, ROWS // 2)
        def _(pair):
            convolved = sum(
                jnp.dot(
                    ws[:, dy * CAT : (dy + 1) * CAT],
                    cat[:, pl.ds(pl.multiple_of((2 * pair + dy) * WIDTH, WIDTH), 2 * WIDTH)],
                    preferred_element_type=F32,
                )
                for dy in range(3)
            )
            rows = [own_row(2 * pair), own_row(2 * pair + 1)]
            if up_out:
                both = jnp.concatenate([ls[row, :] for row in rows], axis=1)
                projected = jnp.dot(skip, both, preferred_element_type=F32)
            for half, row in enumerate(rows):
                cols = slice(half * WIDTH, (half + 1) * WIDTH)
                kept = (xs[row, :].astype(F32) + convolved[:, cols]).astype(BF)
                result[row, :] = kept
                if not last:
                    following = kept.astype(F32)
                    if up_out:
                        following = following + projected[:, cols]
                        sums[row, :] = following
                    totals[...] += following
                    squares[...] += following * following

        if last:
            finals = [
                pltpu.make_async_copy(
                    result.at[pl.ds(chunk_at(info[1], k), PIECE)], wholes[k], out_sem.at[k]
                )
                for k in range(4)
            ]
        else:
            finals = [pltpu.make_async_copy(result, wholes[0], out_sem.at[0])]
        if up_out:
            finals.append(pltpu.make_async_copy(sums, summed_out, out_sem.at[1]))
        for copy in finals:
            copy.start()
        if not last:
            send_sums(info, totals[...], squares[...], result, near_out, cross_out, stats_out)
        for copy in finals:
            copy.wait()

    if last:
        hand_on(info, passing, wholes, result, in_sem, out_sem)


def hand_on(info, passing, outs, held, in_sem, out_sem):
    for at, ref in enumerate(passing):

        @pl.when(info[3] == at)
        def _():
            arrive = pltpu.make_async_copy(ref, held, in_sem.at[0])
            arrive.start()
            arrive.wait()
            copies = [
                pltpu.make_async_copy(
                    held.at[pl.ds(chunk_at(info[4], k), PIECE)], outs[k], out_sem.at[k]
                )
                for k in range(4)
            ]
            for copy in copies:
                copy.start()
            for copy in copies:
                copy.wait()


EXCHANGED = [
    jax.ShapeDtypeStruct((CH + STATS, WIDTH), BF),
    jax.ShapeDtypeStruct((CH + STATS, WIDTH), BF),
    jax.ShapeDtypeStruct((STATS, WIDTH), BF),
]
WHOLE = jax.ShapeDtypeStruct((OWN, WIDTH), BF)
PART = jax.ShapeDtypeStruct((PIECE, WIDTH), BF)


def first_call(info, pieces):
    return pl.pallas_call(
        first_body,
        out_shape=EXCHANGED + [WHOLE],
        in_specs=[SM] + [ANY] * 4,
        out_specs=[VM] * 3 + [ANY],
        scratch_shapes=[pltpu.VMEM((OWN, WIDTH), BF), pltpu.SemaphoreType.DMA((4,))],
        compiler_params=pltpu.CompilerParams(vmem_limit_bytes=16 * MIB),
        name="first_sums",
    )(info, *pieces)


def block_call(cores, info, source, exchanged, member, weights, lateral_edges, lateral, nexts, passing):
    up_in, up_out, last = lateral_edges is not None, lateral is not None, len(passing)
    operands = [source, *exchanged, member, *weights]
    specs = [ANY] + [VM] * 5 + [ANY] * 2
    shapes, out_specs = [WHOLE] + EXCHANGED, [ANY] + [VM] * 3
    if last:
        shapes, out_specs = [PART] * 4, [ANY] * 4
    scratch = [
        pltpu.VMEM((OWN, WIDTH), F32 if up_in else BF),
        pltpu.VMEM((CH, LEAD), BF),
        pltpu.VMEM((CAT, (ROWS + 2) * WIDTH), BF),
        pltpu.VMEM((OWN, WIDTH), BF),
        pltpu.VMEM((CH, WIDTH), F32),
        pltpu.VMEM((CH, WIDTH), F32),
        pltpu.SemaphoreType.DMA((1,)),
        pltpu.SemaphoreType.DMA((2,)),
        pltpu.SemaphoreType.DMA((4,)),
    ]
    if up_in:
        operands += list(lateral_edges)
        specs += [VM] * 2
        scratch.append(pltpu.VMEM((CH, FULL - LEAD), BF))
    if up_out:
        operands += [lateral, *nexts]
        specs += [ANY] * 3
        shapes = shapes + [jax.ShapeDtypeStruct((OWN, WIDTH), F32)]
        out_specs = out_specs + [ANY]
        scratch += [
            pltpu.VMEM((OWN, WIDTH), BF),
            pltpu.VMEM((CH, FULL - LEAD), BF),
            pltpu.VMEM((OWN, WIDTH), F32),
            pltpu.SemaphoreType.DMA((2,)),
        ]
    operands += passing
    specs += [ANY] * last
    out = pl.pallas_call(
        functools.partial(block_body, *cores, up_in, up_out, last),
        out_shape=shapes,
        in_specs=[SM] + specs,
        out_specs=out_specs,
        scratch_shapes=scratch,
        compiler_params=pltpu.CompilerParams(vmem_limit_bytes=40 * MIB),
        cost_estimate=pl.CostEstimate(
            flops=2 * OWN * WIDTH * TAPS, bytes_accessed=4 * MIB, transcendentals=OWN * WIDTH
        ),
        name="res_block",
    )(info, *operands)
    if last:
        return out, None, None
    return out[0], out[1:4], out[4] if up_out else None


def split_body(count, info, *refs):
    hand_on(info, refs[:count], refs[count : count + 4], *refs[count + 4 :])


def split(info, wholes):
    return pl.pallas_call(
        functools.partial(split_body, len(wholes)),
        out_shape=[PART] * 4,
        in_specs=[SM] + [ANY] * len(wholes),
        out_specs=[ANY] * 4,
        scratch_shapes=[
            pltpu.VMEM((OWN, WIDTH), BF),
            pltpu.SemaphoreType.DMA((1,)),
            pltpu.SemaphoreType.DMA((4,)),
        ],
        compiler_params=pltpu.CompilerParams(vmem_limit_bytes=16 * MIB),
        name="split",
    )(info, *wholes)


def collect_body(groups, info, *refs):
    out, held, in_sem, out_sem = refs[-4:]
    for at in range(groups):

        @pl.when(info[0] == at)
        def _():
            copies = []
            for k in range(4):
                for high in range(2):
                    slot, n = 4 * high + lax.rem(info[1] + 4 - k, 4), 2 * k + high
                    copies.append(
                        (
                            pltpu.make_async_copy(refs[at * 8 + n], held.at[n], in_sem.at[n]),
                            pltpu.make_async_copy(held.at[n], out.at[slot], out_sem.at[n]),
                        )
                    )
            for arrive, _ in copies:
                arrive.start()
            for arrive, leave in copies:
                arrive.wait()
                leave.start()
            for _, leave in copies:
                leave.wait()


def collect(info, received):
    flat = [piece for group in received for piece in group]
    return pl.pallas_call(
        functools.partial(collect_body, len(received)),
        out_shape=jax.ShapeDtypeStruct((MICRO, PIECE, WIDTH), BF),
        in_specs=[SM] + [ANY] * len(flat),
        out_specs=ANY,
        scratch_shapes=[
            pltpu.VMEM((MICRO, PIECE, WIDTH), BF),
            pltpu.SemaphoreType.DMA((8,)),
            pltpu.SemaphoreType.DMA((8,)),
        ],
        compiler_params=pltpu.CompilerParams(vmem_limit_bytes=16 * MIB),
        name="collect",
    )(info, *flat)


def sinusoid(steps, half_width):
    rates = jnp.exp(-math.log(10000.0) * jnp.arange(half_width, dtype=F32) / half_width)
    angles = steps.astype(F32)[:, None] * rates[None, :]
    return jnp.concatenate([jnp.cos(angles), jnp.sin(angles)], axis=-1)


def on_device(
    features, timesteps, plan, conv_weight, skip_weight, time_weight, norm_gain, norm_bias
):
    segment, tile = lax.axis_index("segment"), lax.axis_index("tile")
    core, odd = segment % 2, tile % 2
    quarter = jnp.where(odd == 1, 1 + core, 3 * core)
    slot = 4 * (tile // 8) + (tile % 8) // 2
    active = (segment < 2).astype(jnp.int32)
    passed = 4 * core + (tile % 8) // 2

    def info_for(group):
        pick = jnp.full((), -1, jnp.int32)
        for at, block in enumerate(group):
            if block < BLOCKS - 1:
                pick = jnp.where(segment // 2 == COLUMN[block], at, pick)
        return jnp.stack([quarter, slot, active, pick, passed]).astype(jnp.int32)

    info = info_for(())

    served = lax.dynamic_index_in_dim(
        features, plan[jnp.minimum(segment, MICRO - 1)], 0, keepdims=False
    )
    served = served.transpose(0, 2, 1).reshape(PIECE, WIDTH)
    pieces = []
    for k in range(4):
        route = [
            (j * TILES + 4 * q + (k + j) % 4, place(j, q)) for j in range(MICRO) for q in range(4)
        ]
        pieces.append(lax.ppermute(served, BOTH, route))

    encoded = sinusoid(timesteps[plan], time_weight.shape[1] // 2)
    shifts = jnp.dot(encoded, time_weight[0], precision=lax.Precision.HIGHEST)
    params = jnp.concatenate([norm_gain, norm_bias, jnp.zeros((6, CH), F32), shifts], axis=0)
    high = lax.reduce_precision(params, 8, 7)
    left = params - high
    middle = lax.reduce_precision(left, 8, 7)
    coded = jnp.concatenate([high, middle, left - middle], axis=0).astype(BF)
    columns = [conv_weight[0].T, coded.T, jnp.zeros((CH, LEAD - TAPS - STATS), BF)]
    lead = jnp.concatenate(columns, axis=1)
    columns += [skip_weight[0].T, jnp.zeros((CH, FULL - LEAD - CH), BF)]
    full = jnp.concatenate(columns, axis=1)
    first_up = BLOCKS - DOWN

    def fetch(pair, after):
        own = full if max(pair) >= first_up else lead
        if after is not None:
            own, _ = lax.optimization_barrier((own, after))
        return lax.ppermute(own, "segment", [(pair[0], 0), (pair[1], 1)])

    def swap(value, mask):
        route = [(place(j, q), place(j, q ^ mask)) for j in range(MICRO) for q in range(4)]
        return lax.ppermute(value, BOTH, route)

    def hand_over(block, whole):
        route = [(place(j, q), helper(block, j, q)) for j in range(MICRO) for q in range(4)]
        return lax.ppermute(whole, BOTH, route)

    def spread(group, outs):
        got = []
        for k in range(4):
            for high in range(2):
                route = [
                    (helper(block, j, q), block * TILES + 4 * q + (k + j) % 4)
                    for block in group
                    for j in range(4 * high, 4 * high + 4)
                    for q in range(4)
                ]
                got.append(lax.ppermute(outs[k], BOTH, route))
        return got

    member_at = jnp.arange(CH) // GROUP
    member = (member_at[:, None] == member_at[None, :]).astype(BF)
    weights, cores, fetched = {}, {}, {}

    def swap_cores(index, own):
        both = own, lax.ppermute(own, "segment", [(0, 1), (1, 0)])
        for at, block in enumerate(PAIRS[index]):
            weights[block], cores[block] = both, at

    swap_cores(0, lead)
    for index in (1, 2):
        fetched[index] = fetch(PAIRS[index], None)
    *exchanged, source = first_call(info, pieces)
    wholes, edges_of, passing, received = [], {}, [], []
    for block in range(BLOCKS):
        up_in, up_out = block >= first_up, first_up - 1 <= block < BLOCKS - 1
        near, cross, stats = exchanged
        near_in, cross_in, far = swap(near, 1), swap(cross, 3), swap(stats, 2)
        edges_of[block] = (near_in, cross_in)
        if block >= 2:
            source, near_in, cross_in, far, passing[block - 2] = lax.optimization_barrier(
                (source, near_in, cross_in, far, passing[block - 2])
            )
        last = block == BLOCKS - 1
        whole, exchanged, summed = block_call(
            (cores[block], cores.get(block + 1, 0)),
            info_for(GROUPS[2]) if last else info,
            source,
            (near_in, cross_in, stats, far),
            member,
            weights[block],
            edges_of[BLOCKS - block] if up_in else None,
            wholes[BLOCKS - 2 - block] if up_out else None,
            weights[block + 1] if up_out else None,
            [passing[b] for b in GROUPS[2][:-1]] if last else [],
        )
        wholes.append(whole)
        source = summed if up_out else whole
        if not last:
            passing.append(hand_over(block, whole))
        if block in SPREAD_AFTER:
            group = GROUPS[SPREAD_AFTER[block]]
            outs = split(info_for(group), [passing[b] for b in group])
            received.append(spread(group, outs))
        if block in SWAP_AFTER:
            index = SWAP_AFTER[block]
            own, _ = lax.optimization_barrier((fetched[index], whole))
            swap_cores(index, own)
        if block in FETCH_AFTER:
            index = FETCH_AFTER[block]
            fetched[index] = fetch(PAIRS[index], whole)
    received.append(spread(GROUPS[2], whole))
    group_of = jnp.zeros((), jnp.int32)
    for at, group in enumerate(GROUPS):
        for block in group:
            group_of = jnp.where(segment == block, at, group_of)
    out = collect(jnp.stack([group_of, tile % 4]).astype(jnp.int32), received)
    out = out.reshape(1, MICRO, 3, CH, WIDTH)
    return out.transpose(0, 1, 2, 4, 3)


def solution(mesh):
    placed = (
        P(None, "tile", None, None),
        P(),
        P(),
        P("segment", None, None),
        P("segment", None, None),
        P("segment", None, None),
        P("segment", None),
        P("segment", None),
    )
    return jax.shard_map(
        on_device,
        mesh=mesh,
        in_specs=placed,
        out_specs=P("segment", None, "tile", None, None),
        check_vma=False,
    )
```

```python
import functools
import math

import jax
import jax.numpy as jnp
from jax import lax
from jax.experimental import pallas as pl
from jax.experimental.pallas import tpu as pltpu
from jax.sharding import PartitionSpec as P

BLOCKS, MICRO, TILES, DOWN = 16, 8, 16, 4
WIDTH, CH, GROUP = 128, 320, 10
CAT = 3 * CH
TAPS = 9 * CH
ROWS = 12
PIECE = 3 * CH
OWN = ROWS * CH
MEMBERS = float(48 * WIDTH * GROUP)
MIB = 1024 * 1024
LEAD = 2944
FULL = LEAD + 384
STATS = 48
BF, F32 = jnp.bfloat16, jnp.float32
ANY = pl.BlockSpec(memory_space=pl.ANY)
VM = pl.BlockSpec(memory_space=pltpu.VMEM)
SM = pl.BlockSpec(memory_space=pltpu.SMEM)
BOTH = ("segment", "tile")

PAIRS = ((0, 1), (2, 6), (3, 7), (4, 8), (5, 9), (10, 14), (11, 15), (12, 13))
FETCH_AFTER = {0: 3, 2: 4, 4: 5, 6: 6, 8: 7}
SWAP_AFTER = {0: 1, 1: 2, 2: 3, 3: 4, 6: 5, 8: 6, 10: 7}
GROUPS = ((2, 3, 4, 5), (6, 7, 8, 9), (10, 11, 12), (0, 1, 13, 14, 15))
SPREAD_AFTER = {7: 0, 11: 1, 14: 2}
SPREAD_BY = {10: 0, 14: 1, 15: 2}
HELPERS = {0: (4, 6, 0), 1: (4, 6, 1), 13: (5, 7, 0), 14: (5, 7, 1)}
HELPERS |= {b: (5, 7, b % 2) for b in (2, 3, 6, 7, 10, 11)}
HELPERS |= {b: (1, 3, b % 2) for b in (4, 5, 8, 9, 12)}


def place(slot, quarter):
    tile = (slot // 4) * 8 + 2 * (slot % 4) + (quarter in (1, 2))
    return (quarter // 2) * TILES + tile


def helper(block, slot, quarter):
    if block == BLOCKS - 1:
        return place(slot, quarter)
    segment = 2 * HELPERS[block][slot // 4] + HELPERS[block][2]
    return segment * TILES + quarter // 2 * 8 + place(slot, quarter) % 8


def chunk_at(turn, k):
    return pl.multiple_of(lax.rem(k + turn, 4) * PIECE, PIECE)


def send_sums(info, totals, squares, source, near, cross, stats):
    ones = jnp.ones((8, WIDTH), F32)
    rows = jnp.concatenate(
        [
            lax.dot_general(
                ones,
                part,
                (((1,), (1,)), ((), ())),
                precision=lax.Precision.HIGHEST,
                preferred_element_type=F32,
            )[0:1]
            for part in (totals, squares)
        ],
        axis=0,
    )
    high = rows.astype(BF).astype(F32)
    left = rows - high
    middle = left.astype(BF).astype(F32)
    low = left - middle
    coded = jnp.concatenate([high, middle, low, jnp.zeros((10, CH), F32)], axis=0)
    coded = jnp.concatenate([coded, jnp.zeros((16, 64), F32)], axis=1).astype(BF)
    even = lax.rem(info[0], 2) == 0
    first, last = source[0:CH, :], source[OWN - CH : OWN, :]
    near[0:CH, :] = jnp.where(even, last, first)
    cross[0:CH, :] = jnp.where(even, first, last)
    for i in range(3):
        part = coded[:, i * 128 : (i + 1) * 128]
        near[CH + 16 * i : CH + 16 * (i + 1), :] = part
        cross[CH + 16 * i : CH + 16 * (i + 1), :] = part
        stats[16 * i : 16 * (i + 1), :] = part


def first_body(info, *refs):
    pieces, (near, cross, stats, whole), (xs, sem) = refs[:4], refs[4:8], refs[8:]

    @pl.when(info[2] == 1)
    def _():
        copies = [
            pltpu.make_async_copy(pieces[k], xs.at[pl.ds(chunk_at(info[1], k), PIECE)], sem.at[k])
            for k in range(4)
        ]
        for copy in copies:
            copy.start()
        for copy in copies:
            copy.wait()
        final = pltpu.make_async_copy(xs, whole, sem.at[0])
        final.start()
        totals = squares = jnp.zeros((CH, WIDTH), F32)
        for r in range(ROWS):
            row = xs[r * CH : (r + 1) * CH, :].astype(F32)
            totals, squares = totals + row, squares + row * row
        send_sums(info, totals, squares, xs, near, cross, stats)
        final.wait()


def block_body(at_core, next_core, up_in, up_out, last, info, *refs):
    refs = list(refs)

    def take(n):
        got = refs[:n]
        del refs[:n]
        return got

    source, near, cross, own_stats, far_stats, member = take(6)
    weights = take(2)
    if up_in:
        lateral_edges = take(2)
    if up_out:
        (lateral,), nexts = take(1), take(2)
    if last:
        passing = take(last)
    wholes = take(4 if last else 1)
    if not last:
        near_out, cross_out, stats_out = take(3)
    if up_out:
        (summed_out,) = take(1)
    xs, result = source, wholes[0]
    if last:
        (result,) = take(1)
    ws, ps, cat, totals, squares, in_sem, w_sem, out_sem = take(8)
    if up_in:
        (sk_in,) = take(1)
    if up_out:
        ls, sums = lateral, summed_out
        sk, l_sem = take(2)

    @pl.when(info[2] == 1)
    def _():
        core = info[0] // 2
        lead, tail = pl.ds(0, LEAD), pl.ds(LEAD, FULL - LEAD)
        head = pl.ds(LEAD - WIDTH, WIDTH)
        for at in range(2):

            @pl.when((core == at_core) == (at == 0))
            def _():
                pltpu.make_async_copy(weights[at].at[:, head], ps, w_sem.at[2]).start()
                pltpu.make_async_copy(weights[at].at[:, lead], ws, w_sem.at[0]).start()
                if up_in:
                    pltpu.make_async_copy(weights[at].at[:, tail], sk_in, w_sem.at[1]).start()

        if up_out:
            for at in range(2):

                @pl.when((core == next_core) == (at == 0))
                def _():
                    pltpu.make_async_copy(nexts[at].at[:, tail], sk, l_sem.at[1]).start()

        coded = [jnp.concatenate([ref[a + 16 * i : a + 16 * i + 16, :] for i in range(3)], axis=1)
                 for ref, a in ((own_stats, 0), (far_stats, 0), (near, CH), (cross, CH))]
        coded = jnp.concatenate(coded, axis=0)[:, 0:CH]
        groups = lax.dot_general(
            member[...], coded, (((1,), (1,)), ((), ())), preferred_element_type=F32
        )
        kind = lax.rem(lax.broadcasted_iota(jnp.int32, (CH, 64), 1), 16)
        even_kind = lax.rem(kind, 2) == 0
        mean = jnp.sum(jnp.where(even_kind, groups, 0.0), axis=1, keepdims=True) / MEMBERS
        mean_sq = jnp.sum(jnp.where(even_kind, 0.0, groups), axis=1, keepdims=True) / MEMBERS
        variance = jnp.maximum(mean_sq - mean * mean, 0.0)
        pltpu.make_async_copy(weights[0].at[:, head], ps, w_sem.at[2]).wait()
        tailing = ps[:, 64:128].astype(F32)
        params = tailing[:, 0:16] + tailing[:, 16:32] + tailing[:, 32:48]
        lane = lax.broadcasted_iota(jnp.int32, (CH, 16), 1)
        shift = jnp.sum(jnp.where(lane == info[1] + 8, params, 0.0), axis=1, keepdims=True)
        wide = (CH, WIDTH)
        gain = jnp.broadcast_to(params[:, 0:1] * lax.rsqrt(variance + 1e-5) * 0.5, wide)
        bias = jnp.broadcast_to(params[:, 1:2] * 0.5, wide)
        mean = jnp.broadcast_to(mean, wide)
        shift = jnp.broadcast_to(shift, wide)
        column = lax.broadcasted_iota(jnp.int32, wide, 1)

        def lift(x, row, keep=None):
            h = (x - mean) * gain + bias
            lifted = h * jnp.tanh(h) + h + shift
            if keep is not None:
                lifted = jnp.where(keep, lifted, 0.0)
            left = jnp.where(column == 0, 0.0, pltpu.roll(lifted, 1, 1)).astype(BF)
            right = jnp.where(column == WIDTH - 1, 0.0, pltpu.roll(lifted, WIDTH - 1, 1)).astype(BF)
            cols = pl.ds(row * WIDTH, WIDTH)
            if not isinstance(row, int):
                cols = pl.ds(pl.multiple_of(row * WIDTH, WIDTH), WIDTH)
            cat[0:CH, cols] = left
            cat[CH : 2 * CH, cols] = lifted.astype(BF)
            cat[2 * CH : 3 * CH, cols] = right

        even = lax.rem(info[0], 2) == 0
        near_rows, cross_rows = near[0:CH, :].astype(F32), cross[0:CH, :].astype(F32)
        if up_in:
            pltpu.make_async_copy(weights[0].at[:, tail], sk_in, w_sem.at[1]).wait()
            skip_in = sk_in[:, 0:CH]
            near_rows, cross_rows = (
                rows + jnp.dot(skip_in, edge[0:CH, :], preferred_element_type=F32)
                for rows, edge in zip((near_rows, cross_rows), lateral_edges)
            )
        def own_row(r):
            return slice(r * CH, (r + 1) * CH)

        if up_out:
            pltpu.make_async_copy(nexts[0].at[:, tail], sk, l_sem.at[1]).wait()
            skip = sk[:, 0:CH]
        totals[...] = jnp.zeros(wide, F32)
        squares[...] = jnp.zeros(wide, F32)

        def lift_at(row):
            if row == 0:
                lift(jnp.where(even, cross_rows, near_rows), 0, info[0] > 0)
            elif row == ROWS + 1:
                lift(jnp.where(even, near_rows, cross_rows), row, info[0] < 3)
            else:
                lift(xs[(row - 1) * CH : row * CH, :].astype(F32), row)

        for row in range(2):
            lift_at(row)
        lift_at(2)
        lift_at(3)
        pltpu.make_async_copy(weights[0].at[:, lead], ws, w_sem.at[0]).wait()
        for pair in range(ROWS // 2):
            if pair:
                lift_at(2 * pair + 2)
                lift_at(2 * pair + 3)
            convolved = sum(
                jnp.dot(
                    ws[:, dy * CAT : (dy + 1) * CAT],
                    cat[:, (2 * pair + dy) * WIDTH : (2 * pair + dy + 2) * WIDTH],
                    preferred_element_type=F32,
                )
                for dy in range(3)
            )
            rows = [own_row(2 * pair), own_row(2 * pair + 1)]
            if up_out:
                both = jnp.concatenate([ls[row, :] for row in rows], axis=1)
                projected = jnp.dot(skip, both, preferred_element_type=F32)
            for half, row in enumerate(rows):
                cols = slice(half * WIDTH, (half + 1) * WIDTH)
                kept = (xs[row, :].astype(F32) + convolved[:, cols]).astype(BF)
                result[row, :] = kept
                if not last:
                    following = kept.astype(F32)
                    if up_out:
                        following = following + projected[:, cols]
                        sums[row, :] = following
                    totals[...] += following
                    squares[...] += following * following

        if last:
            finals = [
                pltpu.make_async_copy(
                    result.at[pl.ds(chunk_at(info[1], k), PIECE)], wholes[k], out_sem.at[k]
                )
                for k in range(4)
            ]
        else:
            finals = []
        for copy in finals:
            copy.start()
        if not last:
            send_sums(info, totals[...], squares[...], result, near_out, cross_out, stats_out)
        for copy in finals:
            copy.wait()

    if last:
        hand_on(info, passing, wholes, result, in_sem, out_sem)


def hand_on(info, passing, outs, held, in_sem, out_sem):
    for at, ref in enumerate(passing):

        @pl.when(info[3] == at)
        def _():
            arrive = pltpu.make_async_copy(ref, held, in_sem.at[0])
            arrive.start()
            arrive.wait()
            copies = [
                pltpu.make_async_copy(
                    held.at[pl.ds(chunk_at(info[4], k), PIECE)], outs[k], out_sem.at[k]
                )
                for k in range(4)
            ]
            for copy in copies:
                copy.start()
            for copy in copies:
                copy.wait()


EXCHANGED = [
    jax.ShapeDtypeStruct((CH + STATS, WIDTH), BF),
    jax.ShapeDtypeStruct((CH + STATS, WIDTH), BF),
    jax.ShapeDtypeStruct((STATS, WIDTH), BF),
]
WHOLE = jax.ShapeDtypeStruct((OWN, WIDTH), BF)
PART = jax.ShapeDtypeStruct((PIECE, WIDTH), BF)


def first_call(info, pieces):
    return pl.pallas_call(
        first_body,
        out_shape=EXCHANGED + [WHOLE],
        in_specs=[SM] + [ANY] * 4,
        out_specs=[VM] * 3 + [ANY],
        scratch_shapes=[pltpu.VMEM((OWN, WIDTH), BF), pltpu.SemaphoreType.DMA((4,))],
        compiler_params=pltpu.CompilerParams(vmem_limit_bytes=16 * MIB),
        name="first_sums",
    )(info, *pieces)


def block_call(cores, info, source, exchanged, member, weights, lateral_edges, lateral, nexts, passing):
    up_in, up_out, last = lateral_edges is not None, lateral is not None, len(passing)
    operands = [source, *exchanged, member, *weights]
    specs = [VM] * 6 + [ANY] * 2
    shapes, out_specs = [WHOLE] + EXCHANGED, [VM] * 4
    scratch = []
    if last:
        shapes, out_specs = [PART] * 4, [ANY] * 4
        scratch.append(pltpu.VMEM((OWN, WIDTH), BF))
    scratch += [
        pltpu.VMEM((CH, LEAD), BF),
        pltpu.VMEM((CH, WIDTH), BF),
        pltpu.VMEM((CAT, (ROWS + 2) * WIDTH), BF),
        pltpu.VMEM((CH, WIDTH), F32),
        pltpu.VMEM((CH, WIDTH), F32),
        pltpu.SemaphoreType.DMA((1,)),
        pltpu.SemaphoreType.DMA((3,)),
        pltpu.SemaphoreType.DMA((4,)),
    ]
    if up_in:
        operands += list(lateral_edges)
        specs += [VM] * 2
        scratch.append(pltpu.VMEM((CH, FULL - LEAD), BF))
    if up_out:
        operands += [lateral, *nexts]
        specs += [VM] + [ANY] * 2
        shapes = shapes + [jax.ShapeDtypeStruct((OWN, WIDTH), F32)]
        out_specs = out_specs + [VM]
        scratch += [
            pltpu.VMEM((CH, FULL - LEAD), BF),
            pltpu.SemaphoreType.DMA((2,)),
        ]
    operands += passing
    specs += [ANY] * last
    out = pl.pallas_call(
        functools.partial(block_body, *cores, up_in, up_out, last),
        out_shape=shapes,
        in_specs=[SM] + specs,
        out_specs=out_specs,
        scratch_shapes=scratch,
        compiler_params=pltpu.CompilerParams(vmem_limit_bytes=28 * MIB),
        cost_estimate=pl.CostEstimate(
            flops=2 * OWN * WIDTH * TAPS, bytes_accessed=4 * MIB, transcendentals=OWN * WIDTH
        ),
        name="res_block",
    )(info, *operands)
    if last:
        return out, None, None
    return out[0], out[1:4], out[4] if up_out else None


def split_body(count, info, *refs):
    hand_on(info, refs[:count], refs[count : count + 4], *refs[count + 4 :])


def split(info, wholes):
    return pl.pallas_call(
        functools.partial(split_body, len(wholes)),
        out_shape=[PART] * 4,
        in_specs=[SM] + [ANY] * len(wholes),
        out_specs=[ANY] * 4,
        scratch_shapes=[
            pltpu.VMEM((OWN, WIDTH), BF),
            pltpu.SemaphoreType.DMA((1,)),
            pltpu.SemaphoreType.DMA((4,)),
        ],
        compiler_params=pltpu.CompilerParams(vmem_limit_bytes=16 * MIB),
        name="split",
    )(info, *wholes)


def collect_body(groups, info, *refs):
    out, held, in_sem, out_sem = refs[-4:]
    for at in range(groups):

        @pl.when(info[0] == at)
        def _():
            copies = []
            for k in range(4):
                for high in range(2):
                    slot, n = 4 * high + lax.rem(info[1] + 4 - k, 4), 2 * k + high
                    copies.append(
                        (
                            pltpu.make_async_copy(refs[at * 8 + n], held.at[n], in_sem.at[n]),
                            pltpu.make_async_copy(held.at[n], out.at[slot], out_sem.at[n]),
                        )
                    )
            for arrive, _ in copies:
                arrive.start()
            for arrive, leave in copies:
                arrive.wait()
                leave.start()
            for _, leave in copies:
                leave.wait()


def collect(info, received):
    flat = [piece for group in received for piece in group]
    return pl.pallas_call(
        functools.partial(collect_body, len(received)),
        out_shape=jax.ShapeDtypeStruct((MICRO, PIECE, WIDTH), BF),
        in_specs=[SM] + [ANY] * len(flat),
        out_specs=ANY,
        scratch_shapes=[
            pltpu.VMEM((MICRO, PIECE, WIDTH), BF),
            pltpu.SemaphoreType.DMA((8,)),
            pltpu.SemaphoreType.DMA((8,)),
        ],
        compiler_params=pltpu.CompilerParams(vmem_limit_bytes=16 * MIB),
        name="collect",
    )(info, *flat)


def sinusoid(steps, half_width):
    rates = jnp.exp(-math.log(10000.0) * jnp.arange(half_width, dtype=F32) / half_width)
    angles = steps.astype(F32)[:, None] * rates[None, :]
    return jnp.concatenate([jnp.cos(angles), jnp.sin(angles)], axis=-1)


def on_device(
    features, timesteps, plan, conv_weight, skip_weight, time_weight, norm_gain, norm_bias
):
    segment, tile = lax.axis_index("segment"), lax.axis_index("tile")
    core, odd = segment % 2, tile % 2
    quarter = jnp.where(odd == 1, 1 + core, 3 * core)
    slot = 4 * (tile // 8) + (tile % 8) // 2
    active = (segment < 2).astype(jnp.int32)

    def info_for(group):
        pick, passed = jnp.full((), -1, jnp.int32), (tile % 8) // 2
        for at, block in enumerate(group):
            if block < BLOCKS - 1:
                *columns, its_core = HELPERS[block]
                for half, column in enumerate(columns):
                    ours = segment == 2 * column + its_core
                    pick = jnp.where(ours, at, pick)
                    passed = jnp.where(ours, passed + 4 * half, passed)
        return jnp.stack([quarter, slot, active, pick, passed]).astype(jnp.int32)

    info = info_for(())

    served = lax.dynamic_index_in_dim(
        features, plan[jnp.minimum(segment, MICRO - 1)], 0, keepdims=False
    )
    served = served.transpose(0, 2, 1).reshape(PIECE, WIDTH)
    pieces = []
    for k in range(4):
        route = [
            (j * TILES + 4 * q + (k + j) % 4, place(j, q)) for j in range(MICRO) for q in range(4)
        ]
        pieces.append(lax.ppermute(served, BOTH, route))

    encoded = sinusoid(timesteps[plan], time_weight.shape[1] // 2)
    shifts = jnp.dot(encoded, time_weight[0], precision=lax.Precision.HIGHEST)
    params = jnp.concatenate([norm_gain, norm_bias, jnp.zeros((6, CH), F32), shifts], axis=0)
    high = lax.reduce_precision(params, 8, 7)
    left = params - high
    middle = lax.reduce_precision(left, 8, 7)
    coded = jnp.concatenate([high, middle, left - middle], axis=0).astype(BF)
    columns = [conv_weight[0].T, coded.T, jnp.zeros((CH, LEAD - TAPS - STATS), BF)]
    lead = jnp.concatenate(columns, axis=1)
    columns += [skip_weight[0].T, jnp.zeros((CH, FULL - LEAD - CH), BF)]
    full = jnp.concatenate(columns, axis=1)
    first_up = BLOCKS - DOWN

    def fetch(pair, after):
        own = full if max(pair) >= first_up else lead
        if after is not None:
            own, _ = lax.optimization_barrier((own, after))
        return lax.ppermute(own, "segment", [(pair[0], 0), (pair[1], 1)])

    def exchange(near, cross, stats):
        other_tile = [(t, t ^ 1) for t in range(TILES)]
        other_core = [(b, b ^ 1) for b in range(BLOCKS)]
        both = [
            (b * TILES + t, (b ^ 1) * TILES + (t ^ 1)) for b in range(BLOCKS) for t in range(TILES)
        ]
        return (
            lax.ppermute(near, "tile", other_tile),
            lax.ppermute(cross, "segment", other_core),
            lax.ppermute(stats, BOTH, both),
        )

    def hand_over(block, whole):
        route = [(place(j, q), helper(block, j, q)) for j in range(MICRO) for q in range(4)]
        return lax.ppermute(whole, BOTH, route)

    def spread(group, outs):
        got = []
        for k in range(4):
            for high in range(2):
                route = [
                    (helper(block, j, q), block * TILES + 4 * q + (k + j) % 4)
                    for block in group
                    for j in range(4 * high, 4 * high + 4)
                    for q in range(4)
                ]
                got.append(lax.ppermute(outs[k], BOTH, route))
        return got

    member_at = jnp.arange(CH) // GROUP
    member = (member_at[:, None] == member_at[None, :]).astype(BF)
    weights, cores, fetched = {}, {}, {}

    def swap_cores(index, own):
        both = own, lax.ppermute(own, "segment", [(b, b ^ 1) for b in range(BLOCKS)])
        for at, block in enumerate(PAIRS[index]):
            weights[block], cores[block] = both, at

    swap_cores(0, lead)
    *exchanged, source = first_call(info, pieces)
    for index in (1, 2):
        fetched[index] = fetch(PAIRS[index], pieces[-1])
    wholes, edges_of, passing, received = [], {}, [], []
    for block in range(BLOCKS):
        up_in, up_out = block >= first_up, first_up - 1 <= block < BLOCKS - 1
        near, cross, stats = exchanged
        near_in, cross_in, far = exchange(near, cross, stats)
        edges_of[block] = (near_in, cross_in)
        if block >= 2:
            source, near_in, cross_in, far, passing[block - 2] = lax.optimization_barrier(
                (source, near_in, cross_in, far, passing[block - 2])
            )
        if block in SPREAD_BY:
            at = SPREAD_BY[block]
            source, received[at] = lax.optimization_barrier((source, received[at]))
        last = block == BLOCKS - 1
        whole, exchanged, summed = block_call(
            (cores[block], cores.get(block + 1, 0)),
            info_for(GROUPS[-1]) if last else info,
            source,
            (near_in, cross_in, stats, far),
            member,
            weights[block],
            edges_of[BLOCKS - block] if up_in else None,
            wholes[BLOCKS - 2 - block] if up_out else None,
            weights[block + 1] if up_out else None,
            [passing[b] for b in GROUPS[-1][:-1]] if last else [],
        )
        wholes.append(whole)
        source = summed if up_out else whole
        if not last:
            passing.append(hand_over(block, whole))
        if block in SPREAD_AFTER:
            group = GROUPS[SPREAD_AFTER[block]]
            outs = split(info_for(group), [passing[b] for b in group])
            received.append(spread(group, outs))
        if block in SWAP_AFTER:
            index = SWAP_AFTER[block]
            own, _ = lax.optimization_barrier((fetched[index], whole))
            swap_cores(index, own)
        if block in FETCH_AFTER:
            index = FETCH_AFTER[block]
            fetched[index] = fetch(PAIRS[index], whole)
    received.append(spread(GROUPS[-1], whole))
    group_of = jnp.zeros((), jnp.int32)
    for at, group in enumerate(GROUPS):
        for block in group:
            group_of = jnp.where(segment == block, at, group_of)
    out = collect(jnp.stack([group_of, tile % 4]).astype(jnp.int32), received)
    out = out.reshape(1, MICRO, 3, CH, WIDTH)
    return out.transpose(0, 1, 2, 4, 3)


def solution(mesh):
    placed = (
        P(None, "tile", None, None),
        P(),
        P(),
        P("segment", None, None),
        P("segment", None, None),
        P("segment", None, None),
        P("segment", None),
        P("segment", None),
    )
    return jax.shard_map(
        on_device,
        mesh=mesh,
        in_specs=placed,
        out_specs=P("segment", None, "tile", None, None),
        check_vma=False,
    )
```

```python
import functools
import math

import jax
import jax.numpy as jnp
from jax import lax
from jax.experimental import pallas as pl
from jax.experimental.pallas import tpu as pltpu
from jax.sharding import PartitionSpec as P

BLOCKS, MICRO, TILES, DOWN = 16, 8, 16, 4
WIDTH, CH, GROUP = 128, 320, 10
CAT = 3 * CH
TAPS = 9 * CH
ROWS = 12
PIECE = 3 * CH
OWN = ROWS * CH
MEMBERS = float(48 * WIDTH * GROUP)
MIB = 1024 * 1024
LEAD = 2944
FULL = LEAD + 384
STATS = 48
BF, F32 = jnp.bfloat16, jnp.float32
ANY = pl.BlockSpec(memory_space=pl.ANY)
VM = pl.BlockSpec(memory_space=pltpu.VMEM)
SM = pl.BlockSpec(memory_space=pltpu.SMEM)
BOTH = ("segment", "tile")

PAIRS = ((0, 1), (2, 6), (3, 7), (4, 8), (5, 9), (10, 14), (11, 15), (12,), (13,))
ROUTES = ((0, 1), (2, 6), (3, 7), (4, 8), (5, 9), (2, 6), (3, 7), (4, 8), (5, 9))
FETCH_AFTER = {0: 3, 2: 4, 4: 5, 6: 6, 8: 7, 9: 8}
SWAP_AFTER = {0: 1, 1: 2, 2: 3, 3: 4, 6: 5, 8: 6, 9: 7, 10: 8}
COLUMN = {0: 6, 1: 7, 2: 2, 3: 3, 8: 4, 9: 5, 4: 4, 5: 5, 6: 6, 7: 7, 10: 2, 11: 3, 12: 4, 13: 5}
ROUNDS = ((0, 1, 2, 3, 8, 9), (4, 5, 6, 7, 10, 11), (12, 13))
ROUND_AFTER = {11: 0, 13: 1, 14: 2}
ROUND_BY = {13: 0, 15: 2}
MOVED = {0: 6, 1: 7, 8: 12, 9: 13}
ACTIVE_ROWS = (0, 1, 8, 9)


def place(slot, quarter):
    tile = (slot // 4) * 8 + 2 * (slot % 4) + (quarter in (1, 2))
    return (quarter // 2) * TILES + tile


def helper(block, slot, quarter):
    return (COLUMN[block] + slot // 4 * 8) * TILES + 4 * quarter + slot % 4


def chunk_at(turn, k):
    chunk = k ^ lax.rem(turn, 4)
    return pl.multiple_of(chunk * PIECE, PIECE)


def send_sums(info, totals, squares, source, near, cross, stats):
    ones = jnp.ones((8, WIDTH), F32)
    rows = jnp.concatenate(
        [
            lax.dot_general(
                ones,
                part,
                (((1,), (1,)), ((), ())),
                precision=lax.Precision.HIGHEST,
                preferred_element_type=F32,
            )[0:1]
            for part in (totals, squares)
        ],
        axis=0,
    )
    high = rows.astype(BF).astype(F32)
    left = rows - high
    middle = left.astype(BF).astype(F32)
    low = left - middle
    coded = jnp.concatenate([high, middle, low, jnp.zeros((10, CH), F32)], axis=0)
    coded = jnp.concatenate([coded, jnp.zeros((16, 64), F32)], axis=1).astype(BF)
    even = lax.rem(info[0], 2) == 0
    first, last = source[0:CH, :], source[OWN - CH : OWN, :]
    near[0:CH, :] = jnp.where(even, last, first)
    cross[0:CH, :] = jnp.where(even, first, last)
    for i in range(3):
        part = coded[:, i * 128 : (i + 1) * 128]
        near[CH + 16 * i : CH + 16 * (i + 1), :] = part
        cross[CH + 16 * i : CH + 16 * (i + 1), :] = part
        stats[16 * i : 16 * (i + 1), :] = part


def first_body(info, *refs):
    pieces, (near, cross, stats, whole), (xs, sem) = refs[:4], refs[4:8], refs[8:]

    @pl.when(info[2] == 1)
    def _():
        copies = [
            pltpu.make_async_copy(pieces[k], xs.at[pl.ds(chunk_at(info[1], k), PIECE)], sem.at[k])
            for k in range(4)
        ]
        for copy in copies:
            copy.start()
        for copy in copies:
            copy.wait()
        final = pltpu.make_async_copy(xs, whole, sem.at[0])
        final.start()
        totals = squares = jnp.zeros((CH, WIDTH), F32)
        for r in range(ROWS):
            row = xs[r * CH : (r + 1) * CH, :].astype(F32)
            totals, squares = totals + row, squares + row * row
        send_sums(info, totals, squares, xs, near, cross, stats)
        final.wait()


def block_body(at_core, next_core, up_in, up_out, cut, last, info, *refs):
    refs = list(refs)

    def take(n):
        got = refs[:n]
        del refs[:n]
        return got

    source, near, cross, own_stats, far_stats, member = take(6)
    weights = take(2)
    if up_in:
        lateral_edges = take(2)
    if up_out:
        (lateral,), nexts = take(1), take(2)
    wholes = take(4 if cut else 1)
    if not last:
        near_out, cross_out, stats_out = take(3)
    if up_out:
        (summed_out,) = take(1)
    xs, result = source, wholes[0]
    if cut:
        (result,) = take(1)
    ws, ps, cat, totals, squares, in_sem, w_sem, out_sem = take(8)
    if up_in:
        (sk_in,) = take(1)
    if up_out:
        ls, sums = lateral, summed_out
        sk, l_sem = take(2)

    @pl.when(info[2] == 1)
    def _():
        core = info[0] // 2
        lead, tail = pl.ds(0, LEAD), pl.ds(LEAD, FULL - LEAD)
        head = pl.ds(LEAD - WIDTH, WIDTH)
        for at in range(2):

            @pl.when((core == at_core) == (at == 0))
            def _():
                pltpu.make_async_copy(weights[at].at[:, head], ps, w_sem.at[2]).start()
                pltpu.make_async_copy(weights[at].at[:, lead], ws, w_sem.at[0]).start()
                if up_in:
                    pltpu.make_async_copy(weights[at].at[:, tail], sk_in, w_sem.at[1]).start()

        if up_out:
            for at in range(2):

                @pl.when((core == next_core) == (at == 0))
                def _():
                    pltpu.make_async_copy(nexts[at].at[:, tail], sk, l_sem.at[1]).start()

        coded = [jnp.concatenate([ref[a + 16 * i : a + 16 * i + 16, :] for i in range(3)], axis=1)
                 for ref, a in ((own_stats, 0), (far_stats, 0), (near, CH), (cross, CH))]
        coded = jnp.concatenate(coded, axis=0)[:, 0:CH]
        groups = lax.dot_general(
            member[...], coded, (((1,), (1,)), ((), ())), preferred_element_type=F32
        )
        kind = lax.rem(lax.broadcasted_iota(jnp.int32, (CH, 64), 1), 16)
        even_kind = lax.rem(kind, 2) == 0
        mean = jnp.sum(jnp.where(even_kind, groups, 0.0), axis=1, keepdims=True) / MEMBERS
        mean_sq = jnp.sum(jnp.where(even_kind, 0.0, groups), axis=1, keepdims=True) / MEMBERS
        variance = jnp.maximum(mean_sq - mean * mean, 0.0)
        pltpu.make_async_copy(weights[0].at[:, head], ps, w_sem.at[2]).wait()
        tailing = ps[:, 64:128].astype(F32)
        params = tailing[:, 0:16] + tailing[:, 16:32] + tailing[:, 32:48]
        lane = lax.broadcasted_iota(jnp.int32, (CH, 16), 1)
        shift = jnp.sum(jnp.where(lane == info[1] + 8, params, 0.0), axis=1, keepdims=True)
        wide = (CH, WIDTH)
        gain = jnp.broadcast_to(params[:, 0:1] * lax.rsqrt(variance + 1e-5) * 0.5, wide)
        bias = jnp.broadcast_to(params[:, 1:2] * 0.5, wide)
        mean = jnp.broadcast_to(mean, wide)
        shift = jnp.broadcast_to(shift, wide)
        column = lax.broadcasted_iota(jnp.int32, wide, 1)

        def lift(x, row, keep=None):
            h = (x - mean) * gain + bias
            lifted = h * jnp.tanh(h) + h + shift
            if keep is not None:
                lifted = jnp.where(keep, lifted, 0.0)
            left = jnp.where(column == 0, 0.0, pltpu.roll(lifted, 1, 1)).astype(BF)
            right = jnp.where(column == WIDTH - 1, 0.0, pltpu.roll(lifted, WIDTH - 1, 1)).astype(BF)
            cols = pl.ds(row * WIDTH, WIDTH)
            if not isinstance(row, int):
                cols = pl.ds(pl.multiple_of(row * WIDTH, WIDTH), WIDTH)
            cat[0:CH, cols] = left
            cat[CH : 2 * CH, cols] = lifted.astype(BF)
            cat[2 * CH : 3 * CH, cols] = right

        even = lax.rem(info[0], 2) == 0
        near_rows, cross_rows = near[0:CH, :].astype(F32), cross[0:CH, :].astype(F32)
        if up_in:
            pltpu.make_async_copy(weights[0].at[:, tail], sk_in, w_sem.at[1]).wait()
            skip_in = sk_in[:, 0:CH]
            near_rows, cross_rows = (
                rows + jnp.dot(skip_in, edge[0:CH, :], preferred_element_type=F32)
                for rows, edge in zip((near_rows, cross_rows), lateral_edges)
            )
        def own_row(r):
            return slice(r * CH, (r + 1) * CH)

        if up_out:
            pltpu.make_async_copy(nexts[0].at[:, tail], sk, l_sem.at[1]).wait()
            skip = sk[:, 0:CH]
        totals[...] = jnp.zeros(wide, F32)
        squares[...] = jnp.zeros(wide, F32)

        def lift_at(row):
            if row == 0:
                lift(jnp.where(even, cross_rows, near_rows), 0, info[0] > 0)
            elif row == ROWS + 1:
                lift(jnp.where(even, near_rows, cross_rows), row, info[0] < 3)
            else:
                lift(xs[(row - 1) * CH : row * CH, :].astype(F32), row)

        for row in range(2):
            lift_at(row)
        lift_at(2)
        lift_at(3)
        pltpu.make_async_copy(weights[0].at[:, lead], ws, w_sem.at[0]).wait()
        for pair in range(ROWS // 2):
            if pair:
                lift_at(2 * pair + 2)
                lift_at(2 * pair + 3)
            convolved = sum(
                jnp.dot(
                    ws[:, dy * CAT : (dy + 1) * CAT],
                    cat[:, (2 * pair + dy) * WIDTH : (2 * pair + dy + 2) * WIDTH],
                    preferred_element_type=F32,
                )
                for dy in range(3)
            )
            rows = [own_row(2 * pair), own_row(2 * pair + 1)]
            if up_out:
                both = jnp.concatenate([ls[row, :] for row in rows], axis=1)
                projected = jnp.dot(skip, both, preferred_element_type=F32)
            for half, row in enumerate(rows):
                cols = slice(half * WIDTH, (half + 1) * WIDTH)
                kept = (xs[row, :].astype(F32) + convolved[:, cols]).astype(BF)
                result[row, :] = kept
                if not last:
                    following = kept.astype(F32)
                    if up_out:
                        following = following + projected[:, cols]
                        sums[row, :] = following
                    totals[...] += following
                    squares[...] += following * following

        finals = []
        if cut:
            finals = [
                pltpu.make_async_copy(
                    result.at[pl.ds(chunk_at(info[1], k), PIECE)], wholes[k], out_sem.at[k]
                )
                for k in range(4)
            ]
        for copy in finals:
            copy.start()
        if not last:
            send_sums(info, totals[...], squares[...], result, near_out, cross_out, stats_out)
        for copy in finals:
            copy.wait()


EXCHANGED = [
    jax.ShapeDtypeStruct((CH + STATS, WIDTH), BF),
    jax.ShapeDtypeStruct((CH + STATS, WIDTH), BF),
    jax.ShapeDtypeStruct((STATS, WIDTH), BF),
]
WHOLE = jax.ShapeDtypeStruct((OWN, WIDTH), BF)
PART = jax.ShapeDtypeStruct((PIECE, WIDTH), BF)


def first_call(info, pieces):
    return pl.pallas_call(
        first_body,
        out_shape=EXCHANGED + [WHOLE],
        in_specs=[SM] + [ANY] * 4,
        out_specs=[VM] * 3 + [ANY],
        scratch_shapes=[pltpu.VMEM((OWN, WIDTH), BF), pltpu.SemaphoreType.DMA((4,))],
        compiler_params=pltpu.CompilerParams(vmem_limit_bytes=16 * MIB),
        name="first_sums",
    )(info, *pieces)


def block_call(cores, info, source, exchanged, member, weights, lateral_edges, lateral, nexts, cut, last):
    up_in, up_out = lateral_edges is not None, lateral is not None
    operands = [source, *exchanged, member, *weights]
    specs = [VM] * 6 + [ANY] * 2
    shapes, out_specs = [WHOLE] + EXCHANGED, [VM] * 4
    scratch = []
    if cut:
        shapes, out_specs = [PART] * 4 + EXCHANGED, [ANY] * 4 + [VM] * 3
        scratch.append(pltpu.VMEM((OWN, WIDTH), BF))
    if last:
        shapes, out_specs = shapes[:4], out_specs[:4]
    scratch += [
        pltpu.VMEM((CH, LEAD), BF),
        pltpu.VMEM((CH, WIDTH), BF),
        pltpu.VMEM((CAT, (ROWS + 2) * WIDTH), BF),
        pltpu.VMEM((CH, WIDTH), F32),
        pltpu.VMEM((CH, WIDTH), F32),
        pltpu.SemaphoreType.DMA((1,)),
        pltpu.SemaphoreType.DMA((3,)),
        pltpu.SemaphoreType.DMA((4,)),
    ]
    if up_in:
        operands += list(lateral_edges)
        specs += [VM] * 2
        scratch.append(pltpu.VMEM((CH, FULL - LEAD), BF))
    if up_out:
        operands += [lateral, *nexts]
        specs += [VM] + [ANY] * 2
        shapes = shapes + [jax.ShapeDtypeStruct((OWN, WIDTH), F32)]
        out_specs = out_specs + [VM]
        scratch += [
            pltpu.VMEM((CH, FULL - LEAD), BF),
            pltpu.SemaphoreType.DMA((2,)),
        ]
    out = pl.pallas_call(
        functools.partial(block_body, *cores, up_in, up_out, cut, last),
        out_shape=shapes,
        in_specs=[SM] + specs,
        out_specs=out_specs,
        scratch_shapes=scratch,
        compiler_params=pltpu.CompilerParams(vmem_limit_bytes=28 * MIB),
        cost_estimate=pl.CostEstimate(
            flops=2 * OWN * WIDTH * TAPS, bytes_accessed=4 * MIB, transcendentals=OWN * WIDTH
        ),
        name="res_block",
    )(info, *operands)
    n = 4 if cut else 1
    return out[:4] if cut else out[0], out[n : n + 3], out[n + 3] if up_out else None


def split_body(count, info, *refs):
    wholes, outs, (held, in_sem, out_sem) = refs[:count], refs[count : count + 4], refs[count + 4 :]
    for at, ref in enumerate(wholes):

        @pl.when(info[0] == at)
        def _():
            arrive = pltpu.make_async_copy(ref, held, in_sem.at[0])
            arrive.start()
            arrive.wait()
            copies = [
                pltpu.make_async_copy(
                    held.at[pl.ds(chunk_at(info[1], k), PIECE)], outs[k], out_sem.at[k]
                )
                for k in range(4)
            ]
            for copy in copies:
                copy.start()
            for copy in copies:
                copy.wait()


def split(info, wholes):
    return pl.pallas_call(
        functools.partial(split_body, len(wholes)),
        out_shape=[PART] * 4,
        in_specs=[SM] + [ANY] * len(wholes),
        out_specs=[ANY] * 4,
        scratch_shapes=[
            pltpu.VMEM((OWN, WIDTH), BF),
            pltpu.SemaphoreType.DMA((1,)),
            pltpu.SemaphoreType.DMA((4,)),
        ],
        compiler_params=pltpu.CompilerParams(vmem_limit_bytes=16 * MIB),
        name="split",
    )(info, *wholes)


def collect_body(groups, moved, info, *refs):
    out, held, in_sem, out_sem = refs[-4:]

    def run(copies):
        for arrive, _ in copies:
            arrive.start()
        for arrive, leave in copies:
            arrive.wait()
            leave.start()
        for _, leave in copies:
            leave.wait()

    def pair(source, n, slot):
        return (
            pltpu.make_async_copy(source, held.at[n], in_sem.at[n]),
            pltpu.make_async_copy(held.at[n], out.at[slot], out_sem.at[n]),
        )

    for at in range(groups):

        @pl.when(info[0] == at)
        def _():
            copies = []
            for n in range(8):
                half = info[2] if n < 4 else 1 - info[2]
                slot = 4 * half + (info[1] ^ (n % 4))
                copies.append(pair(refs[at * 8 + n], n, slot))
            run(copies)

    for at in range(moved):

        @pl.when(info[0] == groups + at)
        def _():
            run([pair(refs[groups * 8 + at].at[n], n, n) for n in range(8)])


def collect(info, received, moved=()):
    flat = [piece for group in received for piece in group] + list(moved)
    return pl.pallas_call(
        functools.partial(collect_body, len(received), len(moved)),
        out_shape=jax.ShapeDtypeStruct((MICRO, PIECE, WIDTH), BF),
        in_specs=[SM] + [ANY] * len(flat),
        out_specs=ANY,
        scratch_shapes=[
            pltpu.VMEM((MICRO, PIECE, WIDTH), BF),
            pltpu.SemaphoreType.DMA((8,)),
            pltpu.SemaphoreType.DMA((8,)),
        ],
        compiler_params=pltpu.CompilerParams(vmem_limit_bytes=16 * MIB),
        name="collect",
    )(info, *flat)


def sinusoid(steps, half_width):
    rates = jnp.exp(-math.log(10000.0) * jnp.arange(half_width, dtype=F32) / half_width)
    angles = steps.astype(F32)[:, None] * rates[None, :]
    return jnp.concatenate([jnp.cos(angles), jnp.sin(angles)], axis=-1)


def on_device(
    features, timesteps, plan, conv_weight, skip_weight, time_weight, norm_gain, norm_bias
):
    segment, tile = lax.axis_index("segment"), lax.axis_index("tile")
    core, odd = segment % 2, tile % 2
    quarter = jnp.where(odd == 1, 1 + core, 3 * core)
    slot = 4 * (tile // 8) + (tile % 8) // 2
    active = (segment < 2).astype(jnp.int32)

    info = jnp.stack([quarter, slot, active]).astype(jnp.int32)
    inner = tile % 4

    def at_segment(values, other):
        got = jnp.full((), other, jnp.int32)
        for its_segment, value in values.items():
            got = jnp.where(segment == its_segment, value, got)
        return got

    served = lax.dynamic_index_in_dim(
        features, plan[jnp.minimum(segment, MICRO - 1)], 0, keepdims=False
    )
    served = served.transpose(0, 2, 1).reshape(PIECE, WIDTH)
    pieces = []
    for k in range(4):
        route = [
            (j * TILES + 4 * q + (k ^ j % 4), place(j, q)) for j in range(MICRO) for q in range(4)
        ]
        pieces.append(lax.ppermute(served, BOTH, route))

    encoded = sinusoid(timesteps[plan], time_weight.shape[1] // 2)
    shifts = jnp.dot(encoded, time_weight[0], precision=lax.Precision.HIGHEST)
    params = jnp.concatenate([norm_gain, norm_bias, jnp.zeros((6, CH), F32), shifts], axis=0)
    high = lax.reduce_precision(params, 8, 7)
    left = params - high
    middle = lax.reduce_precision(left, 8, 7)
    coded = jnp.concatenate([high, middle, left - middle], axis=0).astype(BF)
    columns = [conv_weight[0].T, coded.T, jnp.zeros((CH, LEAD - TAPS - STATS), BF)]
    lead = jnp.concatenate(columns, axis=1)
    columns += [skip_weight[0].T, jnp.zeros((CH, FULL - LEAD - CH), BF)]
    full = jnp.concatenate(columns, axis=1)
    first_up = BLOCKS - DOWN

    rows = [b for b in range(BLOCKS) if b not in ACTIVE_ROWS]
    relay_route = [(b * TILES + t, (b ^ 8) * TILES + t) for b in rows for t in range(TILES)]
    relayed = lax.ppermute(lax.optimization_barrier((full, pieces[-1]))[0], BOTH, relay_route)

    def fetch(index, after):
        own = relayed if PAIRS[index][0] >= 10 else lead
        own, _ = lax.optimization_barrier((own, after))
        first, second = ROUTES[index]
        return lax.ppermute(own, "segment", [(first, 0), (second, 1)])

    def exchange(near, cross, stats):
        other_tile = [(t, t ^ 1) for t in range(TILES)]
        other_core = [(b, b ^ 1) for b in range(BLOCKS)]
        both = [
            (b * TILES + t, (b ^ 1) * TILES + (t ^ 1)) for b in range(BLOCKS) for t in range(TILES)
        ]
        return (
            lax.ppermute(near, "tile", other_tile),
            lax.ppermute(cross, "segment", other_core),
            lax.ppermute(stats, BOTH, both),
        )

    def hand_over(block, whole):
        route = [(place(j, q), helper(block, j, q)) for j in range(MICRO) for q in range(4)]
        return lax.ppermute(whole, BOTH, route)

    def spread(at):
        group = ROUNDS[at]
        values = {COLUMN[b] + far: n for n, b in enumerate(group) for far in (0, 8)}
        outs = split(
            jnp.stack([at_segment(values, -1), inner]).astype(jnp.int32),
            [passing[b] for b in group],
        )
        got = [outs[0]]
        for far in (0, 8):
            for k in range(4):
                if k or far:
                    route = [(b * TILES + t, (b ^ far) * TILES + (t ^ k)) for b in rows for t in range(TILES)]
                    got.append(lax.ppermute(outs[k], BOTH, route))
        return got

    def straight(outs):
        got = []
        for high in range(2):
            for k in range(4):
                route = [
                    (place(j, q), (BLOCKS - 1) * TILES + 4 * q + (k ^ j % 4))
                    for j in range(4 * high, 4 * high + 4)
                    for q in range(4)
                ]
                got.append(lax.ppermute(outs[k], BOTH, route))
        return got

    def collect_at(values, received, moved=(), high_half=segment // 8):
        chosen = jnp.stack([at_segment(values, -1), inner, high_half]).astype(jnp.int32)
        return collect(chosen, received, moved)

    other_core = [(b, b ^ 1) for b in range(BLOCKS)]
    member_at = jnp.arange(CH) // GROUP
    member = (member_at[:, None] == member_at[None, :]).astype(BF)
    weights, cores, fetched = {}, {}, {}

    def swap_cores(index, own):
        both = own, lax.ppermute(own, "segment", [(b, b ^ 1) for b in range(BLOCKS)])
        for at, block in enumerate(PAIRS[index]):
            weights[block], cores[block] = both, at

    swap_cores(0, lead)
    *exchanged, source = first_call(info, pieces)
    for index in (1, 2):
        fetched[index] = fetch(index, pieces[-1])
    wholes, edges_of, passing, received = [], {}, [], {}
    for block in range(BLOCKS):
        up_in, up_out = block >= first_up, first_up - 1 <= block < BLOCKS - 1
        near, cross, stats = exchanged
        near_in, cross_in, far = exchange(near, cross, stats)
        edges_of[block] = (near_in, cross_in)
        if block >= 2:
            source, near_in, cross_in, far, passing[block - 2] = lax.optimization_barrier(
                (source, near_in, cross_in, far, passing[block - 2])
            )
        if block - 1 in ROUND_AFTER:
            received[ROUND_AFTER[block - 1]] = spread(ROUND_AFTER[block - 1])
        if block in ROUND_BY:
            at = ROUND_BY[block]
            source, received[at] = lax.optimization_barrier((source, received[at]))
        if block == 13:
            values = {its_segment: 0 for its_segment in MOVED.values()}
            moving = collect_at(values, [received[0]])
            route = [(source_of * TILES + t, b * TILES + t) for b, source_of in MOVED.items() for t in range(TILES)]
            moved = lax.ppermute(moving, BOTH, route)
        cut, last = block >= BLOCKS - 2, block == BLOCKS - 1
        whole, exchanged, summed = block_call(
            (cores[block], cores.get(block + 1, 0)),
            info,
            source,
            (near_in, cross_in, stats, far),
            member,
            weights[block],
            edges_of[BLOCKS - block] if up_in else None,
            wholes[BLOCKS - 2 - block] if up_out else None,
            weights[block + 1] if up_out else None,
            cut,
            last,
        )
        wholes.append(whole)
        source = summed if up_out else whole
        if cut:
            received[block] = straight(whole)
        else:
            passing.append(hand_over(block, whole))
        if block in SWAP_AFTER:
            index = SWAP_AFTER[block]
            own, _ = lax.optimization_barrier((fetched[index], whole))
            swap_cores(index, own)
        if block in FETCH_AFTER:
            index = FETCH_AFTER[block]
            fetched[index] = fetch(index, whole)
    zero = jnp.zeros((), jnp.int32)
    early = collect_at({BLOCKS - 1: 0}, [received[BLOCKS - 2]], high_half=zero)
    swapped = lax.ppermute(early, "segment", other_core)
    values = {BLOCKS - 1: 3, BLOCKS - 2: 4} | {b: 5 for b in MOVED}
    for at, group in enumerate(ROUNDS):
        values |= {b: at for b in group if b not in MOVED}
    half = jnp.where(segment == BLOCKS - 1, 0, segment // 8)
    lists = [received[0], received[1], received[2], received[BLOCKS - 1]]
    out = collect_at(values, lists, [swapped, moved], half)
    out = out.reshape(1, MICRO, 3, CH, WIDTH)
    return out.transpose(0, 1, 2, 4, 3)


def solution(mesh):
    placed = (
        P(None, "tile", None, None),
        P(),
        P(),
        P("segment", None, None),
        P("segment", None, None),
        P("segment", None, None),
        P("segment", None),
        P("segment", None),
    )
    return jax.shard_map(
        on_device,
        mesh=mesh,
        in_specs=placed,
        out_specs=P("segment", None, "tile", None, None),
        check_vma=False,
    )
```

```python
import functools
import math

import jax
import jax.numpy as jnp
from jax import lax
from jax.experimental import pallas as pl
from jax.experimental.pallas import tpu as pltpu
from jax.sharding import PartitionSpec as P

BLOCKS, MICRO, TILES, DOWN = 16, 8, 16, 4
WIDTH, CH, GROUP = 128, 320, 10
CAT = 3 * CH
TAPS = 9 * CH
ROWS = 12
PIECE = 3 * CH
OWN = ROWS * CH
MEMBERS = float(48 * WIDTH * GROUP)
MIB = 1024 * 1024
LEAD = 2944
FULL = LEAD + 384
STATS = 48
BF, F32 = jnp.bfloat16, jnp.float32
ANY = pl.BlockSpec(memory_space=pl.ANY)
VM = pl.BlockSpec(memory_space=pltpu.VMEM)
SM = pl.BlockSpec(memory_space=pltpu.SMEM)
BOTH = ("segment", "tile")

PAIRS = ((0, 1), (2, 6), (3, 7), (4, 8), (5, 9), (10, 14), (11, 15), (12, 13))
FETCH_AFTER = {0: 3, 2: 4, 4: 5, 6: 6, 8: 7}
SWAP_AFTER = {0: 1, 1: 2, 2: 3, 3: 4, 6: 5, 8: 6, 10: 7}


def place(slot, quarter):
    tile = (slot // 4) * 8 + 2 * (slot % 4) + (quarter in (1, 2))
    return (quarter // 2) * TILES + tile


def helper(block, slot, quarter):
    return (block % 8 + slot // 4 * 8) * TILES + 4 * quarter + slot % 4


def chunk_at(turn, k):
    chunk = k ^ lax.rem(turn, 4)
    return pl.multiple_of(chunk * PIECE, PIECE)


def send_sums(info, totals, squares, source, near, cross, stats):
    ones = jnp.ones((8, WIDTH), F32)
    rows = jnp.concatenate(
        [
            lax.dot_general(
                ones,
                part,
                (((1,), (1,)), ((), ())),
                precision=lax.Precision.HIGHEST,
                preferred_element_type=F32,
            )[0:1]
            for part in (totals, squares)
        ],
        axis=0,
    )
    high = rows.astype(BF).astype(F32)
    left = rows - high
    middle = left.astype(BF).astype(F32)
    low = left - middle
    coded = jnp.concatenate([high, middle, low, jnp.zeros((10, CH), F32)], axis=0)
    coded = jnp.concatenate([coded, jnp.zeros((16, 64), F32)], axis=1).astype(BF)
    even = lax.rem(info[0], 2) == 0
    first, last = source[0:CH, :], source[OWN - CH : OWN, :]
    near[0:CH, :] = jnp.where(even, last, first)
    cross[0:CH, :] = jnp.where(even, first, last)
    for i in range(3):
        part = coded[:, i * 128 : (i + 1) * 128]
        near[CH + 16 * i : CH + 16 * (i + 1), :] = part
        cross[CH + 16 * i : CH + 16 * (i + 1), :] = part
        stats[16 * i : 16 * (i + 1), :] = part


def first_body(info, *refs):
    pieces, (near, cross, stats, whole), (xs, sem) = refs[:4], refs[4:8], refs[8:]

    @pl.when(info[2] == 1)
    def _():
        copies = [
            pltpu.make_async_copy(pieces[k], xs.at[pl.ds(chunk_at(info[1], k), PIECE)], sem.at[k])
            for k in range(4)
        ]
        for copy in copies:
            copy.start()
        for copy in copies:
            copy.wait()
        final = pltpu.make_async_copy(xs, whole, sem.at[0])
        final.start()
        totals = squares = jnp.zeros((CH, WIDTH), F32)
        for r in range(ROWS):
            row = xs[r * CH : (r + 1) * CH, :].astype(F32)
            totals, squares = totals + row, squares + row * row
        send_sums(info, totals, squares, xs, near, cross, stats)
        final.wait()


def block_body(at_core, next_core, up_in, up_out, last, info, *refs):
    refs = list(refs)

    def take(n):
        got = refs[:n]
        del refs[:n]
        return got

    source, near, cross, own_stats, far_stats, member = take(6)
    weights = take(2)
    if up_in:
        lateral_edges = take(2)
    if up_out:
        (lateral,), nexts = take(1), take(2)
    (result,) = take(1)
    if not last:
        near_out, cross_out, stats_out = take(3)
    if up_out:
        (summed_out,) = take(1)
    xs = source
    ws, ps, cat, totals, squares, w_sem = take(6)
    if up_in:
        (sk_in,) = take(1)
    if up_out:
        ls, sums = lateral, summed_out
        sk, l_sem = take(2)

    @pl.when(info[2] == 1)
    def _():
        core = info[0] // 2
        lead, tail = pl.ds(0, LEAD), pl.ds(LEAD, FULL - LEAD)
        head = pl.ds(LEAD - WIDTH, WIDTH)
        for at in range(2):

            @pl.when((core == at_core) == (at == 0))
            def _():
                pltpu.make_async_copy(weights[at].at[:, head], ps, w_sem.at[2]).start()
                pltpu.make_async_copy(weights[at].at[:, lead], ws, w_sem.at[0]).start()
                if up_in:
                    pltpu.make_async_copy(weights[at].at[:, tail], sk_in, w_sem.at[1]).start()

        if up_out:
            for at in range(2):

                @pl.when((core == next_core) == (at == 0))
                def _():
                    pltpu.make_async_copy(nexts[at].at[:, tail], sk, l_sem.at[1]).start()

        coded = [jnp.concatenate([ref[a + 16 * i : a + 16 * i + 16, :] for i in range(3)], axis=1)
                 for ref, a in ((own_stats, 0), (far_stats, 0), (near, CH), (cross, CH))]
        coded = jnp.concatenate(coded, axis=0)[:, 0:CH]
        groups = lax.dot_general(
            member[...], coded, (((1,), (1,)), ((), ())), preferred_element_type=F32
        )
        kind = lax.rem(lax.broadcasted_iota(jnp.int32, (CH, 64), 1), 16)
        even_kind = lax.rem(kind, 2) == 0
        mean = jnp.sum(jnp.where(even_kind, groups, 0.0), axis=1, keepdims=True) / MEMBERS
        mean_sq = jnp.sum(jnp.where(even_kind, 0.0, groups), axis=1, keepdims=True) / MEMBERS
        variance = jnp.maximum(mean_sq - mean * mean, 0.0)
        pltpu.make_async_copy(weights[0].at[:, head], ps, w_sem.at[2]).wait()
        tailing = ps[:, 64:128].astype(F32)
        params = tailing[:, 0:16] + tailing[:, 16:32] + tailing[:, 32:48]
        lane = lax.broadcasted_iota(jnp.int32, (CH, 16), 1)
        shift = jnp.sum(jnp.where(lane == info[1] + 8, params, 0.0), axis=1, keepdims=True)
        wide = (CH, WIDTH)
        gain = jnp.broadcast_to(params[:, 0:1] * lax.rsqrt(variance + 1e-5) * 0.5, wide)
        bias = jnp.broadcast_to(params[:, 1:2] * 0.5, wide)
        mean = jnp.broadcast_to(mean, wide)
        shift = jnp.broadcast_to(shift, wide)
        column = lax.broadcasted_iota(jnp.int32, wide, 1)

        def lift(x, row, keep=None):
            h = (x - mean) * gain + bias
            lifted = h * jnp.tanh(h) + h + shift
            if keep is not None:
                lifted = jnp.where(keep, lifted, 0.0)
            left = jnp.where(column == 0, 0.0, pltpu.roll(lifted, 1, 1)).astype(BF)
            right = jnp.where(column == WIDTH - 1, 0.0, pltpu.roll(lifted, WIDTH - 1, 1)).astype(BF)
            cols = pl.ds(row * WIDTH, WIDTH)
            if not isinstance(row, int):
                cols = pl.ds(pl.multiple_of(row * WIDTH, WIDTH), WIDTH)
            cat[0:CH, cols] = left
            cat[CH : 2 * CH, cols] = lifted.astype(BF)
            cat[2 * CH : 3 * CH, cols] = right

        even = lax.rem(info[0], 2) == 0
        near_rows, cross_rows = near[0:CH, :].astype(F32), cross[0:CH, :].astype(F32)
        if up_in:
            pltpu.make_async_copy(weights[0].at[:, tail], sk_in, w_sem.at[1]).wait()
            skip_in = sk_in[:, 0:CH]
            near_rows, cross_rows = (
                rows + jnp.dot(skip_in, edge[0:CH, :], preferred_element_type=F32)
                for rows, edge in zip((near_rows, cross_rows), lateral_edges)
            )
        def own_row(r):
            return slice(r * CH, (r + 1) * CH)

        if up_out:
            pltpu.make_async_copy(nexts[0].at[:, tail], sk, l_sem.at[1]).wait()
            skip = sk[:, 0:CH]
        totals[...] = jnp.zeros(wide, F32)
        squares[...] = jnp.zeros(wide, F32)

        def lift_at(row):
            if row == 0:
                lift(jnp.where(even, cross_rows, near_rows), 0, info[0] > 0)
            elif row == ROWS + 1:
                lift(jnp.where(even, near_rows, cross_rows), row, info[0] < 3)
            else:
                lift(xs[(row - 1) * CH : row * CH, :].astype(F32), row)

        for row in range(2):
            lift_at(row)
        lift_at(2)
        lift_at(3)
        pltpu.make_async_copy(weights[0].at[:, lead], ws, w_sem.at[0]).wait()
        for pair in range(ROWS // 2):
            if pair:
                lift_at(2 * pair + 2)
                lift_at(2 * pair + 3)
            convolved = sum(
                jnp.dot(
                    ws[:, dy * CAT : (dy + 1) * CAT],
                    cat[:, (2 * pair + dy) * WIDTH : (2 * pair + dy + 2) * WIDTH],
                    preferred_element_type=F32,
                )
                for dy in range(3)
            )
            rows = [own_row(2 * pair), own_row(2 * pair + 1)]
            if up_out:
                both = jnp.concatenate([ls[row, :] for row in rows], axis=1)
                projected = jnp.dot(skip, both, preferred_element_type=F32)
            for half, row in enumerate(rows):
                cols = slice(half * WIDTH, (half + 1) * WIDTH)
                kept = (xs[row, :].astype(F32) + convolved[:, cols]).astype(BF)
                result[row, :] = kept
                if not last:
                    following = kept.astype(F32)
                    if up_out:
                        following = following + projected[:, cols]
                        sums[row, :] = following
                    totals[...] += following
                    squares[...] += following * following

        if not last:
            send_sums(info, totals[...], squares[...], result, near_out, cross_out, stats_out)


EXCHANGED = [
    jax.ShapeDtypeStruct((CH + STATS, WIDTH), BF),
    jax.ShapeDtypeStruct((CH + STATS, WIDTH), BF),
    jax.ShapeDtypeStruct((STATS, WIDTH), BF),
]
WHOLE = jax.ShapeDtypeStruct((OWN, WIDTH), BF)


def first_call(info, pieces):
    return pl.pallas_call(
        first_body,
        out_shape=EXCHANGED + [WHOLE],
        in_specs=[SM] + [ANY] * 4,
        out_specs=[VM] * 3 + [ANY],
        scratch_shapes=[pltpu.VMEM((OWN, WIDTH), BF), pltpu.SemaphoreType.DMA((4,))],
        compiler_params=pltpu.CompilerParams(vmem_limit_bytes=16 * MIB),
        name="first_sums",
    )(info, *pieces)


def block_call(cores, info, source, exchanged, member, weights, lateral_edges, lateral, nexts, last):
    up_in, up_out = lateral_edges is not None, lateral is not None
    operands = [source, *exchanged, member, *weights]
    specs = [VM] * 6 + [ANY] * 2
    shapes, out_specs = [WHOLE] + EXCHANGED, [VM] * 4
    if last:
        shapes, out_specs = shapes[:1], out_specs[:1]
    scratch = [
        pltpu.VMEM((CH, LEAD), BF),
        pltpu.VMEM((CH, WIDTH), BF),
        pltpu.VMEM((CAT, (ROWS + 2) * WIDTH), BF),
        pltpu.VMEM((CH, WIDTH), F32),
        pltpu.VMEM((CH, WIDTH), F32),
        pltpu.SemaphoreType.DMA((3,)),
    ]
    if up_in:
        operands += list(lateral_edges)
        specs += [VM] * 2
        scratch.append(pltpu.VMEM((CH, FULL - LEAD), BF))
    if up_out:
        operands += [lateral, *nexts]
        specs += [VM] + [ANY] * 2
        shapes = shapes + [jax.ShapeDtypeStruct((OWN, WIDTH), F32)]
        out_specs = out_specs + [VM]
        scratch += [
            pltpu.VMEM((CH, FULL - LEAD), BF),
            pltpu.SemaphoreType.DMA((2,)),
        ]
    out = pl.pallas_call(
        functools.partial(block_body, *cores, up_in, up_out, last),
        out_shape=shapes,
        in_specs=[SM] + specs,
        out_specs=out_specs,
        scratch_shapes=scratch,
        compiler_params=pltpu.CompilerParams(vmem_limit_bytes=28 * MIB),
        cost_estimate=pl.CostEstimate(
            flops=2 * OWN * WIDTH * TAPS, bytes_accessed=4 * MIB, transcendentals=OWN * WIDTH
        ),
        name="res_block",
    )(info, *operands)
    return out[0], out[1:4], out[4] if up_out else None


def pick_body(info, *refs):
    wholes, out, held, in_sem, out_sem = refs[:BLOCKS], *refs[BLOCKS:]
    for at in range(8):

        @pl.when(info[0] == at)
        def _():
            copies = [
                (
                    pltpu.make_async_copy(wholes[at + 8 * n], held.at[n], in_sem.at[n]),
                    pltpu.make_async_copy(held.at[n], out.at[n], out_sem.at[n]),
                )
                for n in range(2)
            ]
            for arrive, _ in copies:
                arrive.start()
            for arrive, leave in copies:
                arrive.wait()
                leave.start()
            for _, leave in copies:
                leave.wait()


def pick(info, wholes):
    return pl.pallas_call(
        pick_body,
        out_shape=jax.ShapeDtypeStruct((2, OWN, WIDTH), BF),
        in_specs=[SM] + [ANY] * BLOCKS,
        out_specs=ANY,
        scratch_shapes=[
            pltpu.VMEM((2, OWN, WIDTH), BF),
            pltpu.SemaphoreType.DMA((2,)),
            pltpu.SemaphoreType.DMA((2,)),
        ],
        compiler_params=pltpu.CompilerParams(vmem_limit_bytes=16 * MIB),
        name="pick",
    )(info, *wholes)


def sinusoid(steps, half_width):
    rates = jnp.exp(-math.log(10000.0) * jnp.arange(half_width, dtype=F32) / half_width)
    angles = steps.astype(F32)[:, None] * rates[None, :]
    return jnp.concatenate([jnp.cos(angles), jnp.sin(angles)], axis=-1)


def on_device(
    features, timesteps, plan, conv_weight, skip_weight, time_weight, norm_gain, norm_bias
):
    segment, tile = lax.axis_index("segment"), lax.axis_index("tile")
    core, odd = segment % 2, tile % 2
    quarter = jnp.where(odd == 1, 1 + core, 3 * core)
    slot = 4 * (tile // 8) + (tile % 8) // 2
    active = (segment < 2).astype(jnp.int32)

    info = jnp.stack([quarter, slot, active]).astype(jnp.int32)

    served = lax.dynamic_index_in_dim(
        features, plan[jnp.minimum(segment, MICRO - 1)], 0, keepdims=False
    )
    served = served.transpose(0, 2, 1).reshape(PIECE, WIDTH)
    pieces = []
    for k in range(4):
        route = [
            (j * TILES + 4 * q + (k ^ j % 4), place(j, q)) for j in range(MICRO) for q in range(4)
        ]
        pieces.append(lax.ppermute(served, BOTH, route))

    encoded = sinusoid(timesteps[plan], time_weight.shape[1] // 2)
    shifts = jnp.dot(encoded, time_weight[0], precision=lax.Precision.HIGHEST)
    params = jnp.concatenate([norm_gain, norm_bias, jnp.zeros((6, CH), F32), shifts], axis=0)
    high = lax.reduce_precision(params, 8, 7)
    left = params - high
    middle = lax.reduce_precision(left, 8, 7)
    coded = jnp.concatenate([high, middle, left - middle], axis=0).astype(BF)
    columns = [conv_weight[0].T, coded.T, jnp.zeros((CH, LEAD - TAPS - STATS), BF)]
    lead = jnp.concatenate(columns, axis=1)
    columns += [skip_weight[0].T, jnp.zeros((CH, FULL - LEAD - CH), BF)]
    full = jnp.concatenate(columns, axis=1)
    first_up = BLOCKS - DOWN

    lead, full = lax.optimization_barrier((lead, full))

    def fetch(index, after):
        own = full if max(PAIRS[index]) >= first_up else lead
        own, _ = lax.optimization_barrier((own, after))
        first, second = PAIRS[index]
        return lax.ppermute(own, "segment", [(first, 0), (second, 1)])

    def exchange(near, cross, stats):
        other_tile = [(t, t ^ 1) for t in range(TILES)]
        other_core = [(b, b ^ 1) for b in range(BLOCKS)]
        both = [
            (b * TILES + t, (b ^ 1) * TILES + (t ^ 1)) for b in range(BLOCKS) for t in range(TILES)
        ]
        return (
            lax.ppermute(near, "tile", other_tile),
            lax.ppermute(cross, "segment", other_core),
            lax.ppermute(stats, BOTH, both),
        )

    def hand_over(block, whole):
        route = [(place(j, q), helper(block, j, q)) for j in range(MICRO) for q in range(4)]
        return lax.ppermute(whole, BOTH, route)

    member_at = jnp.arange(CH) // GROUP
    member = (member_at[:, None] == member_at[None, :]).astype(BF)
    weights, cores, fetched = {}, {}, {}

    def swap_cores(index, own):
        both = own, lax.ppermute(own, "segment", [(b, b ^ 1) for b in range(BLOCKS)])
        for at, block in enumerate(PAIRS[index]):
            weights[block], cores[block] = both, at

    swap_cores(0, lead)
    *exchanged, source = first_call(info, pieces)
    for index in (1, 2):
        fetched[index] = fetch(index, pieces[-1])
    wholes, edges_of, passing = [], {}, []
    for block in range(BLOCKS):
        up_in, up_out = block >= first_up, first_up - 1 <= block < BLOCKS - 1
        near, cross, stats = exchanged
        near_in, cross_in, far = exchange(near, cross, stats)
        edges_of[block] = (near_in, cross_in)
        if block >= 2:
            source, near_in, cross_in, far, passing[block - 2] = lax.optimization_barrier(
                (source, near_in, cross_in, far, passing[block - 2])
            )
        whole, exchanged, summed = block_call(
            (cores[block], cores.get(block + 1, 0)),
            info,
            source,
            (near_in, cross_in, stats, far),
            member,
            weights[block],
            edges_of[BLOCKS - block] if up_in else None,
            wholes[BLOCKS - 2 - block] if up_out else None,
            weights[block + 1] if up_out else None,
            block == BLOCKS - 1,
        )
        wholes.append(whole)
        source = summed if up_out else whole
        passing.append(hand_over(block, whole))
        if block in SWAP_AFTER:
            index = SWAP_AFTER[block]
            own, _ = lax.optimization_barrier((fetched[index], whole))
            swap_cores(index, own)
        if block in FETCH_AFTER:
            index = FETCH_AFTER[block]
            fetched[index] = fetch(index, whole)
    held = pick((segment % 8).astype(jnp.int32)[None], passing)
    peers = [
        [(s + 8 * far) * TILES + 4 * q + i for far in range(2) for i in range(4)]
        for s in range(8)
        for q in range(4)
    ]
    out = lax.all_to_all(
        held.reshape(MICRO, PIECE, WIDTH), BOTH, 0, 0, axis_index_groups=peers, tiled=True
    )
    out = out.reshape(1, MICRO, 3, CH, WIDTH)
    return out.transpose(0, 1, 2, 4, 3)


def solution(mesh):
    placed = (
        P(None, "tile", None, None),
        P(),
        P(),
        P("segment", None, None),
        P("segment", None, None),
        P("segment", None, None),
        P("segment", None),
        P("segment", None),
    )
    return jax.shard_map(
        on_device,
        mesh=mesh,
        in_specs=placed,
        out_specs=P("segment", None, "tile", None, None),
        check_vma=False,
    )
```

```python
import functools
import math

import jax
import jax.numpy as jnp
from jax import lax
from jax.experimental import pallas as pl
from jax.experimental.pallas import tpu as pltpu
from jax.sharding import PartitionSpec as P

BLOCKS, MICRO, TILES, DOWN = 16, 8, 16, 4
WIDTH, CH, GROUP = 128, 320, 10
CAT = 3 * CH
TAPS = 9 * CH
ROWS = 12
PIECE = 3 * CH
OWN = ROWS * CH
MEMBERS = float(48 * WIDTH * GROUP)
MIB = 1024 * 1024
STATS = 48
BF, F32 = jnp.bfloat16, jnp.float32
ANY = pl.BlockSpec(memory_space=pl.ANY)
VM = pl.BlockSpec(memory_space=pltpu.VMEM)
SM = pl.BlockSpec(memory_space=pltpu.SMEM)
BOTH = ("segment", "tile")

PAIRS = ((0, 1), (2, 6), (3, 7), (4, 8), (5, 9), (10, 14), (11, 15), (12, 13))
FETCH_AFTER = {0: 3, 2: 4, 4: 5, 6: 6, 8: 7}
SWAP_AFTER = {0: 1, 1: 2, 2: 3, 3: 4, 6: 5, 8: 6, 10: 7}


MOVE_AFTER = {4: 0, 5: 1, 12: 8, 13: 9}


def place(slot, quarter):
    tile = (slot // 4) * 8 + 2 * (slot % 4) + (quarter in (1, 2))
    return (quarter // 2) * TILES + tile


def helper(block, slot, quarter):
    column = block % 8 if block % 8 > 1 else 6 + block % 8
    return (column + slot // 4 * 8) * TILES + 4 * quarter + slot % 4


def chunk_at(turn, k):
    chunk = k ^ lax.rem(turn, 4)
    return pl.multiple_of(chunk * PIECE, PIECE)


def send_sums(info, totals, squares, source, near, cross, stats):
    ones = jnp.ones((8, WIDTH), F32)
    rows = jnp.concatenate(
        [
            lax.dot_general(
                ones,
                part,
                (((1,), (1,)), ((), ())),
                precision=lax.Precision.HIGHEST,
                preferred_element_type=F32,
            )[0:1]
            for part in (totals, squares)
        ],
        axis=0,
    )
    high = rows.astype(BF).astype(F32)
    left = rows - high
    middle = left.astype(BF).astype(F32)
    low = left - middle
    coded = jnp.concatenate([high, middle, low, jnp.zeros((10, CH), F32)], axis=0)
    coded = jnp.concatenate([coded, jnp.zeros((16, 64), F32)], axis=1).astype(BF)
    even = lax.rem(info[0], 2) == 0
    first, last = source[0:CH, :], source[OWN - CH : OWN, :]
    near[0:CH, :] = jnp.where(even, last, first)
    cross[0:CH, :] = jnp.where(even, first, last)
    for i in range(3):
        part = coded[:, i * 128 : (i + 1) * 128]
        near[CH + 16 * i : CH + 16 * (i + 1), :] = part
        cross[CH + 16 * i : CH + 16 * (i + 1), :] = part
        stats[16 * i : 16 * (i + 1), :] = part


def first_body(info, *refs):
    pieces, (near, cross, stats, whole), (xs, sem) = refs[:4], refs[4:8], refs[8:]

    @pl.when(info[2] == 1)
    def _():
        copies = [
            pltpu.make_async_copy(pieces[k], xs.at[pl.ds(chunk_at(info[1], k), PIECE)], sem.at[k])
            for k in range(4)
        ]
        for copy in copies:
            copy.start()
        for copy in copies:
            copy.wait()
        final = pltpu.make_async_copy(xs, whole, sem.at[0])
        final.start()
        totals = squares = jnp.zeros((CH, WIDTH), F32)
        for r in range(ROWS):
            row = xs[r * CH : (r + 1) * CH, :].astype(F32)
            totals, squares = totals + row, squares + row * row
        send_sums(info, totals, squares, xs, near, cross, stats)
        final.wait()


def block_body(block, at_core, up_in, up_out, last, info, *refs):
    refs = list(refs)

    def take(n):
        got = refs[:n]
        del refs[:n]
        return got

    source, near, cross, own_stats, far_stats, member, params_all = take(7)
    weights = take(2)
    if up_in or up_out:
        (skips,) = take(1)
    if up_in:
        lateral_edges = take(2)
    if up_out:
        (lateral,) = take(1)
    (result,) = take(1)
    if not last:
        near_out, cross_out, stats_out = take(3)
    if up_out:
        (summed_out,) = take(1)
    xs = source
    ws, ps, cat, totals, squares, w_sem = take(6)
    if up_in:
        (sk_in,) = take(1)
    if up_out:
        ls, sums = lateral, summed_out
        sk, l_sem = take(2)

    @pl.when(info[2] == 1)
    def _():
        core = info[0] // 2
        params_copy = pltpu.make_async_copy(params_all.at[block], ps, w_sem.at[2])
        params_copy.start()
        for at in range(2):

            @pl.when((core == at_core) == (at == 0))
            def _():
                pltpu.make_async_copy(weights[at], ws, w_sem.at[0]).start()

        if up_in:
            in_copy = pltpu.make_async_copy(skips.at[block], sk_in, w_sem.at[1])
            in_copy.start()
        if up_out:
            out_copy = pltpu.make_async_copy(skips.at[block + 1], sk, l_sem.at[0])
            out_copy.start()

        coded = [jnp.concatenate([ref[a + 16 * i : a + 16 * i + 16, :] for i in range(3)], axis=1)
                 for ref, a in ((own_stats, 0), (far_stats, 0), (near, CH), (cross, CH))]
        coded = jnp.concatenate(coded, axis=0)[:, 0:CH]
        groups = lax.dot_general(
            member[...], coded, (((1,), (1,)), ((), ())), preferred_element_type=F32
        )
        kind = lax.rem(lax.broadcasted_iota(jnp.int32, (CH, 64), 1), 16)
        even_kind = lax.rem(kind, 2) == 0
        mean = jnp.sum(jnp.where(even_kind, groups, 0.0), axis=1, keepdims=True) / MEMBERS
        mean_sq = jnp.sum(jnp.where(even_kind, 0.0, groups), axis=1, keepdims=True) / MEMBERS
        variance = jnp.maximum(mean_sq - mean * mean, 0.0)
        params_copy.wait()
        params = jnp.transpose(ps[...])
        lane = lax.broadcasted_iota(jnp.int32, (CH, 16), 1)
        shift = jnp.sum(jnp.where(lane == info[1] + 8, params, 0.0), axis=1, keepdims=True)
        wide = (CH, WIDTH)
        gain = jnp.broadcast_to(params[:, 0:1] * lax.rsqrt(variance + 1e-5) * 0.5, wide)
        bias = jnp.broadcast_to(params[:, 1:2] * 0.5, wide)
        mean = jnp.broadcast_to(mean, wide)
        shift = jnp.broadcast_to(shift, wide)
        column = lax.broadcasted_iota(jnp.int32, wide, 1)

        def lift(x, row, keep=None):
            h = (x - mean) * gain + bias
            lifted = h * jnp.tanh(h) + h + shift
            if keep is not None:
                lifted = jnp.where(keep, lifted, 0.0)
            left = jnp.where(column == 0, 0.0, pltpu.roll(lifted, 1, 1)).astype(BF)
            right = jnp.where(column == WIDTH - 1, 0.0, pltpu.roll(lifted, WIDTH - 1, 1)).astype(BF)
            cols = pl.ds(row * WIDTH, WIDTH)
            if not isinstance(row, int):
                cols = pl.ds(pl.multiple_of(row * WIDTH, WIDTH), WIDTH)
            cat[0:CH, cols] = left
            cat[CH : 2 * CH, cols] = lifted.astype(BF)
            cat[2 * CH : 3 * CH, cols] = right

        even = lax.rem(info[0], 2) == 0
        near_rows, cross_rows = near[0:CH, :].astype(F32), cross[0:CH, :].astype(F32)
        if up_in:
            in_copy.wait()
            skip_in = sk_in[...]
            near_rows, cross_rows = (
                rows + jnp.dot(skip_in, edge[0:CH, :], preferred_element_type=F32)
                for rows, edge in zip((near_rows, cross_rows), lateral_edges)
            )
        def own_row(r):
            return slice(r * CH, (r + 1) * CH)

        if up_out:
            out_copy.wait()
            skip = sk[...]
        totals[...] = jnp.zeros(wide, F32)
        squares[...] = jnp.zeros(wide, F32)

        def lift_at(row):
            if row == 0:
                lift(jnp.where(even, cross_rows, near_rows), 0, info[0] > 0)
            elif row == ROWS + 1:
                lift(jnp.where(even, near_rows, cross_rows), row, info[0] < 3)
            else:
                lift(xs[(row - 1) * CH : row * CH, :].astype(F32), row)

        for row in range(2):
            lift_at(row)
        lift_at(2)
        lift_at(3)
        pltpu.make_async_copy(weights[0], ws, w_sem.at[0]).wait()
        for pair in range(ROWS // 2):
            if pair:
                lift_at(2 * pair + 2)
                lift_at(2 * pair + 3)
            convolved = sum(
                jnp.dot(
                    ws[:, dy * CAT : (dy + 1) * CAT],
                    cat[:, (2 * pair + dy) * WIDTH : (2 * pair + dy + 2) * WIDTH],
                    preferred_element_type=F32,
                )
                for dy in range(3)
            )
            rows = [own_row(2 * pair), own_row(2 * pair + 1)]
            if up_out:
                both = jnp.concatenate([ls[row, :] for row in rows], axis=1)
                projected = jnp.dot(skip, both, preferred_element_type=F32)
            for half, row in enumerate(rows):
                cols = slice(half * WIDTH, (half + 1) * WIDTH)
                kept = (xs[row, :].astype(F32) + convolved[:, cols]).astype(BF)
                result[row, :] = kept
                if not last:
                    following = kept.astype(F32)
                    if up_out:
                        following = following + projected[:, cols]
                        sums[row, :] = following
                    totals[...] += following
                    squares[...] += following * following

        if not last:
            send_sums(info, totals[...], squares[...], result, near_out, cross_out, stats_out)


EXCHANGED = [
    jax.ShapeDtypeStruct((CH + STATS, WIDTH), BF),
    jax.ShapeDtypeStruct((CH + STATS, WIDTH), BF),
    jax.ShapeDtypeStruct((STATS, WIDTH), BF),
]
WHOLE = jax.ShapeDtypeStruct((OWN, WIDTH), BF)


def first_call(info, pieces):
    return pl.pallas_call(
        first_body,
        out_shape=EXCHANGED + [WHOLE],
        in_specs=[SM] + [ANY] * 4,
        out_specs=[VM] * 3 + [ANY],
        scratch_shapes=[pltpu.VMEM((OWN, WIDTH), BF), pltpu.SemaphoreType.DMA((4,))],
        compiler_params=pltpu.CompilerParams(vmem_limit_bytes=16 * MIB),
        name="first_sums",
    )(info, *pieces)


def block_call(block, at_core, info, source, exchanged, member, params, weights, skips, lateral_edges, lateral):
    up_in, up_out = lateral_edges is not None, lateral is not None
    last = block == BLOCKS - 1
    operands = [source, *exchanged, member, params, *weights]
    specs = [VM] * 6 + [ANY] * 3
    shapes, out_specs = [WHOLE] + EXCHANGED, [VM] * 4
    if last:
        shapes, out_specs = shapes[:1], out_specs[:1]
    scratch = [
        pltpu.VMEM((CH, TAPS), BF),
        pltpu.VMEM((16, CH), F32),
        pltpu.VMEM((CAT, (ROWS + 2) * WIDTH), BF),
        pltpu.VMEM((CH, WIDTH), F32),
        pltpu.VMEM((CH, WIDTH), F32),
        pltpu.SemaphoreType.DMA((3,)),
    ]
    if up_in or up_out:
        operands.append(skips)
        specs.append(ANY)
    if up_in:
        operands += list(lateral_edges)
        specs += [VM] * 2
        scratch.append(pltpu.VMEM((CH, CH), BF))
    if up_out:
        operands.append(lateral)
        specs.append(VM)
        shapes = shapes + [jax.ShapeDtypeStruct((OWN, WIDTH), F32)]
        out_specs = out_specs + [VM]
        scratch += [pltpu.VMEM((CH, CH), BF), pltpu.SemaphoreType.DMA((1,))]
    out = pl.pallas_call(
        functools.partial(block_body, block, at_core, up_in, up_out, last),
        out_shape=shapes,
        in_specs=[SM] + specs,
        out_specs=out_specs,
        scratch_shapes=scratch,
        compiler_params=pltpu.CompilerParams(vmem_limit_bytes=28 * MIB),
        cost_estimate=pl.CostEstimate(
            flops=2 * OWN * WIDTH * TAPS, bytes_accessed=4 * MIB, transcendentals=OWN * WIDTH
        ),
        name="res_block",
    )(info, *operands)
    return out[0], out[1:4], out[4] if up_out else None


def pick_body(info, *refs):
    wholes, out, held, in_sem, out_sem = refs[:BLOCKS], *refs[BLOCKS:]
    for at in range(8):

        @pl.when(info[0] == at)
        def _():
            copies = [
                (
                    pltpu.make_async_copy(wholes[at + 8 * n], held.at[n], in_sem.at[n]),
                    pltpu.make_async_copy(held.at[n], out.at[n], out_sem.at[n]),
                )
                for n in range(2)
            ]
            for arrive, _ in copies:
                arrive.start()
            for arrive, leave in copies:
                arrive.wait()
                leave.start()
            for _, leave in copies:
                leave.wait()


def pick(info, wholes):
    return pl.pallas_call(
        pick_body,
        out_shape=jax.ShapeDtypeStruct((2, OWN, WIDTH), BF),
        in_specs=[SM] + [ANY] * BLOCKS,
        out_specs=ANY,
        scratch_shapes=[
            pltpu.VMEM((2, OWN, WIDTH), BF),
            pltpu.SemaphoreType.DMA((2,)),
            pltpu.SemaphoreType.DMA((2,)),
        ],
        compiler_params=pltpu.CompilerParams(vmem_limit_bytes=16 * MIB),
        name="pick",
    )(info, *wholes)


def sinusoid(steps, half_width):
    rates = jnp.exp(-math.log(10000.0) * jnp.arange(half_width, dtype=F32) / half_width)
    angles = steps.astype(F32)[:, None] * rates[None, :]
    return jnp.concatenate([jnp.cos(angles), jnp.sin(angles)], axis=-1)


def on_device(
    features, timesteps, plan, conv_weight, skip_weight, time_weight, norm_gain, norm_bias
):
    segment, tile = lax.axis_index("segment"), lax.axis_index("tile")
    core, odd = segment % 2, tile % 2
    quarter = jnp.where(odd == 1, 1 + core, 3 * core)
    slot = 4 * (tile // 8) + (tile % 8) // 2
    active = (segment < 2).astype(jnp.int32)

    info = jnp.stack([quarter, slot, active]).astype(jnp.int32)

    served = lax.dynamic_index_in_dim(
        features, plan[jnp.minimum(segment, MICRO - 1)], 0, keepdims=False
    )
    served = served.transpose(0, 2, 1).reshape(PIECE, WIDTH)
    pieces = []
    for k in range(4):
        route = [
            (j * TILES + 4 * q + (k ^ j % 4), place(j, q)) for j in range(MICRO) for q in range(4)
        ]
        pieces.append(lax.ppermute(served, BOTH, route))

    encoded = sinusoid(timesteps[plan], time_weight.shape[1] // 2)
    shifts = jnp.dot(encoded, time_weight[0], precision=lax.Precision.HIGHEST)
    params = jnp.concatenate([norm_gain, norm_bias, jnp.zeros((6, CH), F32), shifts], axis=0)
    params = lax.all_gather(params, "segment")
    skips = lax.all_gather(skip_weight[0].T, "segment")
    lead = conv_weight[0].T
    first_up = BLOCKS - DOWN

    def fetch(index, after):
        own, _ = lax.optimization_barrier((lead, after))
        first, second = PAIRS[index]
        return lax.ppermute(own, "segment", [(first, 0), (second, 1)])

    def exchange(near, cross, stats):
        other_tile = [(t, t ^ 1) for t in range(TILES)]
        other_core = [(b, b ^ 1) for b in range(BLOCKS)]
        both = [
            (b * TILES + t, (b ^ 1) * TILES + (t ^ 1)) for b in range(BLOCKS) for t in range(TILES)
        ]
        return (
            lax.ppermute(near, "tile", other_tile),
            lax.ppermute(cross, "segment", other_core),
            lax.ppermute(stats, BOTH, both),
        )

    def hand_over(block, whole):
        route = [(place(j, q), helper(block, j, q)) for j in range(MICRO) for q in range(4)]
        return lax.ppermute(whole, BOTH, route)

    member_at = jnp.arange(CH) // GROUP
    member = (member_at[:, None] == member_at[None, :]).astype(BF)
    weights, cores, fetched = {}, {}, {}

    def swap_cores(index, own):
        both = own, lax.ppermute(own, "segment", [(b, b ^ 1) for b in range(BLOCKS)])
        for at, block in enumerate(PAIRS[index]):
            weights[block], cores[block] = both, at

    swap_cores(0, lead)
    *exchanged, source = first_call(info, pieces)
    fetched[1] = fetch(1, pieces)
    fetched[2] = fetch(2, source)
    wholes, edges_of, passing = [], {}, []
    for block in range(BLOCKS):
        up_in, up_out = block >= first_up, first_up - 1 <= block < BLOCKS - 1
        near, cross, stats = exchanged
        near_in, cross_in, far = exchange(near, cross, stats)
        edges_of[block] = (near_in, cross_in)
        if block >= 1:
            sent, _ = lax.optimization_barrier((wholes[-1], (near_in, cross_in, far)))
            passing.append(hand_over(block - 1, sent))
        if block >= 3:
            source, near_in, cross_in, far, passing[block - 3] = lax.optimization_barrier(
                (source, near_in, cross_in, far, passing[block - 3])
            )
        for after, moving in MOVE_AFTER.items():
            if block == after + 3:
                source, passing[moving] = lax.optimization_barrier((source, passing[moving]))
        whole, exchanged, summed = block_call(
            block,
            cores[block],
            info,
            source,
            (near_in, cross_in, stats, far),
            member,
            params,
            weights[block],
            skips,
            edges_of[BLOCKS - block] if up_in else None,
            wholes[BLOCKS - 2 - block] if up_out else None,
        )
        wholes.append(whole)
        source = summed if up_out else whole
        if block in MOVE_AFTER:
            moving = MOVE_AFTER[block]
            column = helper(moving, 0, 0) // TILES
            moved, _ = lax.optimization_barrier((passing[moving], whole))
            passing[moving] = lax.ppermute(
                moved, "segment", [(column + far, moving % 8 + far) for far in (0, 8)]
            )
        if block in SWAP_AFTER:
            index = SWAP_AFTER[block]
            own, _ = lax.optimization_barrier((fetched[index], whole))
            swap_cores(index, own)
        if block in FETCH_AFTER:
            index = FETCH_AFTER[block]
            fetched[index] = fetch(index, whole)
    passing.append(hand_over(BLOCKS - 1, wholes[-1]))
    held = pick((segment % 8).astype(jnp.int32)[None], passing)
    peers = [
        [(s + 8 * far) * TILES + 4 * q + i for far in range(2) for i in range(4)]
        for s in range(8)
        for q in range(4)
    ]
    out = lax.all_to_all(
        held.reshape(MICRO, PIECE, WIDTH), BOTH, 0, 0, axis_index_groups=peers, tiled=True
    )
    out = out.reshape(1, MICRO, 3, CH, WIDTH)
    return out.transpose(0, 1, 2, 4, 3)


def solution(mesh):
    placed = (
        P(None, "tile", None, None),
        P(),
        P(),
        P("segment", None, None),
        P("segment", None, None),
        P("segment", None, None),
        P("segment", None),
        P("segment", None),
    )
    return jax.shard_map(
        on_device,
        mesh=mesh,
        in_specs=placed,
        out_specs=P("segment", None, "tile", None, None),
        check_vma=False,
    )
```

```python
import functools
import math

import jax
import jax.numpy as jnp
from jax import lax
from jax.experimental import pallas as pl
from jax.experimental.pallas import tpu as pltpu
from jax.sharding import PartitionSpec as P

BLOCKS, MICRO, TILES, DOWN = 16, 8, 16, 4
WIDTH, CH, GROUP = 128, 320, 10
CAT = 3 * CH
TAPS = 9 * CH
ROWS = 12
PIECE = 3 * CH
OWN = ROWS * CH
MEMBERS = float(48 * WIDTH * GROUP)
MIB = 1024 * 1024
STATS = 48
BF, F32 = jnp.bfloat16, jnp.float32
ANY = pl.BlockSpec(memory_space=pl.ANY)
VM = pl.BlockSpec(memory_space=pltpu.VMEM)
SM = pl.BlockSpec(memory_space=pltpu.SMEM)
BOTH = ("segment", "tile")

PAIRS = ((0, 1), (2, 6), (3, 7), (4, 8), (5, 9), (10, 14), (11, 15), (12, 13))
FETCH_AFTER = {0: 3, 2: 4, 4: 5, 6: 6, 8: 7}
SWAP_AFTER = {0: 1, 1: 2, 2: 3, 3: 4, 6: 5, 8: 6, 10: 7}


def place(slot, quarter):
    tile = (slot // 4) * 8 + 2 * (slot % 4) + (quarter in (1, 2))
    return (quarter // 2) * TILES + tile


def helper(block, slot, quarter):
    segment = block % 8 + slot // 4 * 8
    return segment * TILES + quarter // 2 * 8 + place(slot, quarter) % 8


def chunk_at(turn, k):
    chunk = k ^ lax.rem(turn, 4)
    return pl.multiple_of(chunk * PIECE, PIECE)


def send_sums(info, totals, squares, source, near, cross, stats):
    ones = jnp.ones((8, WIDTH), F32)
    rows = jnp.concatenate(
        [
            lax.dot_general(
                ones,
                part,
                (((1,), (1,)), ((), ())),
                precision=lax.Precision.HIGHEST,
                preferred_element_type=F32,
            )[0:1]
            for part in (totals, squares)
        ],
        axis=0,
    )
    high = rows.astype(BF).astype(F32)
    left = rows - high
    middle = left.astype(BF).astype(F32)
    low = left - middle
    coded = jnp.concatenate([high, middle, low, jnp.zeros((10, CH), F32)], axis=0)
    coded = jnp.concatenate([coded, jnp.zeros((16, 64), F32)], axis=1).astype(BF)
    even = lax.rem(info[0], 2) == 0
    first, last = source[0:CH, :], source[OWN - CH : OWN, :]
    near[0:CH, :] = jnp.where(even, last, first)
    cross[0:CH, :] = jnp.where(even, first, last)
    for i in range(3):
        part = coded[:, i * 128 : (i + 1) * 128]
        near[CH + 16 * i : CH + 16 * (i + 1), :] = part
        cross[CH + 16 * i : CH + 16 * (i + 1), :] = part
        stats[16 * i : 16 * (i + 1), :] = part


def first_body(info, *refs):
    pieces, (near, cross, stats, whole), (xs, sem) = refs[:4], refs[4:8], refs[8:]

    @pl.when(info[2] == 1)
    def _():
        copies = [
            pltpu.make_async_copy(pieces[k], xs.at[pl.ds(chunk_at(info[1], k), PIECE)], sem.at[k])
            for k in range(4)
        ]
        for copy in copies:
            copy.start()
        for copy in copies:
            copy.wait()
        final = pltpu.make_async_copy(xs, whole, sem.at[0])
        final.start()
        totals = squares = jnp.zeros((CH, WIDTH), F32)
        for r in range(ROWS):
            row = xs[r * CH : (r + 1) * CH, :].astype(F32)
            totals, squares = totals + row, squares + row * row
        send_sums(info, totals, squares, xs, near, cross, stats)
        final.wait()


def block_body(block, at_core, up_in, up_out, last, info, *refs):
    refs = list(refs)

    def take(n):
        got = refs[:n]
        del refs[:n]
        return got

    source, near, cross, own_stats, far_stats, member, params_all = take(7)
    weights = take(2)
    if up_in or up_out:
        (skips,) = take(1)
    if up_in:
        lateral_edges = take(2)
    if up_out:
        (lateral,) = take(1)
    (result,) = take(1)
    if not last:
        near_out, cross_out, stats_out = take(3)
    if up_out:
        (summed_out,) = take(1)
    xs = source
    ws, ps, cat, totals, squares, w_sem = take(6)
    if up_in:
        (sk_in,) = take(1)
    if up_out:
        ls, sums = lateral, summed_out
        sk, l_sem = take(2)

    @pl.when(info[2] == 1)
    def _():
        core = info[0] // 2
        params_copy = pltpu.make_async_copy(params_all.at[block], ps, w_sem.at[2])
        params_copy.start()
        for at in range(2):

            @pl.when((core == at_core) == (at == 0))
            def _():
                pltpu.make_async_copy(weights[at], ws, w_sem.at[0]).start()

        if up_in:
            in_copy = pltpu.make_async_copy(skips.at[block], sk_in, w_sem.at[1])
            in_copy.start()
        if up_out:
            out_copy = pltpu.make_async_copy(skips.at[block + 1], sk, l_sem.at[0])
            out_copy.start()

        coded = [jnp.concatenate([ref[a + 16 * i : a + 16 * i + 16, :] for i in range(3)], axis=1)
                 for ref, a in ((own_stats, 0), (far_stats, 0), (near, CH), (cross, CH))]
        coded = jnp.concatenate(coded, axis=0)[:, 0:CH]
        groups = lax.dot_general(
            member[...], coded, (((1,), (1,)), ((), ())), preferred_element_type=F32
        )
        kind = lax.rem(lax.broadcasted_iota(jnp.int32, (CH, 64), 1), 16)
        even_kind = lax.rem(kind, 2) == 0
        mean = jnp.sum(jnp.where(even_kind, groups, 0.0), axis=1, keepdims=True) / MEMBERS
        mean_sq = jnp.sum(jnp.where(even_kind, 0.0, groups), axis=1, keepdims=True) / MEMBERS
        variance = jnp.maximum(mean_sq - mean * mean, 0.0)
        params_copy.wait()
        params = jnp.transpose(ps[...])
        lane = lax.broadcasted_iota(jnp.int32, (CH, 16), 1)
        shift = jnp.sum(jnp.where(lane == info[1] + 8, params, 0.0), axis=1, keepdims=True)
        wide = (CH, WIDTH)
        gain = jnp.broadcast_to(params[:, 0:1] * lax.rsqrt(variance + 1e-5) * 0.5, wide)
        bias = jnp.broadcast_to(params[:, 1:2] * 0.5, wide)
        mean = jnp.broadcast_to(mean, wide)
        shift = jnp.broadcast_to(shift, wide)
        column = lax.broadcasted_iota(jnp.int32, wide, 1)

        def lift(x, row, keep=None):
            h = (x - mean) * gain + bias
            lifted = h * jnp.tanh(h) + h + shift
            if keep is not None:
                lifted = jnp.where(keep, lifted, 0.0)
            left = jnp.where(column == 0, 0.0, pltpu.roll(lifted, 1, 1)).astype(BF)
            right = jnp.where(column == WIDTH - 1, 0.0, pltpu.roll(lifted, WIDTH - 1, 1)).astype(BF)
            cols = pl.ds(row * WIDTH, WIDTH)
            if not isinstance(row, int):
                cols = pl.ds(pl.multiple_of(row * WIDTH, WIDTH), WIDTH)
            cat[0:CH, cols] = left
            cat[CH : 2 * CH, cols] = lifted.astype(BF)
            cat[2 * CH : 3 * CH, cols] = right

        even = lax.rem(info[0], 2) == 0
        near_rows, cross_rows = near[0:CH, :].astype(F32), cross[0:CH, :].astype(F32)
        if up_in:
            in_copy.wait()
            skip_in = sk_in[...]
            near_rows, cross_rows = (
                rows + jnp.dot(skip_in, edge[0:CH, :], preferred_element_type=F32)
                for rows, edge in zip((near_rows, cross_rows), lateral_edges)
            )
        def own_row(r):
            return slice(r * CH, (r + 1) * CH)

        if up_out:
            out_copy.wait()
            skip = sk[...]
        totals[...] = jnp.zeros(wide, F32)
        squares[...] = jnp.zeros(wide, F32)

        def lift_at(row):
            if row == 0:
                lift(jnp.where(even, cross_rows, near_rows), 0, info[0] > 0)
            elif row == ROWS + 1:
                lift(jnp.where(even, near_rows, cross_rows), row, info[0] < 3)
            else:
                lift(xs[(row - 1) * CH : row * CH, :].astype(F32), row)

        for row in range(2):
            lift_at(row)
        lift_at(2)
        lift_at(3)
        pltpu.make_async_copy(weights[0], ws, w_sem.at[0]).wait()
        for pair in range(ROWS // 2):
            if pair:
                lift_at(2 * pair + 2)
                lift_at(2 * pair + 3)
            convolved = sum(
                jnp.dot(
                    ws[:, dy * CAT : (dy + 1) * CAT],
                    cat[:, (2 * pair + dy) * WIDTH : (2 * pair + dy + 2) * WIDTH],
                    preferred_element_type=F32,
                )
                for dy in range(3)
            )
            rows = [own_row(2 * pair), own_row(2 * pair + 1)]
            if up_out:
                both = jnp.concatenate([ls[row, :] for row in rows], axis=1)
                projected = jnp.dot(skip, both, preferred_element_type=F32)
            for half, row in enumerate(rows):
                cols = slice(half * WIDTH, (half + 1) * WIDTH)
                kept = (xs[row, :].astype(F32) + convolved[:, cols]).astype(BF)
                result[row, :] = kept
                if not last:
                    following = kept.astype(F32)
                    if up_out:
                        following = following + projected[:, cols]
                        sums[row, :] = following
                    totals[...] += following
                    squares[...] += following * following

        if not last:
            send_sums(info, totals[...], squares[...], result, near_out, cross_out, stats_out)


EXCHANGED = [
    jax.ShapeDtypeStruct((CH + STATS, WIDTH), BF),
    jax.ShapeDtypeStruct((CH + STATS, WIDTH), BF),
    jax.ShapeDtypeStruct((STATS, WIDTH), BF),
]
WHOLE = jax.ShapeDtypeStruct((OWN, WIDTH), BF)


def first_call(info, pieces):
    return pl.pallas_call(
        first_body,
        out_shape=EXCHANGED + [WHOLE],
        in_specs=[SM] + [ANY] * 4,
        out_specs=[VM] * 3 + [ANY],
        scratch_shapes=[pltpu.VMEM((OWN, WIDTH), BF), pltpu.SemaphoreType.DMA((4,))],
        compiler_params=pltpu.CompilerParams(vmem_limit_bytes=16 * MIB),
        name="first_sums",
    )(info, *pieces)


def block_call(block, at_core, info, source, exchanged, member, params, weights, skips, lateral_edges, lateral):
    up_in, up_out = lateral_edges is not None, lateral is not None
    last = block == BLOCKS - 1
    operands = [source, *exchanged, member, params, *weights]
    specs = [VM] * 6 + [ANY] * 3
    shapes, out_specs = [WHOLE] + EXCHANGED, [VM] * 4
    if last:
        shapes, out_specs = shapes[:1], out_specs[:1]
    scratch = [
        pltpu.VMEM((CH, TAPS), BF),
        pltpu.VMEM((16, CH), F32),
        pltpu.VMEM((CAT, (ROWS + 2) * WIDTH), BF),
        pltpu.VMEM((CH, WIDTH), F32),
        pltpu.VMEM((CH, WIDTH), F32),
        pltpu.SemaphoreType.DMA((3,)),
    ]
    if up_in or up_out:
        operands.append(skips)
        specs.append(ANY)
    if up_in:
        operands += list(lateral_edges)
        specs += [VM] * 2
        scratch.append(pltpu.VMEM((CH, CH), BF))
    if up_out:
        operands.append(lateral)
        specs.append(VM)
        shapes = shapes + [jax.ShapeDtypeStruct((OWN, WIDTH), F32)]
        out_specs = out_specs + [VM]
        scratch += [pltpu.VMEM((CH, CH), BF), pltpu.SemaphoreType.DMA((1,))]
    out = pl.pallas_call(
        functools.partial(block_body, block, at_core, up_in, up_out, last),
        out_shape=shapes,
        in_specs=[SM] + specs,
        out_specs=out_specs,
        scratch_shapes=scratch,
        compiler_params=pltpu.CompilerParams(vmem_limit_bytes=28 * MIB),
        cost_estimate=pl.CostEstimate(
            flops=2 * OWN * WIDTH * TAPS, bytes_accessed=4 * MIB, transcendentals=OWN * WIDTH
        ),
        name="res_block",
    )(info, *operands)
    return out[0], out[1:4], out[4] if up_out else None


def pick_body(info, *refs):
    wholes, out, held, in_sem, out_sem = refs[:BLOCKS], *refs[BLOCKS:]
    for at in range(8):

        @pl.when(info[0] == at)
        def _():
            arrivals = [
                pltpu.make_async_copy(wholes[at + 8 * n], held.at[n], in_sem.at[n])
                for n in range(2)
            ]
            leaves = [
                pltpu.make_async_copy(held.at[n // 2], out.at[n], out_sem.at[n]) for n in range(4)
            ]
            for arrive in arrivals:
                arrive.start()
            for n, leave in enumerate(leaves):
                if n % 2 == 0:
                    arrivals[n // 2].wait()
                leave.start()
            for leave in leaves:
                leave.wait()


def pick(info, wholes):
    return pl.pallas_call(
        pick_body,
        out_shape=jax.ShapeDtypeStruct((4, OWN, WIDTH), BF),
        in_specs=[SM] + [ANY] * BLOCKS,
        out_specs=ANY,
        scratch_shapes=[
            pltpu.VMEM((2, OWN, WIDTH), BF),
            pltpu.SemaphoreType.DMA((2,)),
            pltpu.SemaphoreType.DMA((4,)),
        ],
        compiler_params=pltpu.CompilerParams(vmem_limit_bytes=16 * MIB),
        name="pick",
    )(info, *wholes)


def sinusoid(steps, half_width):
    rates = jnp.exp(-math.log(10000.0) * jnp.arange(half_width, dtype=F32) / half_width)
    angles = steps.astype(F32)[:, None] * rates[None, :]
    return jnp.concatenate([jnp.cos(angles), jnp.sin(angles)], axis=-1)


def on_device(
    features, timesteps, plan, conv_weight, skip_weight, time_weight, norm_gain, norm_bias
):
    segment, tile = lax.axis_index("segment"), lax.axis_index("tile")
    core, odd = segment % 2, tile % 2
    quarter = jnp.where(odd == 1, 1 + core, 3 * core)
    slot = 4 * (tile // 8) + (tile % 8) // 2
    active = (segment < 2).astype(jnp.int32)

    info = jnp.stack([quarter, slot, active]).astype(jnp.int32)

    served = lax.dynamic_index_in_dim(
        features, plan[jnp.minimum(segment, MICRO - 1)], 0, keepdims=False
    )
    served = served.transpose(0, 2, 1).reshape(PIECE, WIDTH)
    pieces = []
    for k in range(4):
        route = [
            (j * TILES + 4 * q + (k ^ j % 4), place(j, q)) for j in range(MICRO) for q in range(4)
        ]
        pieces.append(lax.ppermute(served, BOTH, route))

    encoded = sinusoid(timesteps[plan], time_weight.shape[1] // 2)
    shifts = jnp.dot(encoded, time_weight[0], precision=lax.Precision.HIGHEST)
    params = jnp.concatenate([norm_gain, norm_bias, jnp.zeros((6, CH), F32), shifts], axis=0)
    params = lax.all_gather(params, "segment")
    skips = lax.all_gather(skip_weight[0].T, "segment")
    lead = conv_weight[0].T
    first_up = BLOCKS - DOWN

    def fetch(index, after):
        own, _ = lax.optimization_barrier((lead, after))
        first, second = PAIRS[index]
        return lax.ppermute(own, "segment", [(first, 0), (second, 1)])

    def exchange(near, cross, stats):
        other_tile = [(t, t ^ 1) for t in range(TILES)]
        other_core = [(b, b ^ 1) for b in range(BLOCKS)]
        both = [
            (b * TILES + t, (b ^ 1) * TILES + (t ^ 1)) for b in range(BLOCKS) for t in range(TILES)
        ]
        return (
            lax.ppermute(near, "tile", other_tile),
            lax.ppermute(cross, "segment", other_core),
            lax.ppermute(stats, BOTH, both),
        )

    def hand_over(block, whole):
        route = [(place(j, q), helper(block, j, q)) for j in range(MICRO) for q in range(4)]
        return lax.ppermute(whole, BOTH, route)

    member_at = jnp.arange(CH) // GROUP
    member = (member_at[:, None] == member_at[None, :]).astype(BF)
    weights, cores, fetched = {}, {}, {}

    def swap_cores(index, own):
        both = own, lax.ppermute(own, "segment", [(b, b ^ 1) for b in range(BLOCKS)])
        for at, block in enumerate(PAIRS[index]):
            weights[block], cores[block] = both, at

    swap_cores(0, lead)
    pieces, params = lax.optimization_barrier((pieces, params))
    *exchanged, source = first_call(info, pieces)
    fetched[1] = fetch(1, pieces)
    fetched[2] = fetch(2, source)
    wholes, edges_of, passing = [], {}, []
    for block in range(BLOCKS):
        up_in, up_out = block >= first_up, first_up - 1 <= block < BLOCKS - 1
        near, cross, stats = exchanged
        near_in, cross_in, far = exchange(near, cross, stats)
        edges_of[block] = (near_in, cross_in)
        if block >= 1:
            sent, _ = lax.optimization_barrier((wholes[-1], (near_in, cross_in, far)))
            passing.append(hand_over(block - 1, sent))
        if block >= 3:
            source, near_in, cross_in, far, passing[block - 3] = lax.optimization_barrier(
                (source, near_in, cross_in, far, passing[block - 3])
            )
        whole, exchanged, summed = block_call(
            block,
            cores[block],
            info,
            source,
            (near_in, cross_in, stats, far),
            member,
            params,
            weights[block],
            skips,
            edges_of[BLOCKS - block] if up_in else None,
            wholes[BLOCKS - 2 - block] if up_out else None,
        )
        wholes.append(whole)
        source = summed if up_out else whole
        if block in SWAP_AFTER:
            index = SWAP_AFTER[block]
            own, _ = lax.optimization_barrier((fetched[index], whole))
            swap_cores(index, own)
        if block in FETCH_AFTER:
            index = FETCH_AFTER[block]
            fetched[index] = fetch(index, whole)
    passing.append(hand_over(BLOCKS - 1, wholes[-1]))
    held = pick((segment % 8).astype(jnp.int32)[None], passing)
    peers = [
        [(s + 8 * far) * TILES + 8 * side + z for far in range(2) for z in range(8)]
        for s in range(8)
        for side in range(2)
    ]
    got = lax.all_to_all(
        held.reshape(2 * MICRO, PIECE, WIDTH), BOTH, 0, 0, axis_index_groups=peers, tiled=True
    )
    parity = (tile % 8) // 4 ^ tile // 8
    out = lax.dynamic_index_in_dim(
        got.reshape(MICRO, 2, PIECE, WIDTH), parity, 1, keepdims=False
    )
    out = out.reshape(1, MICRO, 3, CH, WIDTH)
    return out.transpose(0, 1, 2, 4, 3)


def solution(mesh):
    placed = (
        P(None, "tile", None, None),
        P(),
        P(),
        P("segment", None, None),
        P("segment", None, None),
        P("segment", None, None),
        P("segment", None),
        P("segment", None),
    )
    return jax.shard_map(
        on_device,
        mesh=mesh,
        in_specs=placed,
        out_specs=P("segment", None, "tile", None, None),
        check_vma=False,
    )
```

```python
import functools
import math

import jax
import jax.numpy as jnp
from jax import lax
from jax.experimental import pallas as pl
from jax.experimental.pallas import tpu as pltpu
from jax.sharding import PartitionSpec as P

BLOCKS, MICRO, TILES, DOWN = 16, 8, 16, 4
WIDTH, CH, GROUP = 128, 320, 10
CAT = 3 * CH
TAPS = 9 * CH
ROWS = 12
PIECE = 3 * CH
OWN = ROWS * CH
MEMBERS = float(48 * WIDTH * GROUP)
MIB = 1024 * 1024
LEAD = 2944
HALF = 1536
STATS = 48
BF, F32 = jnp.bfloat16, jnp.float32
ANY = pl.BlockSpec(memory_space=pl.ANY)
VM = pl.BlockSpec(memory_space=pltpu.VMEM)
SM = pl.BlockSpec(memory_space=pltpu.SMEM)
BOTH = ("segment", "tile")

PAIRS = ((0, 1), (2, 6), (3, 7), (4, 8), (5, 9), (10, 14), (11, 12), (13, 15))
FETCH_AFTER = {(2, 0): 0, (2, 1): 1, (3, 0): 1, (3, 1): 2, (4, 0): 2, (4, 1): 3}
FETCH_AFTER |= {(5, 0): 5, (5, 1): 6, (6, 0): 7, (6, 1): 8, (7, 0): 9, (7, 1): 10}
SWAP_AFTER = {(1, 0): 0, (1, 1): 1, (2, 0): 1, (2, 1): 2, (3, 0): 2, (3, 1): 3, (4, 0): 3, (4, 1): 4}
SWAP_AFTER |= {(5, 0): 6, (5, 1): 7, (6, 0): 8, (6, 1): 9, (7, 0): 10, (7, 1): 11}


def place(slot, quarter):
    tile = (slot // 4) * 8 + 2 * (slot % 4) + (quarter in (1, 2))
    return (quarter // 2) * TILES + tile


def helper(block, slot, quarter):
    segment = block % 8 + slot // 4 * 8
    return segment * TILES + quarter // 2 * 8 + place(slot, quarter) % 8


def chunk_at(turn, k):
    chunk = k ^ lax.rem(turn, 4)
    return pl.multiple_of(chunk * PIECE, PIECE)


def send_sums(info, totals, squares, source, near, cross, stats):
    ones = jnp.ones((8, WIDTH), F32)
    rows = jnp.concatenate(
        [
            lax.dot_general(
                ones,
                part,
                (((1,), (1,)), ((), ())),
                precision=lax.Precision.HIGHEST,
                preferred_element_type=F32,
            )[0:1]
            for part in (totals, squares)
        ],
        axis=0,
    )
    high = rows.astype(BF).astype(F32)
    left = rows - high
    middle = left.astype(BF).astype(F32)
    low = left - middle
    coded = jnp.concatenate([high, middle, low, jnp.zeros((10, CH), F32)], axis=0)
    coded = jnp.concatenate([coded, jnp.zeros((16, 64), F32)], axis=1).astype(BF)
    even = lax.rem(info[0], 2) == 0
    first, last = source[0:CH, :], source[OWN - CH : OWN, :]
    near[0:CH, :] = jnp.where(even, last, first)
    cross[0:CH, :] = jnp.where(even, first, last)
    for i in range(3):
        part = coded[:, i * 128 : (i + 1) * 128]
        near[CH + 16 * i : CH + 16 * (i + 1), :] = part
        cross[CH + 16 * i : CH + 16 * (i + 1), :] = part
        stats[16 * i : 16 * (i + 1), :] = part


def first_body(info, *refs):
    pieces, (near, cross, stats, whole), (xs, sem) = refs[:4], refs[4:8], refs[8:]

    @pl.when(info[2] == 1)
    def _():
        copies = [
            pltpu.make_async_copy(pieces[k], xs.at[pl.ds(chunk_at(info[1], k), PIECE)], sem.at[k])
            for k in range(4)
        ]
        for copy in copies:
            copy.start()
        for copy in copies:
            copy.wait()
        final = pltpu.make_async_copy(xs, whole, sem.at[0])
        final.start()
        totals = squares = jnp.zeros((CH, WIDTH), F32)
        for r in range(ROWS):
            row = xs[r * CH : (r + 1) * CH, :].astype(F32)
            totals, squares = totals + row, squares + row * row
        send_sums(info, totals, squares, xs, near, cross, stats)
        final.wait()


def block_body(block, at_core, up_in, up_out, last, info, *refs):
    refs = list(refs)

    def take(n):
        got = refs[:n]
        del refs[:n]
        return got

    source, near, cross, own_stats, far_stats, member = take(6)
    weights = take(4)
    if up_in or up_out:
        (skips,) = take(1)
    if up_in:
        lateral_edges = take(2)
    if up_out:
        (lateral,) = take(1)
    (result,) = take(1)
    if not last:
        near_out, cross_out, stats_out = take(3)
    if up_out:
        (summed_out,) = take(1)
    xs = source
    ws, ps, cat, totals, squares, w_sem = take(6)
    if up_in:
        (sk_in,) = take(1)
    if up_out:
        ls, sums = lateral, summed_out
        sk, l_sem = take(2)

    @pl.when(info[2] == 1)
    def _():
        core = info[0] // 2
        head = pl.ds(LEAD - HALF - WIDTH, WIDTH)
        halves = (pl.ds(0, HALF), pl.ds(HALF, LEAD - HALF))
        for at in range(2):

            @pl.when((core == at_core) == (at == 0))
            def _():
                pltpu.make_async_copy(weights[2 + at].at[:, head], ps, w_sem.at[2]).start()
                for n, part in enumerate(halves):
                    pltpu.make_async_copy(
                        weights[2 * n + at], ws.at[:, part], w_sem.at[3 * n]
                    ).start()

        if up_in:
            in_copy = pltpu.make_async_copy(skips.at[block], sk_in, w_sem.at[1])
            in_copy.start()
        if up_out:
            out_copy = pltpu.make_async_copy(skips.at[block + 1], sk, l_sem.at[0])
            out_copy.start()

        coded = [jnp.concatenate([ref[a + 16 * i : a + 16 * i + 16, :] for i in range(3)], axis=1)
                 for ref, a in ((own_stats, 0), (far_stats, 0), (near, CH), (cross, CH))]
        coded = jnp.concatenate(coded, axis=0)[:, 0:CH]
        groups = lax.dot_general(
            member[...], coded, (((1,), (1,)), ((), ())), preferred_element_type=F32
        )
        kind = lax.rem(lax.broadcasted_iota(jnp.int32, (CH, 64), 1), 16)
        even_kind = lax.rem(kind, 2) == 0
        mean = jnp.sum(jnp.where(even_kind, groups, 0.0), axis=1, keepdims=True) / MEMBERS
        mean_sq = jnp.sum(jnp.where(even_kind, 0.0, groups), axis=1, keepdims=True) / MEMBERS
        variance = jnp.maximum(mean_sq - mean * mean, 0.0)
        pltpu.make_async_copy(weights[2].at[:, head], ps, w_sem.at[2]).wait()
        tailing = ps[:, 64:128].astype(F32)
        params = tailing[:, 0:16] + tailing[:, 16:32] + tailing[:, 32:48]
        lane = lax.broadcasted_iota(jnp.int32, (CH, 16), 1)
        shift = jnp.sum(jnp.where(lane == info[1] + 8, params, 0.0), axis=1, keepdims=True)
        wide = (CH, WIDTH)
        gain = jnp.broadcast_to(params[:, 0:1] * lax.rsqrt(variance + 1e-5) * 0.5, wide)
        bias = jnp.broadcast_to(params[:, 1:2] * 0.5, wide)
        mean = jnp.broadcast_to(mean, wide)
        shift = jnp.broadcast_to(shift, wide)
        column = lax.broadcasted_iota(jnp.int32, wide, 1)

        def lift(x, row, keep=None):
            h = (x - mean) * gain + bias
            lifted = h * jnp.tanh(h) + h + shift
            if keep is not None:
                lifted = jnp.where(keep, lifted, 0.0)
            left = jnp.where(column == 0, 0.0, pltpu.roll(lifted, 1, 1)).astype(BF)
            right = jnp.where(column == WIDTH - 1, 0.0, pltpu.roll(lifted, WIDTH - 1, 1)).astype(BF)
            cols = pl.ds(row * WIDTH, WIDTH)
            if not isinstance(row, int):
                cols = pl.ds(pl.multiple_of(row * WIDTH, WIDTH), WIDTH)
            cat[0:CH, cols] = left
            cat[CH : 2 * CH, cols] = lifted.astype(BF)
            cat[2 * CH : 3 * CH, cols] = right

        even = lax.rem(info[0], 2) == 0
        near_rows, cross_rows = near[0:CH, :].astype(F32), cross[0:CH, :].astype(F32)
        if up_in:
            in_copy.wait()
            skip_in = sk_in[...]
            near_rows, cross_rows = (
                rows + jnp.dot(skip_in, edge[0:CH, :], preferred_element_type=F32)
                for rows, edge in zip((near_rows, cross_rows), lateral_edges)
            )
        def own_row(r):
            return slice(r * CH, (r + 1) * CH)

        if up_out:
            out_copy.wait()
            skip = sk[...]
        totals[...] = jnp.zeros(wide, F32)
        squares[...] = jnp.zeros(wide, F32)

        def lift_at(row):
            if row == 0:
                lift(jnp.where(even, cross_rows, near_rows), 0, info[0] > 0)
            elif row == ROWS + 1:
                lift(jnp.where(even, near_rows, cross_rows), row, info[0] < 3)
            else:
                lift(xs[(row - 1) * CH : row * CH, :].astype(F32), row)

        for row in range(2):
            lift_at(row)
        lift_at(2)
        lift_at(3)
        for n, part in enumerate(halves):
            pltpu.make_async_copy(weights[2 * n], ws.at[:, part], w_sem.at[3 * n]).wait()
        for pair in range(ROWS // 2):
            if pair:
                lift_at(2 * pair + 2)
                lift_at(2 * pair + 3)
            convolved = sum(
                jnp.dot(
                    ws[:, dy * CAT : (dy + 1) * CAT],
                    cat[:, (2 * pair + dy) * WIDTH : (2 * pair + dy + 2) * WIDTH],
                    preferred_element_type=F32,
                )
                for dy in range(3)
            )
            rows = [own_row(2 * pair), own_row(2 * pair + 1)]
            if up_out:
                both = jnp.concatenate([ls[row, :] for row in rows], axis=1)
                projected = jnp.dot(skip, both, preferred_element_type=F32)
            for half, row in enumerate(rows):
                cols = slice(half * WIDTH, (half + 1) * WIDTH)
                kept = (xs[row, :].astype(F32) + convolved[:, cols]).astype(BF)
                result[row, :] = kept
                if not last:
                    following = kept.astype(F32)
                    if up_out:
                        following = following + projected[:, cols]
                        sums[row, :] = following
                    totals[...] += following
                    squares[...] += following * following

        if not last:
            send_sums(info, totals[...], squares[...], result, near_out, cross_out, stats_out)


EXCHANGED = [
    jax.ShapeDtypeStruct((CH + STATS, WIDTH), BF),
    jax.ShapeDtypeStruct((CH + STATS, WIDTH), BF),
    jax.ShapeDtypeStruct((STATS, WIDTH), BF),
]
WHOLE = jax.ShapeDtypeStruct((OWN, WIDTH), BF)


def first_call(info, pieces):
    return pl.pallas_call(
        first_body,
        out_shape=EXCHANGED + [WHOLE],
        in_specs=[SM] + [ANY] * 4,
        out_specs=[VM] * 3 + [ANY],
        scratch_shapes=[pltpu.VMEM((OWN, WIDTH), BF), pltpu.SemaphoreType.DMA((4,))],
        compiler_params=pltpu.CompilerParams(vmem_limit_bytes=16 * MIB),
        name="first_sums",
    )(info, *pieces)


def block_call(block, at_core, info, source, exchanged, member, weights, skips, lateral_edges, lateral):
    up_in, up_out = lateral_edges is not None, lateral is not None
    last = block == BLOCKS - 1
    operands = [source, *exchanged, member, *weights]
    specs = [VM] * 6 + [ANY] * 4
    shapes, out_specs = [WHOLE] + EXCHANGED, [VM] * 4
    if last:
        shapes, out_specs = shapes[:1], out_specs[:1]
    scratch = [
        pltpu.VMEM((CH, LEAD), BF),
        pltpu.VMEM((CH, WIDTH), BF),
        pltpu.VMEM((CAT, (ROWS + 2) * WIDTH), BF),
        pltpu.VMEM((CH, WIDTH), F32),
        pltpu.VMEM((CH, WIDTH), F32),
        pltpu.SemaphoreType.DMA((4,)),
    ]
    if up_in or up_out:
        operands.append(skips)
        specs.append(ANY)
    if up_in:
        operands += list(lateral_edges)
        specs += [VM] * 2
        scratch.append(pltpu.VMEM((CH, CH), BF))
    if up_out:
        operands.append(lateral)
        specs.append(VM)
        shapes = shapes + [jax.ShapeDtypeStruct((OWN, WIDTH), F32)]
        out_specs = out_specs + [VM]
        scratch += [pltpu.VMEM((CH, CH), BF), pltpu.SemaphoreType.DMA((1,))]
    out = pl.pallas_call(
        functools.partial(block_body, block, at_core, up_in, up_out, last),
        out_shape=shapes,
        in_specs=[SM] + specs,
        out_specs=out_specs,
        scratch_shapes=scratch,
        compiler_params=pltpu.CompilerParams(vmem_limit_bytes=28 * MIB),
        cost_estimate=pl.CostEstimate(
            flops=OWN * WIDTH * TAPS // 4, bytes_accessed=MIB, transcendentals=0
        ),
        name="res_block",
    )(info, *operands)
    return out[0], out[1:4], out[4] if up_out else None


def pick_body(info, *refs):
    wholes, out, held, in_sem, out_sem = refs[:BLOCKS], *refs[BLOCKS:]
    for at in range(8):

        @pl.when(info[0] == at)
        def _():
            arrivals = [
                pltpu.make_async_copy(wholes[at + 8 * n], held.at[n], in_sem.at[n])
                for n in range(2)
            ]
            leaves = [
                pltpu.make_async_copy(held.at[n // 2], out.at[n], out_sem.at[n]) for n in range(4)
            ]
            for arrive in arrivals:
                arrive.start()
            for n, leave in enumerate(leaves):
                if n % 2 == 0:
                    arrivals[n // 2].wait()
                leave.start()
            for leave in leaves:
                leave.wait()


def pick(info, wholes):
    return pl.pallas_call(
        pick_body,
        out_shape=jax.ShapeDtypeStruct((4, OWN, WIDTH), BF),
        in_specs=[SM] + [ANY] * BLOCKS,
        out_specs=ANY,
        scratch_shapes=[
            pltpu.VMEM((2, OWN, WIDTH), BF),
            pltpu.SemaphoreType.DMA((2,)),
            pltpu.SemaphoreType.DMA((4,)),
        ],
        compiler_params=pltpu.CompilerParams(vmem_limit_bytes=56 * MIB),
        name="pick",
    )(info, *wholes)


def sinusoid(steps, half_width):
    rates = jnp.exp(-math.log(10000.0) * jnp.arange(half_width, dtype=F32) / half_width)
    angles = steps.astype(F32)[:, None] * rates[None, :]
    return jnp.concatenate([jnp.cos(angles), jnp.sin(angles)], axis=-1)


def on_device(
    features, timesteps, plan, conv_weight, skip_weight, time_weight, norm_gain, norm_bias
):
    segment, tile = lax.axis_index("segment"), lax.axis_index("tile")
    core, odd = segment % 2, tile % 2
    quarter = jnp.where(odd == 1, 1 + core, 3 * core)
    slot = 4 * (tile // 8) + (tile % 8) // 2
    active = (segment < 2).astype(jnp.int32)

    info = jnp.stack([quarter, slot, active]).astype(jnp.int32)

    served = lax.dynamic_index_in_dim(
        features, plan[jnp.minimum(segment, MICRO - 1)], 0, keepdims=False
    )
    served = served.transpose(0, 2, 1).reshape(PIECE, WIDTH)
    pieces = []
    for k in range(4):
        route = [
            (j * TILES + 4 * q + (k ^ j % 4), place(j, q)) for j in range(MICRO) for q in range(4)
        ]
        pieces.append(lax.ppermute(served, BOTH, route))

    encoded = sinusoid(timesteps[plan], time_weight.shape[1] // 2)
    shifts = jnp.dot(encoded, time_weight[0], precision=lax.Precision.HIGHEST)
    params = jnp.concatenate([norm_gain, norm_bias, jnp.zeros((6, CH), F32), shifts], axis=0)
    high = lax.reduce_precision(params, 8, 7)
    left = params - high
    middle = lax.reduce_precision(left, 8, 7)
    coded = jnp.concatenate([high, middle, left - middle], axis=0).astype(BF)
    skips = lax.all_gather(skip_weight[0].T, "segment")
    conv = conv_weight[0].T
    padding = jnp.zeros((CH, LEAD - TAPS - STATS), BF)
    lead = (conv[:, :HALF], jnp.concatenate([conv[:, HALF:], coded.T, padding], axis=1))
    first_up = BLOCKS - DOWN

    def fetch(index, half, after):
        own, _ = lax.optimization_barrier((lead[half], after))
        first, second = PAIRS[index]
        return lax.ppermute(own, "segment", [(first, 0), (second, 1)])

    def exchange(near, cross, stats):
        other_tile = [(t, t ^ 1) for t in range(TILES)]
        other_core = [(b, b ^ 1) for b in range(BLOCKS)]
        both = [
            (b * TILES + t, (b ^ 1) * TILES + (t ^ 1)) for b in range(BLOCKS) for t in range(TILES)
        ]
        return (
            lax.ppermute(near, "tile", other_tile),
            lax.ppermute(cross, "segment", other_core),
            lax.ppermute(stats, BOTH, both),
        )

    def hand_over(block, whole):
        route = [(place(j, q), helper(block, j, q)) for j in range(MICRO) for q in range(4)]
        return lax.ppermute(whole, BOTH, route)

    member_at = jnp.arange(CH) // GROUP
    member = (member_at[:, None] == member_at[None, :]).astype(BF)
    weights, cores, fetched = {}, {}, {}

    def swap_cores(index, own):
        both = [own, lax.ppermute(own, "segment", [(b, b ^ 1) for b in range(BLOCKS)])]
        for at, block in enumerate(PAIRS[index]):
            weights[block], cores[block] = weights.get(block, []) + both, at

    for own in lead:
        swap_cores(0, own)
    *exchanged, source = first_call(info, pieces)
    fetched[1, 0] = fetch(1, 0, pieces[0])
    fetched[1, 1] = fetch(1, 1, source)
    wholes, edges_of, passing = [], {}, []
    for block in range(BLOCKS):
        up_in, up_out = block >= first_up, first_up - 1 <= block < BLOCKS - 1
        near, cross, stats = exchanged
        near_in, cross_in, far = exchange(near, cross, stats)
        edges_of[block] = (near_in, cross_in)
        if block >= 1:
            sent, _ = lax.optimization_barrier((wholes[-1], (near_in, cross_in, far)))
            passing.append(hand_over(block - 1, sent))
        if block >= 4:
            source, near_in, cross_in, far, passing[block - 4] = lax.optimization_barrier(
                (source, near_in, cross_in, far, passing[block - 4])
            )
        whole, exchanged, summed = block_call(
            block,
            cores[block],
            info,
            source,
            (near_in, cross_in, stats, far),
            member,
            weights[block],
            skips,
            edges_of[BLOCKS - block] if up_in else None,
            wholes[BLOCKS - 2 - block] if up_out else None,
        )
        wholes.append(whole)
        source = summed if up_out else whole
        for key, after in SWAP_AFTER.items():
            if after == block:
                own, _ = lax.optimization_barrier((fetched[key], whole))
                swap_cores(key[0], own)
        for key, after in FETCH_AFTER.items():
            if after == block:
                fetched[key] = fetch(*key, whole)
    passing.append(hand_over(BLOCKS - 1, wholes[-1]))
    held = pick((segment % 8).astype(jnp.int32)[None], passing)
    peers = [
        [(s + 8 * far) * TILES + 8 * side + z for far in range(2) for z in range(8)]
        for s in range(8)
        for side in range(2)
    ]
    got = lax.all_to_all(
        held.reshape(2 * MICRO, PIECE, WIDTH), BOTH, 0, 0, axis_index_groups=peers, tiled=True
    )
    parity = (tile % 8) // 4 ^ tile // 8
    out = lax.dynamic_index_in_dim(
        got.reshape(MICRO, 2, PIECE, WIDTH), parity, 1, keepdims=False
    )
    out = out.reshape(1, MICRO, 3, CH, WIDTH)
    return out.transpose(0, 1, 2, 4, 3)


def solution(mesh):
    placed = (
        P(None, "tile", None, None),
        P(),
        P(),
        P("segment", None, None),
        P("segment", None, None),
        P("segment", None, None),
        P("segment", None),
        P("segment", None),
    )
    return jax.shard_map(
        on_device,
        mesh=mesh,
        in_specs=placed,
        out_specs=P("segment", None, "tile", None, None),
        check_vma=False,
    )
```

```python
import functools
import math

import jax
import jax.numpy as jnp
from jax import lax
from jax.experimental import pallas as pl
from jax.experimental.pallas import tpu as pltpu
from jax.sharding import PartitionSpec as P

BLOCKS, MICRO, TILES, DOWN = 16, 8, 16, 4
WIDTH, CH, GROUP = 128, 320, 10
CAT = 3 * CH
TAPS = 9 * CH
ROWS = 12
PIECE = 3 * CH
OWN = ROWS * CH
MEMBERS = float(48 * WIDTH * GROUP)
MIB = 1024 * 1024
LEAD = 2944
HALF = 1536
STATS = 48
BF, F32 = jnp.bfloat16, jnp.float32
ANY = pl.BlockSpec(memory_space=pl.ANY)
VM = pl.BlockSpec(memory_space=pltpu.VMEM)
SM = pl.BlockSpec(memory_space=pltpu.SMEM)
BOTH = ("segment", "tile")

PAIRS = ((0, 1), (2, 6), (3, 7), (4, 8), (5, 9), (10, 14), (11, 12), (13, 15))
FETCH_AFTER = {(2, 0): 0, (2, 1): 1, (3, 0): 1, (3, 1): 2, (4, 0): 2, (4, 1): 3}
FETCH_AFTER |= {(5, 0): 5, (5, 1): 6, (6, 0): 7, (6, 1): 8, (7, 0): 9, (7, 1): 10}
SWAP_AFTER = {(1, 0): 0, (1, 1): 1, (2, 0): 1, (2, 1): 2, (3, 0): 2, (3, 1): 3, (4, 0): 3, (4, 1): 4}
SWAP_AFTER |= {(5, 0): 6, (5, 1): 7, (6, 0): 8, (6, 1): 9, (7, 0): 10, (7, 1): 11}

DONE_BY = {14: [11, 12], 15: [13]}


def place(slot, quarter):
    tile = (slot // 4) * 8 + 2 * (slot % 4) + (quarter in (1, 2))
    return (quarter // 2) * TILES + tile


def helper(block, slot, quarter):
    segment = block % 8 + slot // 4 * 8
    return segment * TILES + quarter // 2 * 8 + place(slot, quarter) % 8


def chunk_at(turn, k):
    chunk = k ^ lax.rem(turn, 4)
    return pl.multiple_of(chunk * PIECE, PIECE)


def send_sums(info, totals, squares, source, near, cross, stats):
    ones = jnp.ones((8, WIDTH), F32)
    rows = jnp.concatenate(
        [
            lax.dot_general(
                ones,
                part,
                (((1,), (1,)), ((), ())),
                precision=lax.Precision.HIGHEST,
                preferred_element_type=F32,
            )[0:1]
            for part in (totals, squares)
        ],
        axis=0,
    )
    high = rows.astype(BF).astype(F32)
    left = rows - high
    middle = left.astype(BF).astype(F32)
    low = left - middle
    coded = jnp.concatenate([high, middle, low, jnp.zeros((10, CH), F32)], axis=0)
    coded = jnp.concatenate([coded, jnp.zeros((16, 64), F32)], axis=1).astype(BF)
    even = lax.rem(info[0], 2) == 0
    first, last = source[0:CH, :], source[OWN - CH : OWN, :]
    near[0:CH, :] = jnp.where(even, last, first)
    cross[0:CH, :] = jnp.where(even, first, last)
    for i in range(3):
        part = coded[:, i * 128 : (i + 1) * 128]
        near[CH + 16 * i : CH + 16 * (i + 1), :] = part
        cross[CH + 16 * i : CH + 16 * (i + 1), :] = part
        stats[16 * i : 16 * (i + 1), :] = part


def first_body(info, *refs):
    pieces, (near, cross, stats, whole), (xs, sem) = refs[:4], refs[4:8], refs[8:]

    @pl.when(info[2] == 1)
    def _():
        copies = [
            pltpu.make_async_copy(pieces[k], xs.at[pl.ds(chunk_at(info[1], k), PIECE)], sem.at[k])
            for k in range(4)
        ]
        for copy in copies:
            copy.start()
        for copy in copies:
            copy.wait()
        final = pltpu.make_async_copy(xs, whole, sem.at[0])
        final.start()
        totals = squares = jnp.zeros((CH, WIDTH), F32)
        for r in range(ROWS):
            row = xs[r * CH : (r + 1) * CH, :].astype(F32)
            totals, squares = totals + row, squares + row * row
        send_sums(info, totals, squares, xs, near, cross, stats)
        final.wait()


def block_body(block, at_core, up_in, up_out, last, info, *refs):
    refs = list(refs)

    def take(n):
        got = refs[:n]
        del refs[:n]
        return got

    source, near, cross, own_stats, far_stats, member = take(6)
    weights = take(4)
    if up_in or up_out:
        (skips,) = take(1)
    if up_in:
        lateral_edges = take(2)
    if up_out:
        (lateral,) = take(1)
    (result,) = take(1)
    if not last:
        near_out, cross_out, stats_out = take(3)
    if up_out:
        (summed_out,) = take(1)
    xs = source
    ws, ps, cat, totals, squares, w_sem = take(6)
    if up_in:
        (sk_in,) = take(1)
    if up_out:
        ls, sums = lateral, summed_out
        sk, l_sem = take(2)

    @pl.when(info[2] == 1)
    def _():
        core = info[0] // 2
        head = pl.ds(LEAD - HALF - WIDTH, WIDTH)
        halves = (pl.ds(0, HALF), pl.ds(HALF, LEAD - HALF))
        for at in range(2):

            @pl.when((core == at_core) == (at == 0))
            def _():
                pltpu.make_async_copy(weights[2 + at].at[:, head], ps, w_sem.at[2]).start()
                for n, part in enumerate(halves):
                    pltpu.make_async_copy(
                        weights[2 * n + at], ws.at[:, part], w_sem.at[3 * n]
                    ).start()

        if up_in:
            in_copy = pltpu.make_async_copy(skips.at[block], sk_in, w_sem.at[1])
            in_copy.start()
        if up_out:
            out_copy = pltpu.make_async_copy(skips.at[block + 1], sk, l_sem.at[0])
            out_copy.start()

        coded = [jnp.concatenate([ref[a + 16 * i : a + 16 * i + 16, :] for i in range(3)], axis=1)
                 for ref, a in ((own_stats, 0), (far_stats, 0), (near, CH), (cross, CH))]
        coded = jnp.concatenate(coded, axis=0)[:, 0:CH]
        groups = lax.dot_general(
            member[...], coded, (((1,), (1,)), ((), ())), preferred_element_type=F32
        )
        kind = lax.rem(lax.broadcasted_iota(jnp.int32, (CH, 64), 1), 16)
        even_kind = lax.rem(kind, 2) == 0
        mean = jnp.sum(jnp.where(even_kind, groups, 0.0), axis=1, keepdims=True) / MEMBERS
        mean_sq = jnp.sum(jnp.where(even_kind, 0.0, groups), axis=1, keepdims=True) / MEMBERS
        variance = jnp.maximum(mean_sq - mean * mean, 0.0)
        pltpu.make_async_copy(weights[2].at[:, head], ps, w_sem.at[2]).wait()
        tailing = ps[:, 64:128].astype(F32)
        params = tailing[:, 0:16] + tailing[:, 16:32] + tailing[:, 32:48]
        lane = lax.broadcasted_iota(jnp.int32, (CH, 16), 1)
        shift = jnp.sum(jnp.where(lane == info[1] + 8, params, 0.0), axis=1, keepdims=True)
        wide = (CH, WIDTH)
        gain = jnp.broadcast_to(params[:, 0:1] * lax.rsqrt(variance + 1e-5) * 0.5, wide)
        bias = jnp.broadcast_to(params[:, 1:2] * 0.5, wide)
        mean = jnp.broadcast_to(mean, wide)
        shift = jnp.broadcast_to(shift, wide)
        column = lax.broadcasted_iota(jnp.int32, wide, 1)

        def lift(x, row, keep=None):
            h = (x - mean) * gain + bias
            lifted = h * jnp.tanh(h) + h + shift
            if keep is not None:
                lifted = jnp.where(keep, lifted, 0.0)
            left = jnp.where(column == 0, 0.0, pltpu.roll(lifted, 1, 1)).astype(BF)
            right = jnp.where(column == WIDTH - 1, 0.0, pltpu.roll(lifted, WIDTH - 1, 1)).astype(BF)
            cols = pl.ds(row * WIDTH, WIDTH)
            if not isinstance(row, int):
                cols = pl.ds(pl.multiple_of(row * WIDTH, WIDTH), WIDTH)
            cat[0:CH, cols] = left
            cat[CH : 2 * CH, cols] = lifted.astype(BF)
            cat[2 * CH : 3 * CH, cols] = right

        even = lax.rem(info[0], 2) == 0
        near_rows, cross_rows = near[0:CH, :].astype(F32), cross[0:CH, :].astype(F32)
        if up_in:
            in_copy.wait()
            skip_in = sk_in[...]
            near_rows, cross_rows = (
                rows + jnp.dot(skip_in, edge[0:CH, :], preferred_element_type=F32)
                for rows, edge in zip((near_rows, cross_rows), lateral_edges)
            )
        def own_row(r):
            return slice(r * CH, (r + 1) * CH)

        if up_out:
            out_copy.wait()
            skip = sk[...]
        totals[...] = jnp.zeros(wide, F32)
        squares[...] = jnp.zeros(wide, F32)

        def lift_at(row):
            if row == 0:
                lift(jnp.where(even, cross_rows, near_rows), 0, info[0] > 0)
            elif row == ROWS + 1:
                lift(jnp.where(even, near_rows, cross_rows), row, info[0] < 3)
            else:
                lift(xs[(row - 1) * CH : row * CH, :].astype(F32), row)

        for row in range(2):
            lift_at(row)
        lift_at(2)
        lift_at(3)
        for n, part in enumerate(halves):
            pltpu.make_async_copy(weights[2 * n], ws.at[:, part], w_sem.at[3 * n]).wait()
        for pair in range(ROWS // 2):
            if pair:
                lift_at(2 * pair + 2)
                lift_at(2 * pair + 3)
            convolved = sum(
                jnp.dot(
                    ws[:, dy * CAT : (dy + 1) * CAT],
                    cat[:, (2 * pair + dy) * WIDTH : (2 * pair + dy + 2) * WIDTH],
                    preferred_element_type=F32,
                )
                for dy in range(3)
            )
            rows = [own_row(2 * pair), own_row(2 * pair + 1)]
            if up_out:
                both = jnp.concatenate([ls[row, :] for row in rows], axis=1)
                projected = jnp.dot(skip, both, preferred_element_type=F32)
            for half, row in enumerate(rows):
                cols = slice(half * WIDTH, (half + 1) * WIDTH)
                kept = (xs[row, :].astype(F32) + convolved[:, cols]).astype(BF)
                result[row, :] = kept
                if not last:
                    following = kept.astype(F32)
                    if up_out:
                        following = following + projected[:, cols]
                        sums[row, :] = following
                    totals[...] += following
                    squares[...] += following * following

        if not last:
            send_sums(info, totals[...], squares[...], result, near_out, cross_out, stats_out)


EXCHANGED = [
    jax.ShapeDtypeStruct((CH + STATS, WIDTH), BF),
    jax.ShapeDtypeStruct((CH + STATS, WIDTH), BF),
    jax.ShapeDtypeStruct((STATS, WIDTH), BF),
]
WHOLE = jax.ShapeDtypeStruct((OWN, WIDTH), BF)


def first_call(info, pieces):
    return pl.pallas_call(
        first_body,
        out_shape=EXCHANGED + [WHOLE],
        in_specs=[SM] + [ANY] * 4,
        out_specs=[VM] * 3 + [ANY],
        scratch_shapes=[pltpu.VMEM((OWN, WIDTH), BF), pltpu.SemaphoreType.DMA((4,))],
        compiler_params=pltpu.CompilerParams(vmem_limit_bytes=16 * MIB),
        name="first_sums",
    )(info, *pieces)


def block_call(block, at_core, info, source, exchanged, member, weights, skips, lateral_edges, lateral):
    up_in, up_out = lateral_edges is not None, lateral is not None
    last = block == BLOCKS - 1
    operands = [source, *exchanged, member, *weights]
    specs = [VM] * 6 + [ANY] * 4
    shapes, out_specs = [WHOLE] + EXCHANGED, [VM] * 4
    if last:
        shapes, out_specs = shapes[:1], out_specs[:1]
    scratch = [
        pltpu.VMEM((CH, LEAD), BF),
        pltpu.VMEM((CH, WIDTH), BF),
        pltpu.VMEM((CAT, (ROWS + 2) * WIDTH), BF),
        pltpu.VMEM((CH, WIDTH), F32),
        pltpu.VMEM((CH, WIDTH), F32),
        pltpu.SemaphoreType.DMA((4,)),
    ]
    if up_in or up_out:
        operands.append(skips)
        specs.append(ANY)
    if up_in:
        operands += list(lateral_edges)
        specs += [VM] * 2
        scratch.append(pltpu.VMEM((CH, CH), BF))
    if up_out:
        operands.append(lateral)
        specs.append(VM)
        shapes = shapes + [jax.ShapeDtypeStruct((OWN, WIDTH), F32)]
        out_specs = out_specs + [VM]
        scratch += [pltpu.VMEM((CH, CH), BF), pltpu.SemaphoreType.DMA((1,))]
    out = pl.pallas_call(
        functools.partial(block_body, block, at_core, up_in, up_out, last),
        out_shape=shapes,
        in_specs=[SM] + specs,
        out_specs=out_specs,
        scratch_shapes=scratch,
        compiler_params=pltpu.CompilerParams(vmem_limit_bytes=28 * MIB),
        cost_estimate=pl.CostEstimate(
            flops=OWN * WIDTH * TAPS // 4, bytes_accessed=MIB, transcendentals=0
        ),
        name="res_block",
    )(info, *operands)
    return out[0], out[1:4], out[4] if up_out else None


def pick_body(info, *refs):
    wholes, out, held, in_sem, out_sem = refs[:BLOCKS], *refs[BLOCKS:]
    for at in range(8):

        @pl.when(info[0] == at)
        def _():
            arrivals = [
                pltpu.make_async_copy(wholes[at + 8 * n], held.at[n], in_sem.at[n])
                for n in range(2)
            ]
            leaves = [
                pltpu.make_async_copy(held.at[n // 2], out.at[n], out_sem.at[n]) for n in range(4)
            ]
            for arrive in arrivals:
                arrive.start()
            for n, leave in enumerate(leaves):
                if n % 2 == 0:
                    arrivals[n // 2].wait()
                leave.start()
            for leave in leaves:
                leave.wait()


def pick(info, wholes):
    return pl.pallas_call(
        pick_body,
        out_shape=jax.ShapeDtypeStruct((4, OWN, WIDTH), BF),
        in_specs=[SM] + [ANY] * BLOCKS,
        out_specs=ANY,
        scratch_shapes=[
            pltpu.VMEM((2, OWN, WIDTH), BF),
            pltpu.SemaphoreType.DMA((2,)),
            pltpu.SemaphoreType.DMA((4,)),
        ],
        compiler_params=pltpu.CompilerParams(vmem_limit_bytes=56 * MIB),
        name="pick",
    )(info, *wholes)


def sinusoid(steps, half_width):
    rates = jnp.exp(-math.log(10000.0) * jnp.arange(half_width, dtype=F32) / half_width)
    angles = steps.astype(F32)[:, None] * rates[None, :]
    return jnp.concatenate([jnp.cos(angles), jnp.sin(angles)], axis=-1)


def on_device(
    features, timesteps, plan, conv_weight, skip_weight, time_weight, norm_gain, norm_bias
):
    segment, tile = lax.axis_index("segment"), lax.axis_index("tile")
    core, odd = segment % 2, tile % 2
    quarter = jnp.where(odd == 1, 1 + core, 3 * core)
    slot = 4 * (tile // 8) + (tile % 8) // 2
    active = (segment < 2).astype(jnp.int32)

    info = jnp.stack([quarter, slot, active]).astype(jnp.int32)

    served = lax.dynamic_index_in_dim(
        features, plan[jnp.minimum(segment, MICRO - 1)], 0, keepdims=False
    )
    served = served.transpose(0, 2, 1).reshape(PIECE, WIDTH)
    pieces = []
    for k in range(4):
        route = [
            (j * TILES + 4 * q + (k ^ j % 4), place(j, q)) for j in range(MICRO) for q in range(4)
        ]
        pieces.append(lax.ppermute(served, BOTH, route))

    encoded = sinusoid(timesteps[plan], time_weight.shape[1] // 2)
    shifts = jnp.dot(encoded, time_weight[0], precision=lax.Precision.HIGHEST)
    params = jnp.concatenate([norm_gain, norm_bias, jnp.zeros((6, CH), F32), shifts], axis=0)
    high = lax.reduce_precision(params, 8, 7)
    left = params - high
    middle = lax.reduce_precision(left, 8, 7)
    coded = jnp.concatenate([high, middle, left - middle], axis=0).astype(BF)
    skips = lax.all_gather(skip_weight[0].T, "segment")
    conv = conv_weight[0].T
    padding = jnp.zeros((CH, LEAD - TAPS - STATS), BF)
    lead = (conv[:, :HALF], jnp.concatenate([conv[:, HALF:], coded.T, padding], axis=1))
    first_up = BLOCKS - DOWN

    def fetch(index, half, after):
        own, _ = lax.optimization_barrier((lead[half], after))
        first, second = PAIRS[index]
        return lax.ppermute(own, "segment", [(first, 0), (second, 1)])

    def exchange(near, cross, stats):
        other_tile = [(t, t ^ 1) for t in range(TILES)]
        other_core = [(b, b ^ 1) for b in range(BLOCKS)]
        both = [
            (b * TILES + t, (b ^ 1) * TILES + (t ^ 1)) for b in range(BLOCKS) for t in range(TILES)
        ]
        return (
            lax.ppermute(near, "tile", other_tile),
            lax.ppermute(cross, "segment", other_core),
            lax.ppermute(stats, BOTH, both),
        )

    def hand_over(block, whole):
        route = [(place(j, q), helper(block, j, q)) for j in range(MICRO) for q in range(4)]
        return lax.ppermute(whole, BOTH, route)

    member_at = jnp.arange(CH) // GROUP
    member = (member_at[:, None] == member_at[None, :]).astype(BF)
    weights, cores, fetched = {}, {}, {}

    def swap_cores(index, own):
        both = [own, lax.ppermute(own, "segment", [(b, b ^ 1) for b in range(BLOCKS)])]
        for at, block in enumerate(PAIRS[index]):
            weights[block], cores[block] = weights.get(block, []) + both, at

    for own in lead:
        own, _ = lax.optimization_barrier((own, pieces))
        swap_cores(0, own)
    *exchanged, source = first_call(info, pieces)
    fetched[1, 0] = fetch(1, 0, pieces)
    fetched[1, 1] = fetch(1, 1, source)
    wholes, edges_of, passing = [], {}, []
    for block in range(BLOCKS):
        up_in, up_out = block >= first_up, first_up - 1 <= block < BLOCKS - 1
        near, cross, stats = exchanged
        near_in, cross_in, far = exchange(near, cross, stats)
        edges_of[block] = (near_in, cross_in)
        if block >= 1:
            sent, _ = lax.optimization_barrier((wholes[-1], (near_in, cross_in, far)))
            passing.append(hand_over(block - 1, sent))
        for arrived in DONE_BY.get(block, [block - 3]):
            if arrived >= 0:
                source, near_in, cross_in, far, passing[arrived] = lax.optimization_barrier(
                    (source, near_in, cross_in, far, passing[arrived])
                )
        whole, exchanged, summed = block_call(
            block,
            cores[block],
            info,
            source,
            (near_in, cross_in, stats, far),
            member,
            weights[block],
            skips,
            edges_of[BLOCKS - block] if up_in else None,
            wholes[BLOCKS - 2 - block] if up_out else None,
        )
        wholes.append(whole)
        source = summed if up_out else whole
        for key, after in SWAP_AFTER.items():
            if after == block:
                own, _ = lax.optimization_barrier((fetched[key], whole))
                swap_cores(key[0], own)
        for key, after in FETCH_AFTER.items():
            if after == block:
                fetched[key] = fetch(*key, whole)
    passing.append(hand_over(BLOCKS - 1, wholes[-1]))
    held = pick((segment % 8).astype(jnp.int32)[None], passing)
    peers = [
        [(s + 8 * far) * TILES + 8 * side + z for far in range(2) for z in range(8)]
        for s in range(8)
        for side in range(2)
    ]
    got = lax.all_to_all(
        held.reshape(2 * MICRO, PIECE, WIDTH), BOTH, 0, 0, axis_index_groups=peers, tiled=True
    )
    parity = (tile % 8) // 4 ^ tile // 8
    out = lax.dynamic_index_in_dim(
        got.reshape(MICRO, 2, PIECE, WIDTH), parity, 1, keepdims=False
    )
    out = out.reshape(1, MICRO, 3, CH, WIDTH)
    return out.transpose(0, 1, 2, 4, 3)


def solution(mesh):
    placed = (
        P(None, "tile", None, None),
        P(),
        P(),
        P("segment", None, None),
        P("segment", None, None),
        P("segment", None, None),
        P("segment", None),
        P("segment", None),
    )
    return jax.shard_map(
        on_device,
        mesh=mesh,
        in_specs=placed,
        out_specs=P("segment", None, "tile", None, None),
        check_vma=False,
    )
```

```python
import functools
import math

import jax
import jax.numpy as jnp
from jax import lax
from jax.experimental import pallas as pl
from jax.experimental.pallas import tpu as pltpu
from jax.sharding import PartitionSpec as P

BLOCKS, MICRO, TILES, DOWN = 16, 8, 16, 4
WIDTH, CH, GROUP = 128, 320, 10
CAT = 3 * CH
TAPS = 9 * CH
ROWS = 12
PIECE = 3 * CH
PART = PIECE // 2
OWN = ROWS * CH
MEMBERS = float(48 * WIDTH * GROUP)
MIB = 1024 * 1024
LEAD = 2944
HALF = 1536
STATS = 48
BF, F32 = jnp.bfloat16, jnp.float32
ANY = pl.BlockSpec(memory_space=pl.ANY)
VM = pl.BlockSpec(memory_space=pltpu.VMEM)
SM = pl.BlockSpec(memory_space=pltpu.SMEM)
BOTH = ("segment", "tile")

PAIRS = ((0, 1), (2, 6), (3, 7), (4, 8), (5, 9), (10, 14), (11, 12), (13, 15))
FETCH_AFTER = {(2, 0): 0, (2, 1): 1, (3, 0): 1, (3, 1): 2, (4, 0): 2, (4, 1): 3}
FETCH_AFTER |= {(5, 0): 5, (5, 1): 6, (6, 0): 7, (6, 1): 8, (7, 0): 9, (7, 1): 10}
SWAP_AFTER = {(1, 0): 0, (1, 1): 1, (2, 0): 1, (2, 1): 2, (3, 0): 2, (3, 1): 3, (4, 0): 3, (4, 1): 4}
SWAP_AFTER |= {(5, 0): 6, (5, 1): 7, (6, 0): 8, (6, 1): 9, (7, 0): 10, (7, 1): 11}

DONE_BY = {14: [11, 12], 15: [13]}


def place(slot, quarter):
    tile = (slot // 4) * 8 + 2 * (slot % 4) + (quarter in (1, 2))
    return (quarter // 2) * TILES + tile


def helper(block, slot, quarter):
    segment = block % 8 + slot // 4 * 8
    return segment * TILES + quarter // 2 * 8 + place(slot, quarter) % 8


def chunk_at(turn, k):
    chunk = k ^ lax.rem(turn, 4)
    return pl.multiple_of(chunk * PIECE, PIECE)


def send_sums(info, totals, squares, source, near, cross, stats):
    ones = jnp.ones((8, WIDTH), F32)
    rows = jnp.concatenate(
        [
            lax.dot_general(
                ones,
                part,
                (((1,), (1,)), ((), ())),
                precision=lax.Precision.HIGHEST,
                preferred_element_type=F32,
            )[0:1]
            for part in (totals, squares)
        ],
        axis=0,
    )
    high = rows.astype(BF).astype(F32)
    left = rows - high
    middle = left.astype(BF).astype(F32)
    low = left - middle
    coded = jnp.concatenate([high, middle, low, jnp.zeros((10, CH), F32)], axis=0)
    coded = jnp.concatenate([coded, jnp.zeros((16, 64), F32)], axis=1).astype(BF)
    even = lax.rem(info[0], 2) == 0
    first, last = source[0:CH, :], source[OWN - CH : OWN, :]
    near[0:CH, :] = jnp.where(even, last, first)
    cross[0:CH, :] = jnp.where(even, first, last)
    for i in range(3):
        part = coded[:, i * 128 : (i + 1) * 128]
        near[CH + 16 * i : CH + 16 * (i + 1), :] = part
        cross[CH + 16 * i : CH + 16 * (i + 1), :] = part
        stats[16 * i : 16 * (i + 1), :] = part


def first_body(info, *refs):
    pieces, (near, cross, stats, whole), (xs, sem) = refs[:4], refs[4:8], refs[8:]

    @pl.when(info[2] == 1)
    def _():
        copies = [
            pltpu.make_async_copy(pieces[k], xs.at[pl.ds(chunk_at(info[1], k), PIECE)], sem.at[k])
            for k in range(4)
        ]
        for copy in copies:
            copy.start()
        for copy in copies:
            copy.wait()
        final = pltpu.make_async_copy(xs, whole, sem.at[0])
        final.start()
        totals = squares = jnp.zeros((CH, WIDTH), F32)
        for r in range(ROWS):
            row = xs[r * CH : (r + 1) * CH, :].astype(F32)
            totals, squares = totals + row, squares + row * row
        send_sums(info, totals, squares, xs, near, cross, stats)
        final.wait()


def block_body(block, at_core, up_in, up_out, last, info, *refs):
    refs = list(refs)

    def take(n):
        got = refs[:n]
        del refs[:n]
        return got

    source, near, cross, own_stats, far_stats, member = take(6)
    weights = take(4)
    if up_in or up_out:
        (skips,) = take(1)
    if up_in:
        lateral_edges = take(2)
    if up_out:
        (lateral,) = take(1)
    (result,) = take(1)
    if not last:
        near_out, cross_out, stats_out = take(3)
    if up_out:
        (summed_out,) = take(1)
    xs = source
    ws, ps, cat, totals, squares, w_sem = take(6)
    if up_in:
        (sk_in,) = take(1)
    if up_out:
        ls, sums = lateral, summed_out
        sk, l_sem = take(2)

    @pl.when(info[2] == 1)
    def _():
        core = info[0] // 2
        head = pl.ds(LEAD - HALF - WIDTH, WIDTH)
        halves = (pl.ds(0, HALF), pl.ds(HALF, LEAD - HALF))
        for at in range(2):

            @pl.when((core == at_core) == (at == 0))
            def _():
                pltpu.make_async_copy(weights[2 + at].at[:, head], ps, w_sem.at[2]).start()
                for n, part in enumerate(halves):
                    pltpu.make_async_copy(
                        weights[2 * n + at], ws.at[:, part], w_sem.at[3 * n]
                    ).start()

        if up_in:
            in_copy = pltpu.make_async_copy(skips.at[block], sk_in, w_sem.at[1])
            in_copy.start()
        if up_out:
            out_copy = pltpu.make_async_copy(skips.at[block + 1], sk, l_sem.at[0])
            out_copy.start()

        coded = [jnp.concatenate([ref[a + 16 * i : a + 16 * i + 16, :] for i in range(3)], axis=1)
                 for ref, a in ((own_stats, 0), (far_stats, 0), (near, CH), (cross, CH))]
        coded = jnp.concatenate(coded, axis=0)[:, 0:CH]
        groups = lax.dot_general(
            member[...], coded, (((1,), (1,)), ((), ())), preferred_element_type=F32
        )
        kind = lax.rem(lax.broadcasted_iota(jnp.int32, (CH, 64), 1), 16)
        even_kind = lax.rem(kind, 2) == 0
        mean = jnp.sum(jnp.where(even_kind, groups, 0.0), axis=1, keepdims=True) / MEMBERS
        mean_sq = jnp.sum(jnp.where(even_kind, 0.0, groups), axis=1, keepdims=True) / MEMBERS
        variance = jnp.maximum(mean_sq - mean * mean, 0.0)
        pltpu.make_async_copy(weights[2].at[:, head], ps, w_sem.at[2]).wait()
        tailing = ps[:, 64:128].astype(F32)
        params = tailing[:, 0:16] + tailing[:, 16:32] + tailing[:, 32:48]
        lane = lax.broadcasted_iota(jnp.int32, (CH, 16), 1)
        shift = jnp.sum(jnp.where(lane == info[1] + 8, params, 0.0), axis=1, keepdims=True)
        wide = (CH, WIDTH)
        gain = jnp.broadcast_to(params[:, 0:1] * lax.rsqrt(variance + 1e-5) * 0.5, wide)
        bias = jnp.broadcast_to(params[:, 1:2] * 0.5, wide)
        mean = jnp.broadcast_to(mean, wide)
        shift = jnp.broadcast_to(shift, wide)
        column = lax.broadcasted_iota(jnp.int32, wide, 1)

        def lift(x, row, keep=None):
            h = (x - mean) * gain + bias
            lifted = h * jnp.tanh(h) + h + shift
            if keep is not None:
                lifted = jnp.where(keep, lifted, 0.0)
            left = jnp.where(column == 0, 0.0, pltpu.roll(lifted, 1, 1)).astype(BF)
            right = jnp.where(column == WIDTH - 1, 0.0, pltpu.roll(lifted, WIDTH - 1, 1)).astype(BF)
            cols = pl.ds(row * WIDTH, WIDTH)
            if not isinstance(row, int):
                cols = pl.ds(pl.multiple_of(row * WIDTH, WIDTH), WIDTH)
            cat[0:CH, cols] = left
            cat[CH : 2 * CH, cols] = lifted.astype(BF)
            cat[2 * CH : 3 * CH, cols] = right

        even = lax.rem(info[0], 2) == 0
        near_rows, cross_rows = near[0:CH, :].astype(F32), cross[0:CH, :].astype(F32)
        if up_in:
            in_copy.wait()
            skip_in = sk_in[...]
            near_rows, cross_rows = (
                rows + jnp.dot(skip_in, edge[0:CH, :], preferred_element_type=F32)
                for rows, edge in zip((near_rows, cross_rows), lateral_edges)
            )
        def own_row(r):
            return slice(r * CH, (r + 1) * CH)

        if up_out:
            out_copy.wait()
            skip = sk[...]
        totals[...] = jnp.zeros(wide, F32)
        squares[...] = jnp.zeros(wide, F32)

        def lift_at(row):
            if row == 0:
                lift(jnp.where(even, cross_rows, near_rows), 0, info[0] > 0)
            elif row == ROWS + 1:
                lift(jnp.where(even, near_rows, cross_rows), row, info[0] < 3)
            else:
                lift(xs[(row - 1) * CH : row * CH, :].astype(F32), row)

        for row in range(2):
            lift_at(row)
        lift_at(2)
        lift_at(3)
        for n, part in enumerate(halves):
            pltpu.make_async_copy(weights[2 * n], ws.at[:, part], w_sem.at[3 * n]).wait()
        for pair in range(ROWS // 2):
            if pair:
                lift_at(2 * pair + 2)
                lift_at(2 * pair + 3)
            convolved = sum(
                jnp.dot(
                    ws[:, dy * CAT : (dy + 1) * CAT],
                    cat[:, (2 * pair + dy) * WIDTH : (2 * pair + dy + 2) * WIDTH],
                    preferred_element_type=F32,
                )
                for dy in range(3)
            )
            rows = [own_row(2 * pair), own_row(2 * pair + 1)]
            if up_out:
                both = jnp.concatenate([ls[row, :] for row in rows], axis=1)
                projected = jnp.dot(skip, both, preferred_element_type=F32)
            for half, row in enumerate(rows):
                cols = slice(half * WIDTH, (half + 1) * WIDTH)
                kept = (xs[row, :].astype(F32) + convolved[:, cols]).astype(BF)
                result[row, :] = kept
                if not last:
                    following = kept.astype(F32)
                    if up_out:
                        following = following + projected[:, cols]
                        sums[row, :] = following
                    totals[...] += following
                    squares[...] += following * following

        if not last:
            send_sums(info, totals[...], squares[...], result, near_out, cross_out, stats_out)


EXCHANGED = [
    jax.ShapeDtypeStruct((CH + STATS, WIDTH), BF),
    jax.ShapeDtypeStruct((CH + STATS, WIDTH), BF),
    jax.ShapeDtypeStruct((STATS, WIDTH), BF),
]
WHOLE = jax.ShapeDtypeStruct((OWN, WIDTH), BF)


def first_call(info, pieces):
    return pl.pallas_call(
        first_body,
        out_shape=EXCHANGED + [WHOLE],
        in_specs=[SM] + [ANY] * 4,
        out_specs=[VM] * 3 + [ANY],
        scratch_shapes=[pltpu.VMEM((OWN, WIDTH), BF), pltpu.SemaphoreType.DMA((4,))],
        compiler_params=pltpu.CompilerParams(vmem_limit_bytes=16 * MIB),
        name="first_sums",
    )(info, *pieces)


def block_call(block, at_core, info, source, exchanged, member, weights, skips, lateral_edges, lateral):
    up_in, up_out = lateral_edges is not None, lateral is not None
    last = block == BLOCKS - 1
    operands = [source, *exchanged, member, *weights]
    specs = [VM] * 6 + [ANY] * 4
    shapes, out_specs = [WHOLE] + EXCHANGED, [VM] * 4
    if last:
        shapes, out_specs = shapes[:1], out_specs[:1]
    scratch = [
        pltpu.VMEM((CH, LEAD), BF),
        pltpu.VMEM((CH, WIDTH), BF),
        pltpu.VMEM((CAT, (ROWS + 2) * WIDTH), BF),
        pltpu.VMEM((CH, WIDTH), F32),
        pltpu.VMEM((CH, WIDTH), F32),
        pltpu.SemaphoreType.DMA((4,)),
    ]
    if up_in or up_out:
        operands.append(skips)
        specs.append(ANY)
    if up_in:
        operands += list(lateral_edges)
        specs += [VM] * 2
        scratch.append(pltpu.VMEM((CH, CH), BF))
    if up_out:
        operands.append(lateral)
        specs.append(VM)
        shapes = shapes + [jax.ShapeDtypeStruct((OWN, WIDTH), F32)]
        out_specs = out_specs + [VM]
        scratch += [pltpu.VMEM((CH, CH), BF), pltpu.SemaphoreType.DMA((1,))]
    out = pl.pallas_call(
        functools.partial(block_body, block, at_core, up_in, up_out, last),
        out_shape=shapes,
        in_specs=[SM] + specs,
        out_specs=out_specs,
        scratch_shapes=scratch,
        compiler_params=pltpu.CompilerParams(vmem_limit_bytes=28 * MIB),
        cost_estimate=pl.CostEstimate(
            flops=OWN * WIDTH * TAPS // 4, bytes_accessed=MIB, transcendentals=0
        ),
        name="res_block",
    )(info, *operands)
    return out[0], out[1:4], out[4] if up_out else None


def pick_body(info, *refs):
    wholes, (kept, sent, held, in_sem, out_sem) = refs[:8], refs[8:]
    for at in range(8):

        @pl.when(info[0] == at)
        def _():
            arrive = pltpu.make_async_copy(wholes[at], held, in_sem.at[0])
            arrive.start()
            arrive.wait()

    leaves = []
    for chunk in range(4):
        for n, out in enumerate((kept, sent)):
            half = info[1] if n == 0 else 1 - info[1]
            rows = pl.ds(pl.multiple_of(chunk * PIECE + half * PART, PART), PART)
            leaves.append(
                pltpu.make_async_copy(held.at[rows], out.at[chunk], out_sem.at[2 * chunk + n])
            )
    for leave in leaves:
        leave.start()
    for leave in leaves:
        leave.wait()


def pick(info, wholes):
    return pl.pallas_call(
        pick_body,
        out_shape=[jax.ShapeDtypeStruct((4, PART, WIDTH), BF)] * 2,
        in_specs=[SM] + [ANY] * 8,
        out_specs=[ANY] * 2,
        scratch_shapes=[
            pltpu.VMEM((OWN, WIDTH), BF),
            pltpu.SemaphoreType.DMA((1,)),
            pltpu.SemaphoreType.DMA((8,)),
        ],
        compiler_params=pltpu.CompilerParams(vmem_limit_bytes=56 * MIB),
        name="pick",
    )(info, *wholes)


def join_body(info, *refs):
    parts, (out, held, in_sem, out_sem) = refs[:4], refs[4:]
    copies = []
    for n, part in enumerate(parts):
        first = info[0] if n % 2 == 0 else 1 - info[0]
        rows = pl.ds(n // 2 * 8 + 4 * (1 - first), 4)
        copies.append(
            (
                pltpu.make_async_copy(part, held.at[n], in_sem.at[n]),
                pltpu.make_async_copy(held.at[n], out.at[rows], out_sem.at[n]),
            )
        )
    for arrive, _ in copies:
        arrive.start()
    for arrive, leave in copies:
        arrive.wait()
        leave.start()
    for _, leave in copies:
        leave.wait()


def join(info, parts):
    return pl.pallas_call(
        join_body,
        out_shape=jax.ShapeDtypeStruct((16, PART, WIDTH), BF),
        in_specs=[SM] + [ANY] * 4,
        out_specs=ANY,
        scratch_shapes=[
            pltpu.VMEM((4, 4, PART, WIDTH), BF),
            pltpu.SemaphoreType.DMA((4,)),
            pltpu.SemaphoreType.DMA((4,)),
        ],
        compiler_params=pltpu.CompilerParams(vmem_limit_bytes=56 * MIB),
        name="join",
    )(info, *parts)


def sinusoid(steps, half_width):
    rates = jnp.exp(-math.log(10000.0) * jnp.arange(half_width, dtype=F32) / half_width)
    angles = steps.astype(F32)[:, None] * rates[None, :]
    return jnp.concatenate([jnp.cos(angles), jnp.sin(angles)], axis=-1)


def on_device(
    features, timesteps, plan, conv_weight, skip_weight, time_weight, norm_gain, norm_bias
):
    segment, tile = lax.axis_index("segment"), lax.axis_index("tile")
    core, odd = segment % 2, tile % 2
    quarter = jnp.where(odd == 1, 1 + core, 3 * core)
    slot = 4 * (tile // 8) + (tile % 8) // 2
    active = (segment < 2).astype(jnp.int32)

    info = jnp.stack([quarter, slot, active]).astype(jnp.int32)

    served = lax.dynamic_index_in_dim(
        features, plan[jnp.minimum(segment, MICRO - 1)], 0, keepdims=False
    )
    served = served.transpose(0, 2, 1).reshape(PIECE, WIDTH)
    pieces = []
    for k in range(4):
        route = [
            (j * TILES + 4 * q + (k ^ j % 4), place(j, q)) for j in range(MICRO) for q in range(4)
        ]
        pieces.append(lax.ppermute(served, BOTH, route))

    encoded = sinusoid(timesteps[plan], time_weight.shape[1] // 2)
    shifts = jnp.dot(encoded, time_weight[0], precision=lax.Precision.HIGHEST)
    params = jnp.concatenate([norm_gain, norm_bias, jnp.zeros((6, CH), F32), shifts], axis=0)
    high = lax.reduce_precision(params, 8, 7)
    left = params - high
    middle = lax.reduce_precision(left, 8, 7)
    coded = jnp.concatenate([high, middle, left - middle], axis=0).astype(BF)
    skips = lax.all_gather(skip_weight[0].T, "segment")
    conv = conv_weight[0].T
    padding = jnp.zeros((CH, LEAD - TAPS - STATS), BF)
    lead = (conv[:, :HALF], jnp.concatenate([conv[:, HALF:], coded.T, padding], axis=1))
    first_up = BLOCKS - DOWN

    def fetch(index, half, after):
        own, _ = lax.optimization_barrier((lead[half], after))
        first, second = PAIRS[index]
        return lax.ppermute(own, "segment", [(first, 0), (second, 1)])

    def exchange(near, cross, stats):
        other_tile = [(t, t ^ 1) for t in range(TILES)]
        other_core = [(b, b ^ 1) for b in range(BLOCKS)]
        both = [
            (b * TILES + t, (b ^ 1) * TILES + (t ^ 1)) for b in range(BLOCKS) for t in range(TILES)
        ]
        return (
            lax.ppermute(near, "tile", other_tile),
            lax.ppermute(cross, "segment", other_core),
            lax.ppermute(stats, BOTH, both),
        )

    def hand_over(block, whole):
        route = [(place(j, q), helper(block, j, q)) for j in range(MICRO) for q in range(4)]
        return lax.ppermute(whole, BOTH, route)

    member_at = jnp.arange(CH) // GROUP
    member = (member_at[:, None] == member_at[None, :]).astype(BF)
    weights, cores, fetched = {}, {}, {}

    def swap_cores(index, own):
        both = [own, lax.ppermute(own, "segment", [(b, b ^ 1) for b in range(BLOCKS)])]
        for at, block in enumerate(PAIRS[index]):
            weights[block], cores[block] = weights.get(block, []) + both, at

    for own in lead:
        own, _ = lax.optimization_barrier((own, pieces))
        swap_cores(0, own)
    *exchanged, source = first_call(info, pieces)
    fetched[1, 0] = fetch(1, 0, pieces)
    fetched[1, 1] = fetch(1, 1, source)
    which = jnp.stack([segment % 8, odd]).astype(jnp.int32)

    def halves_of(outputs):
        kept, sent = pick(which, outputs)
        return kept, lax.ppermute(sent, "tile", [(t, t ^ 1) for t in range(TILES)])

    wholes, edges_of, passing = [], {}, []
    for block in range(BLOCKS):
        up_in, up_out = block >= first_up, first_up - 1 <= block < BLOCKS - 1
        near, cross, stats = exchanged
        near_in, cross_in, far = exchange(near, cross, stats)
        edges_of[block] = (near_in, cross_in)
        if block >= 1:
            sent, _ = lax.optimization_barrier((wholes[-1], (near_in, cross_in, far)))
            passing.append(hand_over(block - 1, sent))
        for arrived in DONE_BY.get(block, [block - 3]):
            if arrived >= 0:
                source, near_in, cross_in, far, passing[arrived] = lax.optimization_barrier(
                    (source, near_in, cross_in, far, passing[arrived])
                )
        if block == 15:
            source, early = lax.optimization_barrier((source, early))
        whole, exchanged, summed = block_call(
            block,
            cores[block],
            info,
            source,
            (near_in, cross_in, stats, far),
            member,
            weights[block],
            skips,
            edges_of[BLOCKS - block] if up_in else None,
            wholes[BLOCKS - 2 - block] if up_out else None,
        )
        wholes.append(whole)
        source = summed if up_out else whole
        if block == 12:
            early = halves_of(passing[:8])
        for key, after in SWAP_AFTER.items():
            if after == block:
                own, _ = lax.optimization_barrier((fetched[key], whole))
                swap_cores(key[0], own)
        for key, after in FETCH_AFTER.items():
            if after == block:
                fetched[key] = fetch(*key, whole)
    passing.append(hand_over(BLOCKS - 1, wholes[-1]))
    late = halves_of(passing[8:])
    kept_first = (odd == tile // 8).astype(jnp.int32)[None]
    held = join(kept_first, [*early, *late])
    peers = [
        [(s + 8 * far) * TILES + 8 * side + z for far in range(2) for z in range(8)]
        for s in range(8)
        for side in range(2)
    ]
    out = lax.all_to_all(held, BOTH, 0, 0, axis_index_groups=peers, tiled=True)
    out = out.reshape(1, MICRO, 3, CH, WIDTH)
    return out.transpose(0, 1, 2, 4, 3)


def solution(mesh):
    placed = (
        P(None, "tile", None, None),
        P(),
        P(),
        P("segment", None, None),
        P("segment", None, None),
        P("segment", None, None),
        P("segment", None),
        P("segment", None),
    )
    return jax.shard_map(
        on_device,
        mesh=mesh,
        in_specs=placed,
        out_specs=P("segment", None, "tile", None, None),
        check_vma=False,
    )
```
